32 devices in a mesh: dp: 8 (over z, x), tensor: 4 (over y, core).
Axes of the slice: x: 2, y: 2, z: 4, core: 2. Of those that a mesh axis runs over, the one named last changes fastest.
Arguments:
- tokens: bfloat16 [8192, 2048], P(('dp', 'tensor')), may hold values from -6 to 6
- norm1_gain: float32 [2048], replicated, may hold values from 0.5 to 1.5
- w_query: bfloat16 [2048, 2048], P(None, 'tensor'), may hold values from -0.125 to 0.125
- w_key: bfloat16 [2048, 2048], P(None, 'tensor'), may hold values from -0.125 to 0.125
- w_value: bfloat16 [2048, 4096], P(None, 'tensor'), may hold values from -0.125 to 0.125
- w_gate_out: bfloat16 [2048, 4096], P(None, 'tensor'), may hold values from -0.125 to 0.125
- w_decay: bfloat16 [2048, 16], P(None, 'tensor'), may hold values from -0.125 to 0.125
- w_beta: bfloat16 [2048, 16], P(None, 'tensor'), may hold values from -0.125 to 0.125
- conv_query: float32 [4, 2048], P(None, 'tensor'), may hold values from -3 to 3
- conv_key: float32 [4, 2048], P(None, 'tensor'), may hold values from -3 to 3
- conv_value: float32 [4, 4096], P(None, 'tensor'), may hold values from -3 to 3
- decay_log: float32 [16], P('tensor'), may hold values from 0 to 2.8
- decay_bias: float32 [16], P('tensor'), may hold values from -9 to -3
- head_gain: float32 [256], replicated, may hold values from 0.5 to 1.5
- w_out: bfloat16 [4096, 2048], P('tensor'), may hold values from -0.1875 to 0.1875
- norm2_gain: float32 [2048], replicated, may hold values from 0.5 to 1.5
- w_gate: bfloat16 [2048, 5504], P(None, 'tensor'), may hold values from -0.125 to 0.125
- w_up: bfloat16 [2048, 5504], P(None, 'tensor'), may hold values from -0.125 to 0.125
- w_down: bfloat16 [5504, 2048], P('tensor'), may hold values from -0.078125 to 0.078125
- state_in: float32 [8, 16, 128, 256], P('dp', 'tensor'), may hold values from -2 to 2
- seq_blocks: int32 [8], P('dp'), may hold values from 1 to 16, 96 in all
- seq_tail: int32 [8], P('dp'), may hold values from 1 to 64
- cotangent: bfloat16 [8192, 2048], P(('dp', 'tensor')), may hold values from -6 to 6
Outputs:
- mixed: bfloat16 [8192, 2048], P(('dp', 'tensor'))
- final_state: float32 [8, 16, 128, 256], P('dp', 'tensor')
- tokens_grad: bfloat16 [8192, 2048], P(('dp', 'tensor'))
- norm1_gain_grad: float32 [2048], replicated
- w_query_grad: float32 [2048, 2048], P('dp', 'tensor')
- w_key_grad: float32 [2048, 2048], P('dp', 'tensor')
- w_value_grad: float32 [2048, 4096], P('dp', 'tensor')
- w_gate_out_grad: float32 [2048, 4096], P('dp', 'tensor')
- w_decay_grad: float32 [2048, 16], P('dp', 'tensor')
- w_beta_grad: float32 [2048, 16], P('dp', 'tensor')
- conv_query_grad: float32 [4, 2048], P(None, 'tensor')
- conv_key_grad: float32 [4, 2048], P(None, 'tensor')
- conv_value_grad: float32 [4, 4096], P(None, 'tensor')
- decay_log_grad: float32 [16], P('tensor')
- decay_bias_grad: float32 [16], P('tensor')
- head_gain_grad: float32 [256], replicated
- w_out_grad: float32 [4096, 2048], P('tensor', 'dp')
- norm2_gain_grad: float32 [2048], replicated
- w_gate_grad: float32 [2048, 5504], P('dp', 'tensor')
- w_up_grad: float32 [2048, 5504], P('dp', 'tensor')
- w_down_grad: float32 [5504, 2048], P('tensor', 'dp')
The draws below stay inside these ranges and needn't reach their ends.
Inputs may be any that keep to these rules, and one draw needn't show every extreme that they name: `seq_blocks`: one group's sequence fills all 16 blocks in every draw.
All inputs are finite; a program needn't handle non-finite values.
Results may differ from the reference program's by a relative error of at most 0.019.
Values may be sent and summed in bfloat16 or wider, within the bound.
A program may use at most 320 MiB of HBM per device.

```python
import math
import jax
import jax.numpy as jnp
import numpy as np
from jax import lax

D = 2048
H = 16
DK = 128
DV = 256
KCONV = 4
FF = 5504
BLOCK = 64
GROUP = 1024
BLOCKS = 16
TOKENS = 8192
N_DP = 8


def touch_ends(result, rng, least, largest):
    index_at = [jax.random.randint(jax.random.fold_in(rng, axis), (), 0, length) for axis, length in enumerate(result.shape)]
    widest = result.shape.index(max(result.shape))
    beside = index_at[:widest] + [(index_at[widest] + 1) % result.shape[widest]] + index_at[widest + 1:]
    return result.at[tuple(index_at)].set(least).at[tuple(beside)].set(largest)


def level_of(rng, shape, cuts, least, largest):
    def one(position, shards_of):
        draws = jax.random.uniform(jax.random.fold_in(jax.random.fold_in(rng, 6), position), (shards_of,), jnp.float32, least / len(cuts), largest / len(cuts))
        return jnp.repeat(jnp.exp(draws), shape[position] // shards_of).reshape((-1,) + (1,) * (len(shape) - position - 1))

    loudness = one(*cuts[0])
    for cut in cuts[1:]:
        loudness = loudness * one(*cut)
    return loudness


def split_up(count, total, most, lean):
    portions = [(1 << 20) // math.isqrt(rank ** lean) + 1 for rank in range(2, count + 1)]
    spare, counts = total - most - (count - 1), [1] * (count - 1)
    while spare > 0:
        movable = [i for i in range(count - 1) if counts[i] < most]
        pool, remaining = sum([portions[i] for i in movable]), spare
        for i in movable:
            more = min(most - counts[i], max(1, remaining * portions[i] // pool), spare)
            counts[i] = counts[i] + more
            spare = spare - more
    return np.array([most] + counts)


def ragged(own_key, number_of, total, reach, skew):
    if number_of == 2:
        one = jax.random.randint(own_key, (), max(1, total - reach), min(reach, total - 1) + 1)
        return jnp.stack([one, total - one])
    tallies = jnp.asarray(split_up(number_of, total, reach, skew), jnp.int32)
    pairs = (number_of - 1) // 2
    source_of, taker = tallies[1:1 + 2 * pairs:2], tallies[2:2 + 2 * pairs:2]
    slack = jnp.minimum(source_of - 1, reach - taker)
    shifted = jax.random.randint(jax.random.fold_in(own_key, 1), (pairs,), 0, 1 << 20) % (slack + 1)
    tallies = tallies.at[1:1 + 2 * pairs:2].set(source_of - shifted).at[2:2 + 2 * pairs:2].set(taker + shifted)
    return tallies[jax.random.permutation(jax.random.fold_in(own_key, 2), number_of)]


def bell_draw(rng, dims, deviation, most, split=(), held_as=jnp.bfloat16):
    result = deviation * jax.random.normal(rng, dims, jnp.float32)
    if split:
        result = result * level_of(rng, dims, split, -0.22, 0.18)
    return jnp.clip(result, -most, most).astype(held_as)


def setup_inputs(seed: int = 0) -> dict:
    splits = jax.random.split(jax.random.key(seed), 24)
    return {
        "tokens": bell_draw(splits[0], (TOKENS, D), 1.0, 6.0, ((0, 32),)),
        "norm1_gain": jnp.clip(1.0 + 0.1 * jax.random.normal(splits[1], (D,), jnp.float32), 0.5, 1.5),
        "w_query": bell_draw(splits[2], (D, H * DK), D ** -0.5, 0.125, ((1, 4),)),
        "w_key": bell_draw(splits[3], (D, H * DK), D ** -0.5, 0.125, ((1, 4),)),
        "w_value": bell_draw(splits[4], (D, H * DV), D ** -0.5, 0.125, ((1, 4),)),
        "w_gate_out": bell_draw(splits[5], (D, H * DV), D ** -0.5, 0.125, ((1, 4),)),
        "w_decay": bell_draw(splits[6], (D, H), D ** -0.5, 0.125, ((1, 4),)),
        "w_beta": bell_draw(splits[7], (D, H), D ** -0.5, 0.125, ((1, 4),)),
        "conv_query": bell_draw(splits[8], (KCONV, H * DK), 0.5, 3.0, ((1, 4),), jnp.float32),
        "conv_key": bell_draw(splits[9], (KCONV, H * DK), 0.5, 3.0, ((1, 4),), jnp.float32),
        "conv_value": bell_draw(splits[10], (KCONV, H * DV), 0.5, 3.0, ((1, 4),), jnp.float32),
        "decay_log": jnp.clip(2.8 * jax.random.uniform(splits[11], (H,), jnp.float32) ** level_of(splits[11], (H,), ((0, 4),), -0.2, 0.2), 0.0, 2.8),
        "decay_bias": jnp.clip(-9.0 + 6.0 * jax.random.uniform(splits[12], (H,), jnp.float32) ** level_of(splits[12], (H,), ((0, 4),), -0.2, 0.2), -9.0, -3.0),
        "head_gain": jnp.clip(1.0 + 0.1 * jax.random.normal(splits[13], (DV,), jnp.float32), 0.5, 1.5),
        "w_out": bell_draw(splits[14], (H * DV, D), (H * DV // 4) ** -0.5, 0.1875, ((0, 4),)),
        "norm2_gain": jnp.clip(1.0 + 0.1 * jax.random.normal(splits[15], (D,), jnp.float32), 0.5, 1.5),
        "w_gate": bell_draw(splits[16], (D, FF), D ** -0.5, 0.125, ((1, 4),)),
        "w_up": bell_draw(splits[17], (D, FF), D ** -0.5, 0.125, ((1, 4),)),
        "w_down": bell_draw(splits[18], (FF, D), FF ** -0.5, 0.078125, ((0, 4),)),
        "state_in": bell_draw(splits[19], (N_DP, H, DK, DV), 0.3, 2.0, ((0, 8), (1, 4)), jnp.float32),
        "seq_blocks": ragged(splits[20], N_DP, (3 * BLOCKS * N_DP) // 4, BLOCKS, 0).astype(jnp.int32),
        "seq_tail": touch_ends(jax.random.randint(splits[21], (N_DP,), 1, BLOCK + 1), jax.random.fold_in(splits[21], 1), 1, BLOCK).astype(jnp.int32),
        "cotangent": bell_draw(splits[22], (TOKENS, D), 1.0, 6.0, ((0, 32),)),
    }


@jax.custom_vjp
def low(v):
    return lax.optimization_barrier(v.astype(jnp.bfloat16)).astype(jnp.float32)

@jax.custom_vjp
def low_back(v):
    return v

def low_keep(v):
    return (low(v), None)

def low_pass(kept, grad):
    return (grad,)

def back_keep(v):
    return (v, None)

def back_low(kept, grad):
    return (low(grad),)
low.defvjp(low_keep, low_pass)
low_back.defvjp(back_keep, back_low)
highest_precision = lax.Precision.HIGHEST

def matmul(left, right):
    return jnp.dot(left, right, precision=highest_precision, preferred_element_type=jnp.float32)

def row_norm(rows, gain):
    return rows * lax.rsqrt(lax.optimization_barrier(jnp.mean(rows * rows, axis=-1, keepdims=True)) + 1e-05) * gain

def unit_rows(rows):
    return rows * lax.rsqrt(lax.optimization_barrier(jnp.sum(rows * rows, axis=-1, keepdims=True)) + 1e-06)

def causal_conv(series, kernel):
    length = series.shape[0]
    taps = kernel.shape[0]
    padded = jnp.pad(series, ((taps - 1, 0), (0, 0)))
    total = padded[0:length] * kernel[0]
    for tap_index in range(1, taps):
        total = total + padded[tap_index:tap_index + length] * kernel[tap_index]
    return jax.nn.silu(total)

def token_step(state_carried_over, inputs):
    query_rows, current_keys, values_now, decays, strength = inputs
    state_after_decay = state_carried_over * jnp.exp(decays)[:, None, None]
    recalled_values = jnp.einsum('mw,mwc->mc', current_keys, state_after_decay, precision=highest_precision)
    update = strength[:, None] * (values_now - recalled_values)
    state_carried_over = state_after_decay + current_keys[:, :, None] * update[:, None, :]
    output_rows = jnp.einsum('mw,mwc->mc', query_rows, state_carried_over, precision=highest_precision)
    return (state_carried_over, output_rows)

def block_steps(state_carried_over, inputs):
    return lax.scan(token_step, state_carried_over, inputs)

def mixer(projected, state_carried_over, validity, conv_query, conv_key, conv_value, decay_log, decay_bias, head_gain):
    rows = projected.shape[0]
    key_width = H * DK
    value_width = H * DV
    query_rows = unit_rows(causal_conv(projected[:, :key_width], conv_query).reshape(rows, H, DK)) * DK ** (-0.5)
    keys_all = unit_rows(causal_conv(projected[:, key_width:2 * key_width], conv_key).reshape(rows, H, DK))
    values_all = causal_conv(projected[:, 2 * key_width:2 * key_width + value_width], conv_value).reshape(rows, H, DV)
    gate_start = 2 * key_width + value_width
    out_gate = projected[:, gate_start:gate_start + value_width].reshape(rows, H, DV)
    decay_start = gate_start + value_width
    decay_in = projected[:, decay_start:decay_start + H]
    beta_in = projected[:, decay_start + H:decay_start + 2 * H]
    decays = -jnp.exp(decay_log) * jax.nn.softplus(decay_in + decay_bias) * validity[:, None]
    strength = jax.nn.sigmoid(beta_in) * validity[:, None]
    blocks = rows // BLOCK

    def arrange(array):
        return array.reshape((blocks, BLOCK) + array.shape[1:])
    final, outputs = lax.scan(jax.checkpoint(block_steps), state_carried_over, (arrange(query_rows), arrange(keys_all), arrange(values_all), arrange(decays), arrange(strength)))
    outputs = outputs.reshape(rows, H, DV)
    normed = outputs * lax.rsqrt(lax.optimization_barrier(jnp.mean(outputs * outputs, axis=-1, keepdims=True)) + 1e-05) * head_gain
    gated = normed * jax.nn.silu(out_gate) * validity[:, None, None]
    return (gated.reshape(rows, value_width), final)

def reference(tokens, norm1_gain, w_query, w_key, w_value, w_gate_out, w_decay, w_beta, conv_query, conv_key, conv_value, decay_log, decay_bias, head_gain, w_out, norm2_gain, w_gate, w_up, w_down, state_in, seq_blocks, seq_tail, cotangent):
    lengths_all = BLOCK * (seq_blocks - 1) + seq_tail
    positions = jnp.arange(GROUP, dtype=jnp.int32)
    validity = (positions[None, :] < lengths_all[:, None]).astype(jnp.float32)
    weights = tuple((weight.astype(jnp.float32) for weight in (norm1_gain, w_query, w_key, w_value, w_gate_out, w_decay, w_beta, conv_query, conv_key, conv_value, decay_log, decay_bias, head_gain, w_out, norm2_gain, w_gate, w_up, w_down)))

    def forward(rows_in, gain_one, query_w, key_w, value_w, gate_out_w, decay_w, beta_w, kernel_query, kernel_key, kernel_value, log_scale, bias_decay, gain_head, out_w, gain_two, gate_w, up_w, down_w):
        normed1 = low(row_norm(rows_in, gain_one))
        projected = jnp.concatenate([low_back(matmul(normed1, weight)) for weight in (query_w, key_w, value_w, gate_out_w, decay_w, beta_w)], axis=1)
        grouped = projected.reshape(N_DP, GROUP, projected.shape[1])

        def one_group(group_inputs):
            return jax.checkpoint(mixer)(group_inputs[0], group_inputs[1], group_inputs[2], kernel_query, kernel_key, kernel_value, log_scale, bias_decay, gain_head)
        gated, finals = lax.map(one_group, (grouped, state_in, validity))
        gated = low(gated.reshape(TOKENS, H * DV))
        resid = low_back(rows_in + matmul(gated, out_w))
        normed2 = low(row_norm(resid, gain_two))
        gate_pre = low_back(matmul(normed2, gate_w))
        up_pre = low_back(matmul(normed2, up_w))
        hidden = low(jax.nn.silu(gate_pre) * up_pre)
        return (resid + matmul(hidden, down_w), finals)
    outputs, pull = jax.vjp(forward, tokens.astype(jnp.float32), *weights)
    grads = pull((cotangent.astype(jnp.float32), jnp.zeros_like(outputs[1])))
    return (outputs[0].astype(jnp.bfloat16), outputs[1], grads[0].astype(jnp.bfloat16), grads[1], grads[2], grads[3], grads[4], grads[5], grads[6], grads[7], grads[8], grads[9], grads[10], grads[11], grads[12], grads[13], grads[14], grads[15], grads[16], grads[17], grads[18])
```

```python
import jax
import jax.numpy as jnp
from jax import lax
from jax.experimental import pallas as pl
from jax.experimental.pallas import tpu as pltpu
from jax.sharding import PartitionSpec as P

BLOCK = 64

CHUNK = 128
f32 = jnp.float32
bf16 = jnp.bfloat16


def mm(left, right):
    return lax.dot_general(
        left.astype(bf16), right.astype(bf16), (((1,), (0,)), ((), ())), preferred_element_type=f32
    )


def mm_nt(left, right):
    return lax.dot_general(
        left.astype(bf16), right.astype(bf16), (((1,), (1,)), ((), ())), preferred_element_type=f32
    )


def mm_tn(left, right):
    return lax.dot_general(
        left.astype(bf16), right.astype(bf16), (((0,), (0,)), ((), ())), preferred_element_type=f32
    )


def conv_rows(rows, before, taps):
    count = rows.shape[0]
    longer = jnp.concatenate([before, rows], axis=0)
    total = rows * taps[3:4]
    for tap in range(3):
        total = total + longer[5 + tap : 5 + tap + count] * taps[tap : tap + 1]
    return total


def sigmoid(value):
    return 1.0 / (1.0 + jnp.exp(-value))


def unit_factor(rows):
    return lax.rsqrt(jnp.sum(rows * rows, axis=-1, keepdims=True) + 1e-06)


def chunk_masks():
    down = lax.broadcasted_iota(jnp.int32, (CHUNK, CHUNK), 0)
    across = lax.broadcasted_iota(jnp.int32, (CHUNK, CHUNK), 1)
    return down, across


def mixer_forward_kernel(
    length_ref, pq, pk, pv, pg, grow, gcol, cq, ck, cv, gain, s0,
    gated_out, final_out, o_out, delta_out, s_out, tt_out,
    state, tq, tk, tv,
):
    chunk = pl.program_id(0)
    heads = s0.shape[0]
    dk, dv = s0.shape[1], s0.shape[2]
    every = range(heads)

    @pl.when(chunk == 0)
    def _():
        state[...] = s0[...]
        tq[...] = jnp.zeros_like(tq)
        tk[...] = jnp.zeros_like(tk)
        tv[...] = jnp.zeros_like(tv)

    down, across = chunk_masks()
    lower = down > across
    full = down >= across
    level = jnp.where(lower, down ^ across, 0)
    eye = jnp.where(down == across, 1.0, 0.0)
    eye_low = eye.astype(bf16)
    kslice = [slice(h * dk, (h + 1) * dk) for h in every]
    vslice = [slice(h * dv, (h + 1) * dv) for h in every]

    def activated(ref, tail, taps, where):
        pre = conv_rows(ref[:, where], tail[:, where], taps[:, where])
        return pre * sigmoid(pre)

    keys, queries, values = [], [], []
    for h in every:
        u = activated(pk, tk, ck, kslice[h])
        keys.append((u * unit_factor(u)).astype(bf16))
    for h in every:
        u = activated(pq, tq, cq, kslice[h])
        queries.append((u * (unit_factor(u) * dk ** (-0.5))).astype(bf16))
    gc = [gcol[:, h : h + 1] for h in every]
    bc = [gcol[:, heads + h : heads + h + 1] for h in every]
    products = [mm_nt(jnp.concatenate([keys[h], queries[h]], axis=0), keys[h]) for h in every]
    gam = [jnp.exp(jnp.where(full, gc[h] - grow[0, h : h + 1, :], -1e30)) for h in every]
    system = [jnp.where(lower, products[h][:CHUNK] * gam[h] * bc[h], 0.0) for h in every]
    attend = [(products[h][CHUNK:] * gam[h]).astype(bf16) for h in every]
    system_low = [system[h].astype(bf16) for h in every]
    first = jnp.where(level == 1, 1.0, 0.0).astype(bf16)
    inverse = [eye_low - system_low[h] * first for h in every]
    size = 2
    while size < CHUNK:
        mask = jnp.where((level >= size) & (level < 2 * size), 1.0, 0.0).astype(bf16)
        inner = [mm(system_low[h] * mask, inverse[h]).astype(bf16) for h in every]
        inverse = [inverse[h] - mm(inverse[h], inner[h]).astype(bf16) for h in every]
        size *= 2
    left_over = [
        (eye - inverse[h].astype(f32))
        - mm(system_low[h], inverse[h])
        - mm((system[h] - system_low[h].astype(f32)).astype(bf16), inverse[h])
        for h in every
    ]
    inverse = [(inverse[h].astype(f32) + mm(inverse[h], left_over[h])) for h in every]
    for h in every:
        tt_out[0, h] = jnp.transpose(inverse[h]).astype(bf16)
    inverse = [inverse[h].astype(bf16) for h in every]
    for h in every:
        values.append(activated(pv, tv, cv, vslice[h]))
    for ref, tail in ((pq, tq), (pk, tk), (pv, tv)):
        tail[...] = ref[CHUNK - 8 :, :]
    growth = [jnp.exp(gc[h]) for h in every]
    keys_f = [keys[h].astype(f32) for h in every]
    pair = [
        jnp.concatenate(
            [(keys_f[h] * growth[h]).astype(bf16), (queries[h].astype(f32) * growth[h]).astype(bf16)], axis=0
        )
        for h in every
    ]
    for h in every:
        s_out[0, h] = state[h].astype(bf16)
    carried = [mm(pair[h], state[h]) for h in every]
    delta = [
        mm(inverse[h], bc[h] * (values[h] - carried[h][:CHUNK])).astype(bf16) for h in every
    ]
    out = [carried[h][CHUNK:] + mm(attend[h], delta[h]) for h in every]
    for h in every:
        last = gc[h][CHUNK - 1 : CHUNK]
        late = (keys_f[h] * jnp.exp(last - gc[h])).astype(bf16)
        state[h] = jnp.exp(last) * state[h] + mm_tn(late, delta[h])
    row_at = chunk * CHUNK + lax.broadcasted_iota(jnp.int32, (CHUNK, 1), 0)
    valid = jnp.where(row_at < length_ref[0], 1.0, 0.0)
    for h in every:
        delta_out[:, vslice[h]] = delta[h]
        o_out[:, vslice[h]] = out[h].astype(bf16)
        inv = lax.rsqrt(jnp.mean(out[h] * out[h], axis=-1, keepdims=True) + 1e-05)
        gate = pg[:, vslice[h]]
        gated_out[:, vslice[h]] = (
            out[h] * (inv * valid) * gain[...] * (gate * sigmoid(gate))
        ).astype(bf16)

    @pl.when(chunk == pl.num_programs(0) - 1)
    def _():
        final_out[...] = state[...]


def mixer_forward(length, pq, pk, pv, pg, grow, gcol, cq, ck, cv, gain, s0):
    rows = pq.shape[0]
    heads, dk, dv = s0.shape
    chunks = rows // CHUNK

    def by_rows(width):
        return pl.BlockSpec((CHUNK, width), lambda c: (c, 0))

    def whole(*shape):
        return pl.BlockSpec(shape, lambda c: (0,) * len(shape))

    def by_chunk(*shape):
        return pl.BlockSpec((1,) + shape, lambda c: (c,) + (0,) * len(shape))

    kw, vw = heads * dk, heads * dv
    return pl.pallas_call(
        mixer_forward_kernel,
        grid=(chunks,),
        in_specs=[
            pl.BlockSpec(memory_space=pltpu.SMEM),
            by_rows(kw), by_rows(kw), by_rows(vw), by_rows(vw),
            by_chunk(grow.shape[1], CHUNK),
            by_rows(2 * heads),
            whole(4, kw), whole(4, kw), whole(4, vw), whole(1, dv), whole(heads, dk, dv),
        ],
        out_specs=[
            by_rows(vw), whole(heads, dk, dv), by_rows(vw), by_rows(vw),
            by_chunk(heads, dk, dv), by_chunk(heads, CHUNK, CHUNK),
        ],
        out_shape=[
            jax.ShapeDtypeStruct((rows, vw), bf16),
            jax.ShapeDtypeStruct((heads, dk, dv), f32),
            jax.ShapeDtypeStruct((rows, vw), bf16),
            jax.ShapeDtypeStruct((rows, vw), bf16),
            jax.ShapeDtypeStruct((chunks, heads, dk, dv), bf16),
            jax.ShapeDtypeStruct((chunks, heads, CHUNK, CHUNK), bf16),
        ],
        scratch_shapes=[
            pltpu.VMEM((heads, dk, dv), f32),
            pltpu.VMEM((8, kw), f32), pltpu.VMEM((8, kw), f32), pltpu.VMEM((8, vw), f32),
        ],
        compiler_params=pltpu.CompilerParams(vmem_limit_bytes=48 * 1024 * 1024),
        cost_estimate=pl.CostEstimate(flops=8_000_000_000, bytes_accessed=32_000_000, transcendentals=4_000_000),
        name="mixer_forward",
    )(length, pq, pk, pv, pg, grow, gcol, cq, ck, cv, gain, s0)


def mixer_backward_kernel(
    length_ref, pq, pk, pv, pg, pq8, pk8, pv8, dgated, o_in, delta_in, s_in, tt_in,
    grow, gcol, cq, ck, cv, gain,
    dpq, dpk, dpv, dpg, dscal, dcq, dck, dcv, dgain,
    dstate, nq, nk, nv,
):
    step = pl.program_id(0)
    chunk = pl.num_programs(0) - 1 - step
    heads, dk, dv = dstate.shape
    every = range(heads)

    @pl.when(step == 0)
    def _():
        for ref in (dstate, nq, nk, nv, dcq, dck, dcv, dgain):
            ref[...] = jnp.zeros_like(ref)

    down, across = chunk_masks()
    lower = down > across
    full = down >= across
    upper = down < across
    ufull = down <= across
    kslice = [slice(h * dk, (h + 1) * dk) for h in every]
    vslice = [slice(h * dv, (h + 1) * dv) for h in every]
    has_before = jnp.where(chunk > 0, 1.0, 0.0)

    def preact(ref, ref8, taps, where):
        pre = conv_rows(ref[:, where], ref8[:, where] * has_before, taps[:, where])
        sig = sigmoid(pre)
        return pre, sig

    def conv_back(dpre, ref, ref8, taps, where, later, dtaps, dref):
        rows = ref[:, where]
        longer = jnp.concatenate([ref8[:, where] * has_before, rows], axis=0)
        after = jnp.concatenate([dpre, later[:, where]], axis=0)
        total = dpre * taps[3:4, where]
        sums = [jnp.sum(dpre * longer[5 + tap : 5 + tap + CHUNK], axis=0, keepdims=True) for tap in range(3)]
        sums.append(jnp.sum(dpre * rows, axis=0, keepdims=True))
        for tap in range(3):
            total = total + after[3 - tap : 3 - tap + CHUNK] * taps[tap : tap + 1, where]
        dtaps[:, where] += jnp.concatenate(sums, axis=0)
        later[:, where] = dpre[:8]
        dref[:, where] = total.astype(bf16)

    row_at = chunk * CHUNK + lax.broadcasted_iota(jnp.int32, (CHUNK, 1), 0)
    valid = jnp.where(row_at < length_ref[0], 1.0, 0.0)
    last_row = lax.broadcasted_iota(jnp.int32, (CHUNK, 1), 0) == CHUNK - 1
    kpre, ksig, kinv, kunit, keys = [], [], [], [], []
    qpre, qsig, qinv, qunit, queries = [], [], [], [], []
    for h in every:
        pre, sig = preact(pk, pk8, ck, kslice[h])
        u = pre * sig
        inv = unit_factor(u)
        kpre.append(pre), ksig.append(sig), kinv.append(inv), kunit.append(u * inv)
        keys.append(kunit[h].astype(bf16))
    for h in every:
        pre, sig = preact(pq, pq8, cq, kslice[h])
        u = pre * sig
        inv = unit_factor(u)
        qpre.append(pre), qsig.append(sig), qinv.append(inv), qunit.append(u * inv)
        queries.append((qunit[h] * dk ** (-0.5)).astype(bf16))
    gc = [gcol[:, h : h + 1] for h in every]
    gr = [grow[0, h : h + 1, :] for h in every]
    bc = [gcol[:, heads + h : heads + h + 1] for h in every]
    br = [grow[0, heads + h : heads + h + 1, :] for h in every]
    do = []
    for h in every:
        dg = dgated[:, vslice[h]].astype(f32) * valid
        gate = pg[:, vslice[h]]
        sig = sigmoid(gate)
        act = gate * sig
        o = o_in[:, vslice[h]].astype(f32)
        inv = lax.rsqrt(jnp.mean(o * o, axis=-1, keepdims=True) + 1e-05)
        norm = o * inv
        through = dg * norm
        dgain[...] += jnp.sum(through * act, axis=0, keepdims=True)
        dpg[:, vslice[h]] = (through * gain[...] * (sig + act * (1.0 - sig))).astype(bf16)
        dn = dg * gain[...] * act
        do.append((inv * (dn - norm * jnp.mean(dn * norm, axis=-1, keepdims=True))).astype(bf16))
    delta = [delta_in[:, vslice[h]] for h in every]
    dnext = [dstate[h].astype(bf16) for h in every]
    growth = [jnp.exp(gc[h]) for h in every]
    ending = [jnp.exp(gc[h][CHUNK - 1 : CHUNK] - gc[h]) for h in every]
    final = [jnp.exp(gc[h][CHUNK - 1 : CHUNK]) for h in every]
    gamma = [jnp.exp(jnp.where(full, gc[h] - gr[h], -1e30)) for h in every]
    gamma_t = [jnp.exp(jnp.where(ufull, gr[h] - gc[h], -1e30)) for h in every]
    kq = [mm_nt(keys[h], queries[h]) for h in every]
    keys_late = [(keys[h].astype(f32) * ending[h]).astype(bf16) for h in every]
    d_delta = [
        mm(
            jnp.concatenate([(kq[h] * gamma_t[h]).astype(bf16), keys_late[h]], axis=1),
            jnp.concatenate([do[h], dnext[h]], axis=0),
        ).astype(bf16)
        for h in every
    ]
    dr = [mm(tt_in[0, h], d_delta[h]) for h in every]
    dr_low = [dr[h].astype(bf16) for h in every]
    both = [jnp.concatenate([do[h], dr_low[h]], axis=0) for h in every]
    pair = [
        jnp.concatenate(
            [
                (queries[h].astype(f32) * growth[h]).astype(bf16),
                (keys[h].astype(f32) * (-growth[h] * bc[h])).astype(bf16),
            ],
            axis=0,
        )
        for h in every
    ]
    state = [s_in[0, h] for h in every]
    new_dstate = [final[h] * dstate[h] + mm_tn(pair[h], both[h]) for h in every]
    dgamma_end = [
        jnp.sum(jnp.sum(state[h].astype(f32) * dstate[h], axis=0, keepdims=True), axis=1, keepdims=True)
        * final[h]
        for h in every
    ]
    d_keys_late = [mm_nt(delta[h], dnext[h]) * ending[h] for h in every]
    for h in every:
        dstate[h] = new_dstate[h]
    strict = [jnp.where(lower, gamma[h] * bc[h], 0.0) for h in every]
    strict_t = [jnp.where(upper, gamma_t[h] * br[h], 0.0) for h in every]
    outer = [mm_nt(both[h], delta[h]) for h in every]
    outer_t = [mm_nt(delta[h], both[h]) for h in every]
    inner = [
        jnp.concatenate(
            [(outer[h][:CHUNK] * gamma[h]).astype(bf16), (-outer[h][CHUNK:] * strict[h]).astype(bf16)], axis=0
        )
        for h in every
    ]
    inner_t = [
        jnp.concatenate(
            [
                (outer_t[h][:, :CHUNK] * gamma_t[h]).astype(bf16),
                (-outer_t[h][:, CHUNK:] * strict_t[h]).astype(bf16),
            ],
            axis=1,
        )
        for h in every
    ]
    by_state = [mm_nt(both[h], state[h]) for h in every]
    by_key = [mm(inner[h], keys[h]) for h in every]
    d_col = [
        mm(inner_t[h], jnp.concatenate([queries[h], keys[h]], axis=0)) + d_keys_late[h] for h in every
    ]
    scal = []
    dbs = []
    for h in every:
        dq = by_key[h][:CHUNK] + by_state[h][:CHUNK] * growth[h]
        d_row = by_key[h][CHUNK:] - by_state[h][CHUNK:] * (growth[h] * bc[h])
        key_f = keys[h].astype(f32)
        q_along = jnp.sum(queries[h].astype(f32) * dq, axis=-1, keepdims=True)
        row_along = jnp.sum(key_f * d_row, axis=-1, keepdims=True)
        col_along = jnp.sum(key_f * d_col[h], axis=-1, keepdims=True)
        late_along = jnp.sum(key_f * d_keys_late[h], axis=-1, keepdims=True)
        at_end = dgamma_end[h] + jnp.sum(late_along, axis=0, keepdims=True)
        scal.append(q_along + row_along - col_along + jnp.where(last_row, at_end, 0.0))
        dbs.append(jnp.sum(dr[h] * delta[h].astype(f32), axis=-1, keepdims=True))
        du = qinv[h] * (dq * dk ** (-0.5) - qunit[h] * q_along)
        dpre = du * (qsig[h] * (1.0 + qpre[h] * (1.0 - qsig[h])))
        conv_back(dpre, pq, pq8, cq, kslice[h], nq, dcq, dpq)
        du = kinv[h] * (d_row + d_col[h] - kunit[h] * (row_along + col_along))
        dpre = du * (ksig[h] * (1.0 + kpre[h] * (1.0 - ksig[h])))
        conv_back(dpre, pk, pk8, ck, kslice[h], nk, dck, dpk)
        pre, sig = preact(pv, pv8, cv, vslice[h])
        dpre = dr[h] * bc[h] * (sig * (1.0 + pre * (1.0 - sig)))
        conv_back(dpre, pv, pv8, cv, vslice[h], nv, dcv, dpv)
    dscal[...] = jnp.concatenate(scal + dbs, axis=1)


def mixer_backward(length, pq, pk, pv, pg, dgated, o, delta, s, tt, grow, gcol, cq, ck, cv, gain):
    rows = pq.shape[0]
    chunks, heads, dk, dv = s.shape
    kw, vw = heads * dk, heads * dv
    per = CHUNK // 8

    def by_rows(width):
        return pl.BlockSpec((CHUNK, width), lambda c: (chunks - 1 - c, 0))

    def before(width):
        return pl.BlockSpec((8, width), lambda c: (jnp.maximum((chunks - 1 - c) * per - 1, 0), 0))

    def whole(*shape):
        return pl.BlockSpec(shape, lambda c: (0,) * len(shape))

    def by_chunk(*shape):
        return pl.BlockSpec((1,) + shape, lambda c: (chunks - 1 - c,) + (0,) * len(shape))

    return pl.pallas_call(
        mixer_backward_kernel,
        grid=(chunks,),
        in_specs=[
            pl.BlockSpec(memory_space=pltpu.SMEM),
            by_rows(kw), by_rows(kw), by_rows(vw), by_rows(vw),
            before(kw), before(kw), before(vw),
            by_rows(vw), by_rows(vw), by_rows(vw),
            by_chunk(heads, dk, dv), by_chunk(heads, CHUNK, CHUNK),
            by_chunk(grow.shape[1], CHUNK), by_rows(2 * heads),
            whole(4, kw), whole(4, kw), whole(4, vw), whole(1, dv),
        ],
        out_specs=[
            by_rows(kw), by_rows(kw), by_rows(vw), by_rows(vw), by_rows(2 * heads),
            whole(4, kw), whole(4, kw), whole(4, vw), whole(1, dv),
        ],
        out_shape=[
            jax.ShapeDtypeStruct((rows, kw), bf16),
            jax.ShapeDtypeStruct((rows, kw), bf16),
            jax.ShapeDtypeStruct((rows, vw), bf16),
            jax.ShapeDtypeStruct((rows, vw), bf16),
            jax.ShapeDtypeStruct((rows, 2 * heads), f32),
            jax.ShapeDtypeStruct((4, kw), f32),
            jax.ShapeDtypeStruct((4, kw), f32),
            jax.ShapeDtypeStruct((4, vw), f32),
            jax.ShapeDtypeStruct((1, dv), f32),
        ],
        scratch_shapes=[
            pltpu.VMEM((heads, dk, dv), f32),
            pltpu.VMEM((8, kw), f32), pltpu.VMEM((8, kw), f32), pltpu.VMEM((8, vw), f32),
        ],
        compiler_params=pltpu.CompilerParams(vmem_limit_bytes=48 * 1024 * 1024),
        cost_estimate=pl.CostEstimate(flops=8_000_000_000, bytes_accessed=40_000_000, transcendentals=6_000_000),
        name="mixer_backward",
    )(length, pq, pk, pv, pg, pq, pk, pv, dgated, o, delta, s, tt, grow, gcol, cq, ck, cv, gain)


def decay_parts(pa, pb, log_scale, bias, valid):
    rows, heads = pa.shape
    decays = -jnp.exp(log_scale) * jax.nn.softplus(pa + bias) * valid
    strength = jax.nn.sigmoid(pb) * valid
    by_chunk = decays.reshape(rows // CHUNK, CHUNK, heads)
    at = jnp.arange(CHUNK)
    ones = (at[:, None] >= at[None, :]).astype(f32)
    running = jnp.einsum("ij,cjh->cih", ones, by_chunk, precision=lax.Precision.HIGHEST)
    strength_c = strength.reshape(rows // CHUNK, CHUNK, heads)
    cols = jnp.concatenate([running, strength_c], axis=-1)
    return jnp.swapaxes(cols, 1, 2), cols.reshape(rows, 2 * heads)


def decay_back(dscal, pa, pb, log_scale, bias, valid):
    rows, heads = pa.shape
    at = jnp.arange(CHUNK)
    ones = (at[:, None] <= at[None, :]).astype(f32)
    dg = dscal[:, :heads].reshape(rows // CHUNK, CHUNK, heads)
    da = jnp.einsum("ij,cjh->cih", ones, dg, precision=lax.Precision.HIGHEST).reshape(rows, heads)
    shifted = pa + bias
    scale = -jnp.exp(log_scale)
    dlog = jnp.sum(da * scale * jax.nn.softplus(shifted) * valid, axis=0)
    dpa = da * scale * jax.nn.sigmoid(shifted) * valid
    dpb = dscal[:, heads:] * jax.nn.sigmoid(-pb)
    return dlog, jnp.sum(dpa, axis=0), dpa, dpb


def product_tn(left, right):
    return lax.dot_general(
        left, right, (((0,), (0,)), ((), ())), preferred_element_type=jnp.float32
    )


def product_nt(left, right):
    return lax.dot_general(
        left, right, (((1,), (1,)), ((), ())), preferred_element_type=jnp.float32
    )


def row_stats(rows):
    inverse = lax.rsqrt(jnp.mean(rows * rows, axis=-1, keepdims=True) + 1e-05)
    return (rows * inverse, inverse)


def norm_back(scaled, inverse, gain, upstream):
    along = upstream * gain
    inner = jnp.mean(along * scaled, axis=-1, keepdims=True)
    return (inverse * (along - scaled * inner), jnp.sum(upstream * scaled, axis=0))


def per_device(
    tokens,
    norm1_gain,
    w_query,
    w_key,
    w_value,
    w_gate_out,
    w_decay,
    w_beta,
    conv_query,
    conv_key,
    conv_value,
    decay_log,
    decay_bias,
    head_gain,
    w_out,
    norm2_gain,
    w_gate,
    w_up,
    w_down,
    state_in,
    seq_blocks,
    seq_tail,
    cotangent,
):
    local_rows = tokens.shape[0]
    rows_in = tokens.astype(jnp.float32)
    scaled1, inverse1 = row_stats(rows_in)
    normed1 = (scaled1 * norm1_gain).astype(jnp.bfloat16)
    gathered1 = lax.all_gather(normed1, "tensor", axis=0, tiled=True)
    in_weights = (w_query, w_key, w_value, w_gate_out, w_decay, w_beta)
    group_rows = gathered1.shape[0]
    heads = decay_log.shape[0]
    w_small = jnp.concatenate([w_decay, w_beta], axis=1)
    p_query, p_key, p_value, p_gate = [
        jnp.dot(gathered1, weight, preferred_element_type=jnp.float32) for weight in in_weights[:4]
    ]
    p_small = jnp.dot(gathered1, w_small, preferred_element_type=jnp.float32)
    p_decay, p_beta = p_small[:, :heads], p_small[:, heads:]
    seq_length = BLOCK * (seq_blocks - 1) + seq_tail
    validity = (jnp.arange(group_rows, dtype=jnp.int32) < seq_length[0]).astype(jnp.float32)[:, None]
    grow, gcol = decay_parts(p_decay, p_beta, decay_log, decay_bias, validity)
    gain_row = head_gain[None]
    gated_low, final, mixer_out, delta, states, inverse_t = mixer_forward(
        seq_length, p_query, p_key, p_value, p_gate, grow, gcol,
        conv_query, conv_key, conv_value, gain_row, state_in[0],
    )
    resid = rows_in + lax.psum_scatter(
        jnp.dot(gated_low, w_out, preferred_element_type=jnp.float32).astype(jnp.bfloat16),
        "tensor",
        scatter_dimension=0,
        tiled=True,
    ).astype(jnp.float32)
    scaled2, inverse2 = row_stats(resid)
    normed2 = (scaled2 * norm2_gain).astype(jnp.bfloat16)
    gathered2 = lax.all_gather(normed2, "tensor", axis=0, tiled=True)
    gate_pre = jnp.dot(gathered2, w_gate, preferred_element_type=jnp.float32)
    up_pre = jnp.dot(gathered2, w_up, preferred_element_type=jnp.float32)
    sigmoid_gate = jax.nn.sigmoid(gate_pre)
    silu_gate = gate_pre * sigmoid_gate
    hidden = (silu_gate * up_pre).astype(jnp.bfloat16)
    mixed = (
        resid
        + lax.psum_scatter(
            jnp.dot(hidden, w_down, preferred_element_type=jnp.float32).astype(jnp.bfloat16),
            "tensor",
            scatter_dimension=0,
            tiled=True,
        ).astype(jnp.float32)
    ).astype(jnp.bfloat16)
    cot_full = lax.all_gather(cotangent, "tensor", axis=0, tiled=True)
    d_hidden = product_nt(cot_full, w_down)
    d_gate = (d_hidden * up_pre * sigmoid_gate * (1.0 + gate_pre * (1.0 - sigmoid_gate))).astype(
        jnp.bfloat16
    )
    d_up = (d_hidden * silu_gate).astype(jnp.bfloat16)
    grad_down = product_tn(hidden, cot_full)
    grad_gate = product_tn(gathered2, d_gate)
    grad_up = product_tn(gathered2, d_up)
    d_normed2 = lax.psum_scatter(
        (product_nt(d_gate, w_gate) + product_nt(d_up, w_up)).astype(jnp.bfloat16),
        "tensor",
        scatter_dimension=0,
        tiled=True,
    ).astype(jnp.float32)
    d_resid_part, grad_norm2 = norm_back(scaled2, inverse2, norm2_gain, d_normed2)
    d_resid = (cotangent.astype(jnp.float32) + d_resid_part).astype(jnp.bfloat16)
    resid_full = lax.all_gather(d_resid, "tensor", axis=0, tiled=True)
    d_gated = product_nt(resid_full, w_out)
    grad_out = product_tn(gated_low, resid_full)
    dp_query, dp_key, dp_value, dp_gate, dscal, dc_query, dc_key, dc_value, dgain = mixer_backward(
        seq_length, p_query, p_key, p_value, p_gate, d_gated, mixer_out, delta, states, inverse_t,
        grow, gcol, conv_query, conv_key, conv_value, gain_row,
    )
    dlog, dbias, dp_decay, dp_beta = decay_back(dscal, p_decay, p_beta, decay_log, decay_bias, validity)
    dp_small = jnp.concatenate([dp_decay, dp_beta], axis=1).astype(jnp.bfloat16)
    dps = (dp_query, dp_key, dp_value, dp_gate, dp_small)
    weights = (w_query, w_key, w_value, w_gate_out, w_small)
    total = product_nt(dps[0], weights[0])
    for dp_part, weight in zip(dps[1:], weights[1:]):
        total = total + product_nt(dp_part, weight)
    d_normed1 = lax.psum_scatter(
        total.astype(jnp.bfloat16), "tensor", scatter_dimension=0, tiled=True
    ).astype(jnp.float32)
    d_tokens_part, grad_norm1 = norm_back(scaled1, inverse1, norm1_gain, d_normed1)
    tokens_grad = (d_resid.astype(jnp.float32) + d_tokens_part).astype(jnp.bfloat16)
    in_grads = [product_tn(gathered1, dp_part) for dp_part in dps]
    in_grads = in_grads[:4] + [in_grads[4][:, :heads], in_grads[4][:, heads:]]
    mixer_grads = (None, dc_query, dc_key, dc_value, dlog, dbias, dgain[0])
    vector_sums = (
        lax.psum(mixer_grads[1].astype(jnp.bfloat16), "dp").astype(jnp.float32),
        lax.psum(mixer_grads[2].astype(jnp.bfloat16), "dp").astype(jnp.float32),
        lax.psum(mixer_grads[3].astype(jnp.bfloat16), "dp").astype(jnp.float32),
        lax.psum(mixer_grads[4].astype(jnp.bfloat16), "dp").astype(jnp.float32),
        lax.psum(mixer_grads[5].astype(jnp.bfloat16), "dp").astype(jnp.float32),
    )
    gain_sums = lax.psum((grad_norm1, grad_norm2, mixer_grads[6]), ("dp", "tensor"))
    all_sums = (
        lax.psum_scatter(
            in_grads[0].astype(jnp.bfloat16), "dp", scatter_dimension=0, tiled=True
        ).astype(jnp.float32),
        lax.psum_scatter(
            in_grads[1].astype(jnp.bfloat16), "dp", scatter_dimension=0, tiled=True
        ).astype(jnp.float32),
        lax.psum_scatter(
            in_grads[2].astype(jnp.bfloat16), "dp", scatter_dimension=0, tiled=True
        ).astype(jnp.float32),
        lax.psum_scatter(
            in_grads[3].astype(jnp.bfloat16), "dp", scatter_dimension=0, tiled=True
        ).astype(jnp.float32),
        lax.psum_scatter(
            in_grads[4].astype(jnp.bfloat16), "dp", scatter_dimension=0, tiled=True
        ).astype(jnp.float32),
        lax.psum_scatter(
            in_grads[5].astype(jnp.bfloat16), "dp", scatter_dimension=0, tiled=True
        ).astype(jnp.float32),
        lax.psum_scatter(
            grad_out.astype(jnp.bfloat16), "dp", scatter_dimension=1, tiled=True
        ).astype(jnp.float32),
        lax.psum_scatter(
            grad_gate.astype(jnp.bfloat16), "dp", scatter_dimension=0, tiled=True
        ).astype(jnp.float32),
        lax.psum_scatter(
            grad_up.astype(jnp.bfloat16), "dp", scatter_dimension=0, tiled=True
        ).astype(jnp.float32),
        lax.psum_scatter(
            grad_down.astype(jnp.bfloat16), "dp", scatter_dimension=1, tiled=True
        ).astype(jnp.float32),
    )
    mixer_sums = all_sums[:7]
    gate_sum, up_sum, down_sum = (all_sums[7], all_sums[8], all_sums[9])
    return (
        mixed,
        final[None],
        tokens_grad,
        gain_sums[0],
        mixer_sums[0],
        mixer_sums[1],
        mixer_sums[2],
        mixer_sums[3],
        mixer_sums[4],
        mixer_sums[5],
        vector_sums[0],
        vector_sums[1],
        vector_sums[2],
        vector_sums[3],
        vector_sums[4],
        gain_sums[2],
        mixer_sums[6],
        gain_sums[1],
        gate_sum,
        up_sum,
        down_sum,
    )


def solution(mesh):
    in_specs = (
        P(("dp", "tensor"), None),
        P(),
        P(None, "tensor"),
        P(None, "tensor"),
        P(None, "tensor"),
        P(None, "tensor"),
        P(None, "tensor"),
        P(None, "tensor"),
        P(None, "tensor"),
        P(None, "tensor"),
        P(None, "tensor"),
        P("tensor"),
        P("tensor"),
        P(),
        P("tensor", None),
        P(),
        P(None, "tensor"),
        P(None, "tensor"),
        P("tensor", None),
        P("dp", "tensor", None, None),
        P("dp"),
        P("dp"),
        P(("dp", "tensor"), None),
    )
    out_specs = (
        P(("dp", "tensor"), None),
        P("dp", "tensor", None, None),
        P(("dp", "tensor"), None),
        P(),
        P("dp", "tensor"),
        P("dp", "tensor"),
        P("dp", "tensor"),
        P("dp", "tensor"),
        P("dp", "tensor"),
        P("dp", "tensor"),
        P(None, "tensor"),
        P(None, "tensor"),
        P(None, "tensor"),
        P("tensor"),
        P("tensor"),
        P(),
        P("tensor", "dp"),
        P(),
        P("dp", "tensor"),
        P("dp", "tensor"),
        P("tensor", "dp"),
    )
    return jax.shard_map(
        per_device, mesh=mesh, in_specs=in_specs, out_specs=out_specs, check_vma=False
    )
```

```python
import jax
import jax.numpy as jnp
from jax import lax
from jax.experimental import pallas as pl
from jax.experimental.pallas import tpu as pltpu
from jax.sharding import PartitionSpec as P

BLOCK = 64

CHUNK = 128
f32 = jnp.float32
bf16 = jnp.bfloat16


def mm(left, right):
    return lax.dot_general(
        left.astype(bf16), right.astype(bf16), (((1,), (0,)), ((), ())), preferred_element_type=f32
    )


def mm_nt(left, right):
    return lax.dot_general(
        left.astype(bf16), right.astype(bf16), (((1,), (1,)), ((), ())), preferred_element_type=f32
    )


def mm_tn(left, right):
    return lax.dot_general(
        left.astype(bf16), right.astype(bf16), (((0,), (0,)), ((), ())), preferred_element_type=f32
    )


def conv_rows(rows, before, taps):
    count = rows.shape[0]
    longer = jnp.concatenate([before, rows], axis=0)
    total = rows * taps[3:4]
    for tap in range(3):
        total = total + longer[5 + tap : 5 + tap + count] * taps[tap : tap + 1]
    return total


def sigmoid(value):
    return 1.0 / (1.0 + jnp.exp(-value))


def unit_factor(rows):
    return lax.rsqrt(jnp.sum(rows * rows, axis=-1, keepdims=True) + 1e-06)


def chunk_masks():
    down = lax.broadcasted_iota(jnp.int32, (CHUNK, CHUNK), 0)
    across = lax.broadcasted_iota(jnp.int32, (CHUNK, CHUNK), 1)
    return down, across


def softplus(value):
    return jnp.maximum(value, 0.0) + jnp.log1p(jnp.exp(-jnp.abs(value)))


def exact(left, right):
    return jnp.dot(left, right, preferred_element_type=f32, precision=lax.Precision.HIGHEST)


def block_place(chunk, place, per):
    return ((chunk // per) ^ place) * per + chunk % per


def decay_terms(small, log_scale, bias, valid, tri):
    heads = log_scale.shape[1]
    decays = -jnp.exp(log_scale) * softplus(small[:, :heads] + bias) * valid
    running = exact(tri, decays)
    strength = sigmoid(small[:, heads:]) * valid
    cols = jnp.concatenate([running, strength], axis=1)
    wide = jnp.concatenate([cols, jnp.zeros((CHUNK, CHUNK - 2 * heads), f32)], axis=1)
    return cols, jnp.transpose(wide)[: 2 * heads]


def mixer_forward_kernel(
    scal, pq, pk, pv, pg, small, cq, ck, cv, dlog, dbias, gain, s0,
    gated_out, final_out, o_out, delta_out, s_out, tt_out,
    state, tq, tk, tv,
):
    chunk = pl.program_id(0)
    heads = s0.shape[0]
    dk, dv = s0.shape[1], s0.shape[2]
    every = range(heads)

    @pl.when(chunk == 0)
    def _():
        state[...] = s0[...]
        tq[...] = jnp.zeros_like(tq)
        tk[...] = jnp.zeros_like(tk)
        tv[...] = jnp.zeros_like(tv)

    down, across = chunk_masks()
    lower = down > across
    full = down >= across
    level = jnp.where(lower, down ^ across, 0)
    eye = jnp.where(down == across, 1.0, 0.0)
    eye_low = eye.astype(bf16)
    kslice = [slice(h * dk, (h + 1) * dk) for h in every]
    vslice = [slice(h * dv, (h + 1) * dv) for h in every]

    row_at = chunk * CHUNK + lax.broadcasted_iota(jnp.int32, (CHUNK, 1), 0)
    valid = jnp.where(row_at < scal[0], 1.0, 0.0)
    tri = jnp.where(full, 1.0, 0.0)
    gcol, grow = decay_terms(small[...], dlog[...], dbias[...], valid, tri)

    def activated(ref, tail, taps, where):
        pre = conv_rows(ref[:, where].astype(f32), tail[:, where], taps[:, where])
        return pre * sigmoid(pre)

    keys, queries, values = [], [], []
    for h in every:
        u = activated(pk, tk, ck, kslice[h])
        keys.append((u * unit_factor(u)).astype(bf16))
    for h in every:
        u = activated(pq, tq, cq, kslice[h])
        queries.append((u * (unit_factor(u) * dk ** (-0.5))).astype(bf16))
    gc = [gcol[:, h : h + 1] for h in every]
    bc = [gcol[:, heads + h : heads + h + 1] for h in every]
    products = [mm_nt(jnp.concatenate([keys[h], queries[h]], axis=0), keys[h]) for h in every]
    gam = [jnp.exp(jnp.where(full, gc[h] - grow[h : h + 1, :], -1e30)) for h in every]
    system = [jnp.where(lower, products[h][:CHUNK] * gam[h] * bc[h], 0.0) for h in every]
    attend = [(products[h][CHUNK:] * gam[h]).astype(bf16) for h in every]
    system_low = [system[h].astype(bf16) for h in every]
    first = jnp.where(level == 1, 1.0, 0.0).astype(bf16)
    inverse = [eye_low - system_low[h] * first for h in every]
    size = 2
    while size < CHUNK:
        mask = jnp.where((level >= size) & (level < 2 * size), 1.0, 0.0).astype(bf16)
        inner = [mm(system_low[h] * mask, inverse[h]).astype(bf16) for h in every]
        inverse = [inverse[h] - mm(inverse[h], inner[h]).astype(bf16) for h in every]
        size *= 2
    left_over = [
        (eye - inverse[h].astype(f32))
        - mm(system_low[h], inverse[h])
        - mm((system[h] - system_low[h].astype(f32)).astype(bf16), inverse[h])
        for h in every
    ]
    inverse = [(inverse[h].astype(f32) + mm(inverse[h], left_over[h])) for h in every]
    for h in every:
        tt_out[0, h] = jnp.transpose(inverse[h]).astype(bf16)
    inverse = [inverse[h].astype(bf16) for h in every]
    for h in every:
        values.append(activated(pv, tv, cv, vslice[h]))
    for ref, tail in ((pq, tq), (pk, tk), (pv, tv)):
        tail[...] = ref[CHUNK - 16 :, :].astype(f32)[8:]
    growth = [jnp.exp(gc[h]) for h in every]
    keys_f = [keys[h].astype(f32) for h in every]
    pair = [
        jnp.concatenate(
            [(keys_f[h] * growth[h]).astype(bf16), (queries[h].astype(f32) * growth[h]).astype(bf16)], axis=0
        )
        for h in every
    ]
    for h in every:
        s_out[0, h] = state[h].astype(bf16)
    carried = [mm(pair[h], state[h]) for h in every]
    delta = [
        mm(inverse[h], bc[h] * (values[h] - carried[h][:CHUNK])).astype(bf16) for h in every
    ]
    out = [carried[h][CHUNK:] + mm(attend[h], delta[h]) for h in every]
    for h in every:
        last = gc[h][CHUNK - 1 : CHUNK]
        late = (keys_f[h] * jnp.exp(last - gc[h])).astype(bf16)
        state[h] = jnp.exp(last) * state[h] + mm_tn(late, delta[h])
    for h in every:
        delta_out[:, vslice[h]] = delta[h]
        o_out[:, vslice[h]] = out[h].astype(bf16)
        inv = lax.rsqrt(jnp.mean(out[h] * out[h], axis=-1, keepdims=True) + 1e-05)
        gate = pg[:, vslice[h]].astype(f32)
        gated_out[:, vslice[h]] = (
            out[h] * (inv * valid) * gain[...] * (gate * sigmoid(gate))
        ).astype(bf16)

    @pl.when(chunk == pl.num_programs(0) - 1)
    def _():
        final_out[...] = state[...]


def mixer_forward(scal, pq, pk, pv, pg, small, cq, ck, cv, dlog, dbias, gain, s0):
    rows = pq.shape[0]
    heads, dk, dv = s0.shape
    chunks = rows // CHUNK
    per = chunks // 4

    def by_rows(width):
        return pl.BlockSpec((CHUNK, width), lambda c, s: (block_place(c, s[1], per), 0))

    def whole(*shape):
        return pl.BlockSpec(shape, lambda c, s: (0,) * len(shape))

    def by_chunk(*shape):
        return pl.BlockSpec((1,) + shape, lambda c, s: (c,) + (0,) * len(shape))

    kw, vw = heads * dk, heads * dv
    return pl.pallas_call(
        mixer_forward_kernel,
        grid_spec=pltpu.PrefetchScalarGridSpec(
            num_scalar_prefetch=1,
            grid=(chunks,),
            in_specs=[
                by_rows(kw), by_rows(kw), by_rows(vw), by_rows(vw), by_rows(2 * heads),
                whole(4, kw), whole(4, kw), whole(4, vw), whole(1, heads), whole(1, heads),
                whole(1, dv), whole(heads, dk, dv),
            ],
            out_specs=[
                by_rows(vw), whole(heads, dk, dv), by_rows(vw), by_rows(vw),
                by_chunk(heads, dk, dv), by_chunk(heads, CHUNK, CHUNK),
            ],
            scratch_shapes=[
                pltpu.VMEM((heads, dk, dv), f32),
                pltpu.VMEM((8, kw), f32), pltpu.VMEM((8, kw), f32), pltpu.VMEM((8, vw), f32),
            ],
        ),
        out_shape=[
            jax.ShapeDtypeStruct((rows, vw), bf16),
            jax.ShapeDtypeStruct((heads, dk, dv), f32),
            jax.ShapeDtypeStruct((rows, vw), bf16),
            jax.ShapeDtypeStruct((rows, vw), bf16),
            jax.ShapeDtypeStruct((chunks, heads, dk, dv), bf16),
            jax.ShapeDtypeStruct((chunks, heads, CHUNK, CHUNK), bf16),
        ],
        compiler_params=pltpu.CompilerParams(vmem_limit_bytes=48 * 1024 * 1024),
        cost_estimate=pl.CostEstimate(flops=20_000_000_000, bytes_accessed=24_000_000, transcendentals=4_000_000),
        name="mixer_forward",
    )(scal, pq, pk, pv, pg, small, cq, ck, cv, dlog, dbias, gain, s0)


def mixer_backward_kernel(
    scal, pq, pk, pv, pq16, pk16, pv16, small, do_in, delta_in, s_in, tt_in,
    cq, ck, cv, dlog_in, dbias_in,
    dpqk, dpv, dsmall, dcq, dck, dcv, ddecay,
    dstate, nq, nk, nv,
):
    step = pl.program_id(0)
    chunk = pl.num_programs(0) - 1 - step
    heads, dk, dv = dstate.shape
    every = range(heads)

    @pl.when(step == 0)
    def _():
        for ref in (dstate, nq, nk, nv, dcq, dck, dcv, ddecay):
            ref[...] = jnp.zeros_like(ref)

    down, across = chunk_masks()
    lower = down > across
    full = down >= across
    upper = down < across
    ufull = down <= across
    kslice = [slice(h * dk, (h + 1) * dk) for h in every]
    vslice = [slice(h * dv, (h + 1) * dv) for h in every]
    has_before = jnp.where(chunk > 0, 1.0, 0.0)

    def preact(ref, ref16, taps, where):
        pre = conv_rows(
            ref[:, where].astype(f32), ref16[:, where].astype(f32)[8:] * has_before, taps[:, where]
        )
        sig = sigmoid(pre)
        return pre, sig

    def conv_back(dpre, ref, ref16, taps, where, later, dtaps, dref, base=0):
        rows = ref[:, where].astype(f32)
        longer = jnp.concatenate([ref16[:, where].astype(f32)[8:] * has_before, rows], axis=0)
        after = jnp.concatenate([dpre, later[:, where]], axis=0)
        total = dpre * taps[3:4, where]
        sums = [jnp.sum(dpre * longer[5 + tap : 5 + tap + CHUNK], axis=0, keepdims=True) for tap in range(3)]
        sums.append(jnp.sum(dpre * rows, axis=0, keepdims=True))
        for tap in range(3):
            total = total + after[3 - tap : 3 - tap + CHUNK] * taps[tap : tap + 1, where]
        dtaps[:, where] += jnp.concatenate(sums, axis=0)
        later[:, where] = dpre[:8]
        dref[:, where.start + base : where.stop + base] = total.astype(bf16)

    row_at = chunk * CHUNK + lax.broadcasted_iota(jnp.int32, (CHUNK, 1), 0)
    valid = jnp.where(row_at < scal[0], 1.0, 0.0)
    tri = jnp.where(full, 1.0, 0.0)
    gcol, grow = decay_terms(small[...], dlog_in[...], dbias_in[...], valid, tri)
    last_row = lax.broadcasted_iota(jnp.int32, (CHUNK, 1), 0) == CHUNK - 1
    kpre, ksig, kinv, kunit, keys = [], [], [], [], []
    qpre, qsig, qinv, qunit, queries = [], [], [], [], []
    for h in every:
        pre, sig = preact(pk, pk16, ck, kslice[h])
        u = pre * sig
        inv = unit_factor(u)
        kpre.append(pre), ksig.append(sig), kinv.append(inv), kunit.append(u * inv)
        keys.append(kunit[h].astype(bf16))
    for h in every:
        pre, sig = preact(pq, pq16, cq, kslice[h])
        u = pre * sig
        inv = unit_factor(u)
        qpre.append(pre), qsig.append(sig), qinv.append(inv), qunit.append(u * inv)
        queries.append((qunit[h] * dk ** (-0.5)).astype(bf16))
    gc = [gcol[:, h : h + 1] for h in every]
    gr = [grow[h : h + 1, :] for h in every]
    bc = [gcol[:, heads + h : heads + h + 1] for h in every]
    br = [grow[heads + h : heads + h + 1, :] for h in every]
    do = [do_in[:, vslice[h]] for h in every]
    delta = [delta_in[:, vslice[h]] for h in every]
    dnext = [dstate[h].astype(bf16) for h in every]
    growth = [jnp.exp(gc[h]) for h in every]
    ending = [jnp.exp(gc[h][CHUNK - 1 : CHUNK] - gc[h]) for h in every]
    final = [jnp.exp(gc[h][CHUNK - 1 : CHUNK]) for h in every]
    gamma = [jnp.exp(jnp.where(full, gc[h] - gr[h], -1e30)) for h in every]
    gamma_t = [jnp.exp(jnp.where(ufull, gr[h] - gc[h], -1e30)) for h in every]
    kq = [mm_nt(keys[h], queries[h]) for h in every]
    keys_late = [(keys[h].astype(f32) * ending[h]).astype(bf16) for h in every]
    d_delta = [
        mm(
            jnp.concatenate([(kq[h] * gamma_t[h]).astype(bf16), keys_late[h]], axis=1),
            jnp.concatenate([do[h], dnext[h]], axis=0),
        ).astype(bf16)
        for h in every
    ]
    dr = [mm(tt_in[0, h], d_delta[h]) for h in every]
    dr_low = [dr[h].astype(bf16) for h in every]
    both = [jnp.concatenate([do[h], dr_low[h]], axis=0) for h in every]
    pair = [
        jnp.concatenate(
            [
                (queries[h].astype(f32) * growth[h]).astype(bf16),
                (keys[h].astype(f32) * (-growth[h] * bc[h])).astype(bf16),
            ],
            axis=0,
        )
        for h in every
    ]
    state = [s_in[0, h] for h in every]
    new_dstate = [final[h] * dstate[h] + mm_tn(pair[h], both[h]) for h in every]
    dgamma_end = [
        jnp.sum(jnp.sum(state[h].astype(f32) * dstate[h], axis=0, keepdims=True), axis=1, keepdims=True)
        * final[h]
        for h in every
    ]
    d_keys_late = [mm_nt(delta[h], dnext[h]) * ending[h] for h in every]
    for h in every:
        dstate[h] = new_dstate[h]
    strict = [jnp.where(lower, gamma[h] * bc[h], 0.0) for h in every]
    strict_t = [jnp.where(upper, gamma_t[h] * br[h], 0.0) for h in every]
    outer = [mm_nt(both[h], delta[h]) for h in every]
    outer_t = [mm_nt(delta[h], both[h]) for h in every]
    inner = [
        jnp.concatenate(
            [(outer[h][:CHUNK] * gamma[h]).astype(bf16), (-outer[h][CHUNK:] * strict[h]).astype(bf16)], axis=0
        )
        for h in every
    ]
    inner_t = [
        jnp.concatenate(
            [
                (outer_t[h][:, :CHUNK] * gamma_t[h]).astype(bf16),
                (-outer_t[h][:, CHUNK:] * strict_t[h]).astype(bf16),
            ],
            axis=1,
        )
        for h in every
    ]
    by_state = [mm_nt(both[h], state[h]) for h in every]
    by_key = [mm(inner[h], keys[h]) for h in every]
    d_col = [
        mm(inner_t[h], jnp.concatenate([queries[h], keys[h]], axis=0)) + d_keys_late[h] for h in every
    ]
    scal_cols = []
    dbs = []
    for h in every:
        dq = by_key[h][:CHUNK] + by_state[h][:CHUNK] * growth[h]
        d_row = by_key[h][CHUNK:] - by_state[h][CHUNK:] * (growth[h] * bc[h])
        key_f = keys[h].astype(f32)
        q_along = jnp.sum(queries[h].astype(f32) * dq, axis=-1, keepdims=True)
        row_along = jnp.sum(key_f * d_row, axis=-1, keepdims=True)
        col_along = jnp.sum(key_f * d_col[h], axis=-1, keepdims=True)
        late_along = jnp.sum(key_f * d_keys_late[h], axis=-1, keepdims=True)
        at_end = dgamma_end[h] + jnp.sum(late_along, axis=0, keepdims=True)
        scal_cols.append(q_along + row_along - col_along + jnp.where(last_row, at_end, 0.0))
        dbs.append(jnp.sum(dr[h] * delta[h].astype(f32), axis=-1, keepdims=True))
        du = qinv[h] * (dq * dk ** (-0.5) - qunit[h] * q_along)
        dpre = du * (qsig[h] * (1.0 + qpre[h] * (1.0 - qsig[h])))
        conv_back(dpre, pq, pq16, cq, kslice[h], nq, dcq, dpqk)
        du = kinv[h] * (d_row + d_col[h] - kunit[h] * (row_along + col_along))
        dpre = du * (ksig[h] * (1.0 + kpre[h] * (1.0 - ksig[h])))
        conv_back(dpre, pk, pk16, ck, kslice[h], nk, dck, dpqk, heads * dk)
        pre, sig = preact(pv, pv16, cv, vslice[h])
        dpre = dr[h] * bc[h] * (sig * (1.0 + pre * (1.0 - sig)))
        conv_back(dpre, pv, pv16, cv, vslice[h], nv, dcv, dpv)
    da = exact(jnp.where(ufull, 1.0, 0.0), jnp.concatenate(scal_cols, axis=1))
    log_scale, shifted = dlog_in[...], small[:, :heads] + dbias_in[...]
    scale = -jnp.exp(log_scale) * valid
    dpa = da * scale * sigmoid(shifted)
    dpb = jnp.concatenate(dbs, axis=1) * sigmoid(-small[:, heads:])
    dsmall[...] = jnp.concatenate([dpa, dpb], axis=1).astype(bf16)
    along = jnp.concatenate([da * scale * softplus(shifted), dpa], axis=1)
    ddecay[...] += jnp.sum(along, axis=0, keepdims=True)


def mixer_backward(scal, pq, pk, pv, small, do, delta, s, tt, cq, ck, cv, dlog, dbias):
    rows = pq.shape[0]
    chunks, heads, dk, dv = s.shape
    kw, vw = heads * dk, heads * dv
    per = chunks // 4
    fine = CHUNK // 16

    def by_rows(width):
        return pl.BlockSpec((CHUNK, width), lambda c, s: (block_place(chunks - 1 - c, s[1], per), 0))

    def before(width):
        def place(c, s):
            earlier = jnp.maximum(chunks - 2 - c, 0)
            return (block_place(earlier, s[1], per) * fine + fine - 1, 0)

        return pl.BlockSpec((16, width), place)

    def whole(*shape):
        return pl.BlockSpec(shape, lambda c, s: (0,) * len(shape))

    def by_chunk(*shape):
        return pl.BlockSpec((1,) + shape, lambda c, s: (chunks - 1 - c,) + (0,) * len(shape))

    return pl.pallas_call(
        mixer_backward_kernel,
        grid_spec=pltpu.PrefetchScalarGridSpec(
            num_scalar_prefetch=1,
            grid=(chunks,),
            in_specs=[
                by_rows(kw), by_rows(kw), by_rows(vw),
                before(kw), before(kw), before(vw),
                by_rows(2 * heads), by_rows(vw), by_rows(vw),
                by_chunk(heads, dk, dv), by_chunk(heads, CHUNK, CHUNK),
                whole(4, kw), whole(4, kw), whole(4, vw), whole(1, heads), whole(1, heads),
            ],
            out_specs=[
                by_rows(2 * kw), by_rows(vw), by_rows(2 * heads),
                whole(4, kw), whole(4, kw), whole(4, vw), whole(1, 2 * heads),
            ],
            scratch_shapes=[
                pltpu.VMEM((heads, dk, dv), f32),
                pltpu.VMEM((8, kw), f32), pltpu.VMEM((8, kw), f32), pltpu.VMEM((8, vw), f32),
            ],
        ),
        out_shape=[
            jax.ShapeDtypeStruct((rows, 2 * kw), bf16),
            jax.ShapeDtypeStruct((rows, vw), bf16),
            jax.ShapeDtypeStruct((rows, 2 * heads), bf16),
            jax.ShapeDtypeStruct((4, kw), f32),
            jax.ShapeDtypeStruct((4, kw), f32),
            jax.ShapeDtypeStruct((4, vw), f32),
            jax.ShapeDtypeStruct((1, 2 * heads), f32),
        ],
        compiler_params=pltpu.CompilerParams(vmem_limit_bytes=48 * 1024 * 1024),
        cost_estimate=pl.CostEstimate(flops=22_000_000_000, bytes_accessed=28_000_000, transcendentals=6_000_000),
        name="mixer_backward",
    )(scal, pq, pk, pv, pq, pk, pv, small, do, delta, s, tt, cq, ck, cv, dlog, dbias)


def product_tn(left, right):
    return lax.dot_general(
        left, right, (((0,), (0,)), ((), ())), preferred_element_type=jnp.float32
    )


def product_nt(left, right):
    return lax.dot_general(
        left, right, (((1,), (1,)), ((), ())), preferred_element_type=jnp.float32
    )


def row_stats(rows):
    inverse = lax.rsqrt(jnp.mean(rows * rows, axis=-1, keepdims=True) + 1e-05)
    return (rows * inverse, inverse)


def norm_back(scaled, inverse, gain, upstream):
    along = upstream * gain
    inner = jnp.mean(along * scaled, axis=-1, keepdims=True)
    return (inverse * (along - scaled * inner), jnp.sum(upstream * scaled, axis=0))


VMEM_MOST = 56 * 1024 * 1024
COLUMNS = 512
MESH = pl.DeviceIdType.MESH


def flipped(place, mask, count):
    out, bit = 0, 1
    while bit < count:
        here = (place // bit) % 2
        out = out + bit * ((1 - here) if mask & bit else here)
        bit *= 2
    return out


def group_order(groups):
    order, bit = [0], groups // 2
    while bit >= 1:
        order = order + [place | bit for place in order]
        bit //= 2
    return order


def split_order(groups, place):
    half = groups // 2
    bit = place % 2
    return [2 * at + bit for at in range(half)] + [2 * at + 1 - bit for at in range(half)]


def column_order(kind, groups, place):
    if kind == "split":
        return split_order(groups, place)
    return [flipped(place, mask, groups) for mask in group_order(groups)]


def take_columns(array, kind):
    groups = lax.axis_size("dp")
    order = jnp.stack([jnp.asarray(at, jnp.int32) for at in column_order(kind, groups, lax.axis_index("dp"))])
    parts = array.reshape(array.shape[0], groups, array.shape[1] // groups)
    return jnp.take(parts, order, axis=1).reshape(array.shape)


def column_copies(kind, groups, source, target, sems):
    each = source.shape[1] // groups
    found = []
    for at, chunk in enumerate(column_order(kind, groups, lax.axis_index("dp"))):
        start = pl.multiple_of(chunk * each, each)
        found.append(
            pltpu.make_async_copy(
                source.at[:, pl.ds(start, each)], target.at[:, pl.ds(at * each, each)], sems.at[at]
            )
        )
    return found


class Gather:
    def __init__(self, own, held, whole, send_sem, recv_sem, out_sem, groups, kind):
        self.kind = kind
        self.own, self.held, self.whole, self.groups = own, held, whole, groups
        self.send_sem, self.recv_sem, self.out_sem = send_sem, recv_sem, out_sem
        place = lax.axis_index("tensor")
        self.beside = flipped(place, 1, 4)
        self.across = flipped(place, 2, 4)

    def copy(self, source, slot, to):
        rows = self.own.shape[0]
        return pltpu.make_async_remote_copy(
            src_ref=self.held.at[pl.ds(source * rows, rows)],
            dst_ref=self.held.at[pl.ds(slot * rows, rows)],
            send_sem=self.send_sem.at[slot - 1],
            recv_sem=self.recv_sem.at[slot - 1],
            device_id={"tensor": to},
            device_id_type=MESH,
        )

    def copies(self):
        return self.copy(0, 1, self.beside), self.copy(0, 2, self.across), self.copy(2, 3, self.beside)

    def outward(self):
        if self.groups == 1:
            return [pltpu.make_async_copy(self.held, self.whole, self.out_sem.at[0])]
        return column_copies(self.kind, self.groups, self.held, self.whole, self.out_sem)

    def begin(self):
        self.held[pl.ds(0, self.own.shape[0]), :] = self.own[...]
        barrier = pltpu.get_barrier_semaphore()
        for other in (self.beside, self.across):
            pl.semaphore_signal(barrier, inc=1, device_id={"tensor": other}, device_id_type=MESH)
        pl.semaphore_wait(barrier, 2)
        to_beside, to_across, _ = self.copies()
        to_across.start()
        to_beside.start()
        to_beside.wait_recv()

    def second(self):
        _, to_across, forward = self.copies()
        to_across.wait_recv()
        forward.start()
        forward.wait_recv()
        for copy in self.outward():
            copy.start()

    def end(self):
        for copy in self.copies():
            copy.wait_send()
        for copy in self.outward():
            copy.wait()

    def at(self, step, steps):
        pl.when(step == 0)(self.begin)
        pl.when(step == steps // 2)(self.second)

    def rows(self, half):
        count = 2 * self.own.shape[0]
        return self.held[pl.ds(pl.multiple_of(half * count, count), count), :]


def gather_call(kernel, name, collective, steps, own, operands, in_specs, out_specs, out_shape, flops, nbytes, kind, more=()):
    rows, width = own.shape
    groups = lax.axis_size("dp")
    if (width // groups) % 128:
        groups = 1

    def body(own_ref, *refs):
        count = len(operands)
        outs = refs[count : count + len(out_shape)]
        whole, held, send_sem, recv_sem, out_sem = refs[count + len(out_shape) :][:5]
        gather = Gather(own_ref, held, whole, send_sem, recv_sem, out_sem, groups, kind)
        outs = outs + refs[count + len(out_shape) + 5 :]
        step = pl.program_id(0)
        gather.at(step, steps)
        kernel(step, gather, *refs[:count], *outs)
        pl.when(step == steps - 1)(gather.end)

    outs = pl.pallas_call(
        body,
        name=name,
        grid=(steps,),
        in_specs=[pl.BlockSpec((rows, width), lambda j: (0, 0))] + in_specs,
        out_specs=out_specs + [pl.BlockSpec(memory_space=pl.ANY)],
        out_shape=out_shape + [jax.ShapeDtypeStruct((4 * rows, width), own.dtype)],
        scratch_shapes=[
            pltpu.VMEM((4 * rows, width), own.dtype),
            pltpu.SemaphoreType.DMA((3,)),
            pltpu.SemaphoreType.DMA((3,)),
            pltpu.SemaphoreType.DMA((groups,)),
        ]
        + list(more),
        compiler_params=pltpu.CompilerParams(
            vmem_limit_bytes=VMEM_MOST, collective_id=collective, has_side_effects=True
        ),
        cost_estimate=pl.CostEstimate(flops=flops, bytes_accessed=nbytes, transcendentals=0),
    )(own, *operands)
    if groups == 1:
        outs = list(outs[:-1]) + [take_columns(outs[-1], kind)]
    return outs


def project_kernel(step, gather, wq, wk, wv, wg, ws, pq, pk, pv, pg, small):
    steps = [(wq, pq), (wk, pk), (wv, pv), (wv, pv), (wg, pg), (wg, pg)]
    half = step // 6

    def run(weight, out):
        out[...] = mm(gather.rows(half), weight[...]).astype(bf16)

    for at, (weight, out) in enumerate(steps):
        pl.when(step % 6 == at)(lambda weight=weight, out=out: run(weight, out))

    @pl.when(step % 6 == 0)
    def _():
        small[...] = mm(gather.rows(half), ws[...])


def project(own, weights):
    rows, width = own.shape
    pair = 2 * rows
    n_small = weights[4].shape[1]
    places = [
        lambda j: 0,
        lambda j: 0,
        lambda j: jnp.clip(j % 6 - 2, 0, 1),
        lambda j: jnp.clip(j % 6 - 4, 0, 1),
    ]
    in_specs = [pl.BlockSpec((width, COLUMNS), lambda j, place=place: (0, place(j))) for place in places]
    in_specs.append(pl.BlockSpec((width, n_small), lambda j: (0, 0)))
    out_specs = [pl.BlockSpec((pair, COLUMNS), lambda j, place=place: (j // 6, place(j))) for place in places]
    out_specs.append(pl.BlockSpec((pair, n_small), lambda j: (j // 6, 0)))
    out_shape = [jax.ShapeDtypeStruct((2 * pair, weight.shape[1]), bf16) for weight in weights[:4]]
    out_shape.append(jax.ShapeDtypeStruct((2 * pair, n_small), f32))
    return gather_call(
        project_kernel, "project", 0, 12, own, weights, in_specs, out_specs, out_shape,
        40_000_000_000, 40_000_000, "flip",
    )


def feed_kernel(blocks, step, gather, e, wg, wu, wd, hidden, d_gate, d_up, e_split, e_sem):
    groups = e_sem.shape[0]
    half = step // blocks
    count = e.shape[0] // 2

    def copies():
        if groups == 1:
            return [pltpu.make_async_copy(e, e_split, e_sem.at[0])]
        return column_copies("split", groups, e, e_split, e_sem)

    @pl.when(step == 0)
    def _():
        for copy in copies():
            copy.start()

    x = gather.rows(half)
    gate = mm_nt(x, wg[...])
    up = mm_nt(x, wu[...])
    back = mm_nt(e[pl.ds(pl.multiple_of(half * count, count), count), :], wd[...])
    sig = sigmoid(gate)
    act = gate * sig
    hidden[...] = (act * up).astype(bf16)
    d_gate[...] = (back * up * (sig + act * (1.0 - sig))).astype(bf16)
    d_up[...] = (back * act).astype(bf16)

    @pl.when(step == 2 * blocks - 1)
    def _():
        for copy in copies():
            copy.wait()


def feed(own, e, wg, wu, wd):
    rows, width = own.shape
    pair = 2 * rows
    units = wd.shape[0]
    blocks = pl.cdiv(units, COLUMNS)
    groups = lax.axis_size("dp")
    if (width // groups) % 128:
        groups = 1
    by_rows = pl.BlockSpec((COLUMNS, width), lambda j: (j % blocks, 0))
    outs = gather_call(
        lambda *refs: feed_kernel(blocks, *refs), "feed", 1, 2 * blocks, own, [e, wg, wu, wd],
        [pl.BlockSpec((2 * pair, width), lambda j: (0, 0)), by_rows, by_rows, by_rows],
        [pl.BlockSpec((pair, COLUMNS), lambda j: (j // blocks, j % blocks))] * 3
        + [pl.BlockSpec(memory_space=pl.ANY)],
        [jax.ShapeDtypeStruct((2 * pair, units), bf16)] * 3
        + [jax.ShapeDtypeStruct((2 * pair, width), bf16)],
        40_000_000_000, 40_000_000, "split", [pltpu.SemaphoreType.DMA((groups,))],
    )
    if groups == 1:
        outs[3] = take_columns(outs[3], "split")
    return outs


def gate_back_kernel(heads, step, gather, length, w, pg, o_in, gain, dpg, do, dgain):
    pair = 2 * gather.own.shape[0]
    each = pair // 2
    dv = gain.shape[1]
    half = step // 2

    @pl.when(step == 0)
    def _():
        dgain[...] = jnp.zeros_like(dgain)

    at = half * pair + lax.broadcasted_iota(jnp.int32, (pair, 1), 0)
    at = (at // each ^ lax.axis_index("tensor").astype(jnp.int32)) * each + at % each
    valid = jnp.where(at < length[0], 1.0, 0.0)
    upstream = mm_nt(gather.rows(half), w[...]) * valid
    for head in range(heads):
        where = slice(head * dv, (head + 1) * dv)
        dg = upstream[:, where]
        gate = pg[:, where].astype(f32)
        sig = sigmoid(gate)
        act = gate * sig
        o = o_in[:, where].astype(f32)
        inv = lax.rsqrt(jnp.mean(o * o, axis=-1, keepdims=True) + 1e-05)
        norm = o * inv
        through = dg * norm
        dgain[...] += jnp.sum(through * act, axis=0, keepdims=True)
        dpg[:, where] = (through * gain[...] * (sig + act * (1.0 - sig))).astype(bf16)
        dn = dg * gain[...] * act
        do[:, where] = (inv * (dn - norm * jnp.mean(dn * norm, axis=-1, keepdims=True))).astype(bf16)


def gate_back(own, length, w_out, pg, o, gain):
    rows, width = own.shape
    pair = 2 * rows
    dv = gain.shape[1]
    heads = w_out.shape[0] // dv // 2
    by_head = pl.BlockSpec((pair, heads * dv), lambda j: (j // 2, j % 2))
    return gather_call(
        lambda *refs: gate_back_kernel(heads, *refs), "gate_back", 2, 4, own, [length, w_out, pg, o, gain],
        [
            pl.BlockSpec(memory_space=pltpu.SMEM),
            pl.BlockSpec((heads * dv, width), lambda j: (j % 2, 0)),
            by_head, by_head,
            pl.BlockSpec((1, dv), lambda j: (0, 0)),
        ],
        [by_head, by_head, pl.BlockSpec((1, dv), lambda j: (0, 0))],
        [
            jax.ShapeDtypeStruct(pg.shape, bf16),
            jax.ShapeDtypeStruct(pg.shape, bf16),
            jax.ShapeDtypeStruct((1, dv), f32),
        ],
        30_000_000_000, 30_000_000, "flip",
    )


def scatter_kernel(turned, count, *refs):
    lefts, rights, out = refs[:count], refs[count : 2 * count], refs[2 * count]
    far_own, leave, other, send_sem, recv_sem = refs[2 * count + 1 :]
    step = pl.program_id(0)
    parts = pl.num_programs(0) // 2
    rows = out.shape[0]
    place = lax.axis_index("tensor")
    beside, across = flipped(place, 1, 4), flipped(place, 2, 4)
    multiply = mm_nt if turned else mm
    CORNER, NEAR, ACROSS = 0, 1, 2

    def columns(part):
        return pl.ds(pl.multiple_of(part * COLUMNS, COLUMNS), COLUMNS)

    def copy(kind, part):
        return pltpu.make_async_remote_copy(
            src_ref=leave.at[kind, :, columns(part)],
            dst_ref=other.at[kind, :, columns(part)],
            send_sem=send_sem.at[kind, part],
            recv_sem=recv_sem.at[kind, part],
            device_id={"tensor": across if kind == ACROSS else beside},
            device_id_type=MESH,
        )

    def product():
        total = multiply(lefts[0][...], rights[0][...])
        for at in range(1, count):
            total = total + multiply(lefts[at][...], rights[at][...])
        return total

    def pass_on(part):
        copy(CORNER, part).wait_recv()
        both = far_own[:, columns(part)] + other[CORNER, :, columns(part)].astype(f32)
        leave[ACROSS, :, columns(part)] = both.astype(bf16)
        copy(ACROSS, part).start()

    @pl.when(step == 0)
    def _():
        barrier = pltpu.get_barrier_semaphore()
        for to in (beside, across):
            pl.semaphore_signal(barrier, inc=1, device_id={"tensor": to}, device_id_type=MESH)
        pl.semaphore_wait(barrier, 2)

    part = step % parts

    @pl.when(step < parts)
    def _():
        total = product()
        far_own[:, columns(part)] = total[:rows]
        leave[CORNER, :, columns(part)] = total[rows:].astype(bf16)
        copy(CORNER, part).start()

        @pl.when(step > 0)
        def _():
            pass_on(part - 1)

    @pl.when(step >= parts)
    def _():
        @pl.when(step == parts)
        def _():
            pass_on(parts - 1)

        total = product()
        out[:, columns(part)] = total[:rows]
        leave[NEAR, :, columns(part)] = total[rows:].astype(bf16)
        copy(NEAR, part).start()

    @pl.when(step == 2 * parts - 1)
    def _():
        def finish(part, carry):
            copy(NEAR, part).wait_recv()
            copy(ACROSS, part).wait_recv()
            where = columns(part)
            out[:, where] = (
                out[:, where] + other[NEAR, :, where].astype(f32) + other[ACROSS, :, where].astype(f32)
            )
            for kind in (CORNER, NEAR, ACROSS):
                copy(kind, part).wait_send()
            return carry

        lax.fori_loop(0, parts, finish, 0)


def scatter_products(lefts, rights, turned, collective):
    lefts = [left if isinstance(left, tuple) else (left, 0, left.shape[1]) for left in lefts]
    rows = lefts[0][0].shape[0] // 4
    width = rights[0].shape[0 if turned else 1]
    parts = width // COLUMNS
    total = sum(left[2] for left in lefts)
    flops = 8 * rows * width * total

    def left_spec(block, size):
        return pl.BlockSpec((2 * rows, size), lambda j: (1 - j // parts, block))

    def right_spec(right):
        if turned:
            return pl.BlockSpec((COLUMNS, right.shape[1]), lambda j: (j % parts, 0))
        return pl.BlockSpec((right.shape[0], COLUMNS), lambda j: (0, j % parts))

    return pl.pallas_call(
        lambda *refs: scatter_kernel(turned, len(lefts), *refs),
        name="scatter_products",
        grid=(2 * parts,),
        in_specs=[left_spec(block, size) for _, block, size in lefts] + [right_spec(right) for right in rights],
        out_specs=pl.BlockSpec((rows, width), lambda j: (0, 0)),
        out_shape=jax.ShapeDtypeStruct((rows, width), f32),
        scratch_shapes=[
            pltpu.VMEM((rows, width), f32),
            pltpu.VMEM((3, rows, width), bf16),
            pltpu.VMEM((3, rows, width), bf16),
            pltpu.SemaphoreType.DMA((3, parts)),
            pltpu.SemaphoreType.DMA((3, parts)),
        ],
        compiler_params=pltpu.CompilerParams(
            vmem_limit_bytes=VMEM_MOST, collective_id=collective, has_side_effects=True
        ),
        cost_estimate=pl.CostEstimate(flops=2 * flops, bytes_accessed=4 * total * width, transcendentals=0),
    )(*[left[0] for left in lefts], *rights)


def low_bit(chunk, groups):
    return groups if chunk == 0 else chunk & -chunk


def reduce_plan(groups, early, late):
    chunks = [chunk for chunk in group_order(groups) if chunk % 2 == 0]
    chunks.sort(key=lambda chunk: low_bit(chunk, groups))
    levels = max(groups.bit_length() - 2, 1)
    plan = []
    for at, tensor in enumerate(late):
        for position, chunk in enumerate(chunks):
            level = low_bit(chunk, groups).bit_length() - 2
            lag = 2.5 * level / levels if chunk == 0 else 0.5 * level
            plan.append((at * len(chunks) + position + lag, tensor, chunk))
    for at, tensor in enumerate(early):
        for position, chunk in enumerate(chunks):
            level = low_bit(chunk, groups).bit_length() - 2
            plan.append((2 * at - 1 + 2 * level + 0.01 * position, tensor, chunk))
    return [step[1:] for step in sorted(plan)], chunks


def reduce_kernel(groups, count, *refs):
    leaves, refs = refs[:count], refs[count:]
    small, gains, partial, resid, refs = refs[0], refs[1], refs[2], refs[3], refs[4:]
    outs, refs = refs[:count], refs[count:]
    small_out, gains_out, mixed, refs = refs[0], refs[1], refs[2], refs[3:]
    lands, refs = refs[:count], refs[count:]
    sends, refs = refs[:count], refs[count:]
    keeps, refs = refs[:count], refs[count:]
    small_land, gains_land, gains_first, rows_leave, rows_land = refs[:5]
    send_sem, recv_sem, sum_send, sum_recv, rows_send, rows_recv, keep_sem = refs[5:]
    place = lax.axis_index("dp")
    beside = lax.axis_index("tensor")
    order = group_order(groups)
    position = {chunk: at for at, chunk in enumerate(order)}
    bits = [1 << at for at in range(groups.bit_length() - 1)]
    each = outs[0].shape[0]
    across_core = {"tensor": flipped(beside, 1, 4)}
    across_chip = {"tensor": flipped(beside, 2, 4)}

    def rows(at):
        return pl.ds(at * each, each)

    def copy(tensor, chunk):
        source = (
            leaves[tensor].at[rows(position[chunk])] if chunk % 2 else sends[tensor].at[rows(chunk // 2 - 1)]
        )
        return pltpu.make_async_remote_copy(
            src_ref=source,
            dst_ref=lands[tensor].at[rows(chunk - 1)],
            send_sem=send_sem.at[tensor * groups + chunk],
            recv_sem=recv_sem.at[tensor * groups + chunk],
            device_id={"dp": flipped(place, low_bit(chunk, groups), groups)},
            device_id_type=MESH,
        )

    def keep_copy(tensor):
        return pltpu.make_async_copy(
            leaves[tensor].at[pl.ds(0, keeps[tensor].shape[0])], keeps[tensor], keep_sem.at[tensor]
        )

    for tensor in range(count):
        keep_copy(tensor).start()
    kept = set()
    partners = [{"dp": flipped(place, bit, groups)} for bit in bits] + [across_core, across_chip]
    barrier = pltpu.get_barrier_semaphore()
    for partner in partners:
        pl.semaphore_signal(barrier, inc=1, device_id=partner, device_id_type=MESH)
    pl.semaphore_wait(barrier, len(partners))

    plan, chunks = reduce_plan(groups, [], list(range(count)))
    pieces = [(tensor, chunk + 1) for tensor in range(count) for chunk in chunks]
    started = []

    def send_piece():
        if len(started) < len(pieces):
            copy(*pieces[len(started)]).start()
            started.append(1)

    for _ in range(3):
        send_piece()

    def plain_copy(source, land, sems, at, partner):
        return pltpu.make_async_remote_copy(
            src_ref=source, dst_ref=land, send_sem=sems[0].at[at], recv_sem=sems[1].at[at],
            device_id=partner, device_id_type=MESH,
        )

    quarter = mixed.shape[0]
    blocks = [pl.ds(at * quarter, quarter) for at in range(4)]
    row_sems = (rows_send, rows_recv)
    corner = plain_copy(partial.at[blocks[3]], rows_land.at[0], row_sems, 0, across_core)
    near = plain_copy(partial.at[blocks[1]], rows_land.at[1], row_sems, 1, across_core)
    far = plain_copy(rows_leave, rows_land.at[2], row_sems, 2, across_chip)
    corner.start()
    near.start()

    gains_first[0] = gains[...]
    small_land[0] = small[...]
    sum_sems = (sum_send, sum_recv)
    hops = [across_core, across_chip] + [{"dp": flipped(place, bit, groups)} for bit in bits]
    gains_copies = [
        plain_copy(gains_first.at[at], gains_land.at[at], sum_sems, at, partner)
        for at, partner in enumerate(hops)
    ]
    small_copies = [
        plain_copy(small_land.at[2 * at], small_land.at[2 * at + 1], sum_sems, len(hops) + at, partner)
        for at, partner in enumerate(hops[2:])
    ]
    gains_copies[0].start()
    small_copies[0].start()
    done = {"gains": 0, "small": 0}

    def next_sum():
        at = done["gains"]
        if at < len(gains_copies):
            gains_copies[at].wait_recv()
            total = gains_first[at] + gains_land[at]
            if at + 1 < len(gains_copies):
                gains_first[at + 1] = total
                gains_copies[at + 1].start()
            else:
                gains_out[...] = total
            done["gains"] += 1
        at = done["small"]
        if at < len(small_copies):
            small_copies[at].wait_recv()
            total = small_land[2 * at] + small_land[2 * at + 1]
            if at + 1 < len(small_copies):
                small_land[2 * at + 2] = total
                small_copies[at + 1].start()
            else:
                small_out[...] = total
            done["small"] += 1

    for index, (tensor, chunk) in enumerate(plan):
        if index == 1:
            corner.wait_recv()
            rows_leave[...] = (
                partial[blocks[2], :].astype(f32) + rows_land[0].astype(f32)
            ).astype(bf16)
            far.start()
        if tensor not in kept:
            keep_copy(tensor).wait()
            kept.add(tensor)
        total = keeps[tensor][rows(position[chunk]), :].astype(f32)
        for bit in bits:
            if bit >= low_bit(chunk, groups):
                break
            copy(tensor, chunk + bit).wait_recv()
            if bit == 1:
                send_piece()
            total = total + lands[tensor][rows(chunk + bit - 1), :].astype(f32)
        if chunk:
            sends[tensor][rows(chunk // 2 - 1), :] = total.astype(bf16)
            copy(tensor, chunk).start()
        else:
            outs[tensor][...] = total
        if index >= 2 and index % 2 == 0:
            next_sum()
        if index == 6:
            near.wait_recv()
            far.wait_recv()
            mixed[...] = (
                resid[...]
                + partial[blocks[0], :].astype(f32)
                + rows_land[1].astype(f32)
                + rows_land[2].astype(f32)
            ).astype(bf16)
    while done["gains"] < len(gains_copies):
        next_sum()
    for tensor in range(count):
        for chunk in range(1, groups):
            copy(tensor, chunk).wait_send()
    for sent in gains_copies + small_copies + [corner, near, far]:
        sent.wait_send()


def reduce_groups(grads, small, gains, partial, resid, collective):
    count = len(grads)
    groups = lax.axis_size("dp")
    bits = groups.bit_length() - 1
    each = grads[0].shape[0] // groups
    rows, width = resid.shape
    widths = [grad.shape[1] for grad in grads]
    vmem = pl.BlockSpec(memory_space=pltpu.VMEM)
    out_shape = [jax.ShapeDtypeStruct((each, size), f32) for size in widths]
    out_shape += [jax.ShapeDtypeStruct(small.shape, f32), jax.ShapeDtypeStruct(gains.shape, f32)]
    out_shape += [jax.ShapeDtypeStruct((rows, width), bf16)]
    return pl.pallas_call(
        lambda *refs: reduce_kernel(groups, count, *refs),
        name="reduce_groups",
        in_specs=[pl.BlockSpec(memory_space=pl.ANY)] * count + [vmem] * 4,
        out_specs=[vmem] * len(out_shape),
        out_shape=out_shape,
        scratch_shapes=[pltpu.VMEM(((groups - 1) * each, size), bf16) for size in widths]
        + [pltpu.VMEM(((groups // 2 - 1) * each, size), bf16) for size in widths]
        + [pltpu.VMEM((groups // 2 * each, size), bf16) for size in widths]
        + [
            pltpu.VMEM((2 * bits,) + small.shape, f32),
            pltpu.VMEM((bits + 2,) + gains.shape, f32),
            pltpu.VMEM((bits + 2,) + gains.shape, f32),
            pltpu.VMEM((rows, width), bf16),
            pltpu.VMEM((3, rows, width), bf16),
            pltpu.SemaphoreType.DMA((count * groups,)),
            pltpu.SemaphoreType.DMA((count * groups,)),
            pltpu.SemaphoreType.DMA((2 * bits + 2,)),
            pltpu.SemaphoreType.DMA((2 * bits + 2,)),
            pltpu.SemaphoreType.DMA((3,)),
            pltpu.SemaphoreType.DMA((3,)),
            pltpu.SemaphoreType.DMA((count,)),
        ],
        compiler_params=pltpu.CompilerParams(
            vmem_limit_bytes=VMEM_MOST, collective_id=collective, has_side_effects=True
        ),
        cost_estimate=pl.CostEstimate(flops=100_000_000_000, bytes_accessed=300_000_000, transcendentals=0),
    )(*grads, small, gains, partial, resid)


def product_nn(left, right):
    return jnp.dot(left, right, preferred_element_type=jnp.float32)


def tie(value, after):
    return lax.optimization_barrier((value, after))[0]


def together(*values):
    return lax.optimization_barrier(values)


def flip(array, axis, bit):
    size = lax.axis_size(axis)
    return lax.ppermute(array, axis, [(place, place ^ bit) for place in range(size)])


def in_order(array):
    groups = lax.axis_size("dp")
    place = lax.axis_index("dp").astype(jnp.int32)
    found = jnp.array(group_order(groups), jnp.int32)[jnp.arange(groups, dtype=jnp.int32) ^ place]
    return jnp.take(array.reshape(array.shape[0], groups, -1), found, axis=1)


def leaving(left, right):
    quarter = right.shape[1] // 4
    return [
        product_tn(left, right[:, at * quarter : (at + 1) * quarter]).astype(jnp.bfloat16) for at in (2, 3)
    ]


def settle(left, right, others):
    half = right.shape[1] // 2
    other = jnp.concatenate(others, axis=1).astype(jnp.float32)
    total = (product_tn(left, right[:, :half]) + other).astype(jnp.bfloat16)
    groups = lax.axis_size("dp")
    alike = [[place for place in range(groups) if place % 2 == bit] for bit in (0, 1)]
    return lax.psum_scatter(
        total, "dp", scatter_dimension=1, axis_index_groups=alike, tiled=True
    ).astype(jnp.float32)


def pack(parts):
    flat = jnp.concatenate([part.reshape(-1) for part in parts])
    return jnp.pad(flat, (0, -flat.shape[0] % 1024)).reshape(-1, 1024)


def unpack(flat, parts):
    flat, at, out = flat.reshape(-1), 0, []
    for part in parts:
        out.append(flat[at : at + part.size].reshape(part.shape))
        at += part.size
    return out


def per_device(
    tokens,
    norm1_gain,
    w_query,
    w_key,
    w_value,
    w_gate_out,
    w_decay,
    w_beta,
    conv_query,
    conv_key,
    conv_value,
    decay_log,
    decay_bias,
    head_gain,
    w_out,
    norm2_gain,
    w_gate,
    w_up,
    w_down,
    state_in,
    seq_blocks,
    seq_tail,
    cotangent,
):
    width = tokens.shape[1]
    heads = decay_log.shape[0]
    rows_in = tokens.astype(jnp.float32)
    scaled1, inverse1 = row_stats(rows_in)
    normed1 = (scaled1 * norm1_gain).astype(jnp.bfloat16)
    seq_length = (BLOCK * (seq_blocks - 1) + seq_tail).astype(jnp.int32)
    place = lax.axis_index("tensor").astype(jnp.int32)
    scal = jnp.stack([seq_length[0], place])
    gain_row, log_row, bias_row = head_gain[None], decay_log[None], decay_bias[None]
    w_small = jnp.concatenate([w_decay, w_beta], axis=1)
    weights1 = (w_query, w_key, w_value, w_gate_out, w_small)
    p_query, p_key, p_value, p_gate, p_small, gathered1 = project(normed1, weights1)
    cotangent = tie(cotangent, p_small)
    e_beside, e_across = flip(cotangent, "tensor", 1), flip(cotangent, "tensor", 2)
    gated, final, mixer_out, delta, states, inverse_t = mixer_forward(
        scal, p_query, p_key, p_value, p_gate, p_small,
        conv_query, conv_key, conv_value, log_row, bias_row, gain_row, state_in[0],
    )
    gated, e_across = together(gated, e_across)
    e_corner = flip(e_across, "tensor", 1)
    cot_full = jnp.concatenate([cotangent, e_beside, e_across, e_corner], axis=0)
    resid = rows_in + scatter_products([gated], [w_out], False, 3)
    scaled2, inverse2 = row_stats(resid)
    normed2 = (scaled2 * norm2_gain).astype(jnp.bfloat16)
    hidden, d_gate, d_up, cot_split, split2 = feed(normed2, cot_full, w_gate.T, w_up.T, w_down)
    down_one, down_two = leaving(hidden, cot_split)
    d_gate, d_up, down_one = together(d_gate, d_up, down_one)
    down_one = flip(down_one, "dp", 1)
    d_normed2 = scatter_products([d_gate, d_up], [w_gate.T, w_up.T], False, 4)
    d_normed2, down_one, d_gate, d_up = together(d_normed2, down_one, d_gate, d_up)
    d_resid_part, grad_norm2 = norm_back(scaled2, inverse2, norm2_gain, d_normed2)
    d_resid = (cotangent.astype(jnp.float32) + d_resid_part).astype(jnp.bfloat16)
    d_resid, down_two = together(d_resid, down_two)
    down_two = flip(down_two, "dp", 1)
    dp_gate, do, dgain, resid_full = gate_back(d_resid, seq_length, w_out, p_gate, mixer_out, gain_row)
    do, dp_gate, dgain, resid_full, down_two = together(do, dp_gate, dgain, resid_full, down_two)
    grad_down = settle(hidden, cot_split, (down_one, down_two))
    up_one, up_two = leaving(d_up, split2)
    do, up_one, up_two = together(do, up_one, up_two)
    up_one, up_two = flip(up_one, "dp", 1), flip(up_two, "dp", 1)
    mixer_grads = mixer_backward(
        scal, p_query, p_key, p_value, p_small, do, delta, states, inverse_t,
        conv_query, conv_key, conv_value, log_row, bias_row,
    )
    dp_pair, dp_value, dp_small, dc_query, dc_key, dc_value, ddecay, up_one, up_two = together(
        *mixer_grads, up_one, up_two
    )
    grad_up = settle(d_up, split2, (up_one, up_two))
    gate_one, gate_two = leaving(d_gate, split2)
    dp_small, gate_one, gate_two = together(dp_small, gate_one, gate_two)
    gate_one, gate_two = flip(gate_one, "dp", 1), flip(gate_two, "dp", 1)
    key_width = w_query.shape[1]
    d_normed1 = scatter_products(
        [(dp_pair, 0, key_width), (dp_pair, 1, key_width), dp_value, dp_gate, dp_small],
        weights1, True, 5,
    )
    grad_out = product_tn(resid_full, gated).astype(jnp.bfloat16)
    grad_gate_out = product_tn(gathered1, dp_gate).astype(jnp.bfloat16)
    grad_value = product_tn(gathered1, dp_value).astype(jnp.bfloat16)
    grad_pair = product_tn(gathered1, dp_pair).astype(jnp.bfloat16)
    grad_small = in_order(product_tn(dp_small, gathered1))
    d_normed1, gate_one, gate_two = together(d_normed1, gate_one, gate_two)
    grad_gate = settle(d_gate, split2, (gate_one, gate_two))
    d_tokens_part, grad_norm1 = norm_back(scaled1, inverse1, norm1_gain, d_normed1)
    tokens_grad = (d_resid.astype(jnp.float32) + d_tokens_part).astype(jnp.bfloat16)
    partial = product_nn(hidden, w_down).astype(jnp.bfloat16)
    small_parts = [dc_query, dc_key, dc_value, ddecay, grad_small]
    gain_parts = [grad_norm1, grad_norm2, dgain]
    grad_out, grad_gate_out, grad_value, grad_pair, small_sum, gain_sum, mixed = reduce_groups(
        [grad_out, grad_gate_out, grad_value, grad_pair],
        pack(small_parts), pack(gain_parts), partial, resid, 6,
    )
    dc_query, dc_key, dc_value, ddecay, grad_small = unpack(small_sum, small_parts)
    grad_norm1, grad_norm2, dgain = unpack(gain_sum, gain_parts)
    grad_small = lax.dynamic_index_in_dim(grad_small, lax.axis_index("dp"), 1, keepdims=False).T
    return (
        mixed,
        final[None],
        tokens_grad,
        grad_norm1,
        grad_pair[:, :key_width],
        grad_pair[:, key_width:],
        grad_value,
        grad_gate_out,
        grad_small[:, :heads],
        grad_small[:, heads:],
        dc_query,
        dc_key,
        dc_value,
        ddecay[0, :heads],
        ddecay[0, heads:],
        dgain[0],
        grad_out.T,
        grad_norm2,
        grad_gate.T,
        grad_up.T,
        grad_down,
    )


def solution(mesh):
    in_specs = (
        P(("dp", "tensor"), None),
        P(),
        P(None, "tensor"),
        P(None, "tensor"),
        P(None, "tensor"),
        P(None, "tensor"),
        P(None, "tensor"),
        P(None, "tensor"),
        P(None, "tensor"),
        P(None, "tensor"),
        P(None, "tensor"),
        P("tensor"),
        P("tensor"),
        P(),
        P("tensor", None),
        P(),
        P(None, "tensor"),
        P(None, "tensor"),
        P("tensor", None),
        P("dp", "tensor", None, None),
        P("dp"),
        P("dp"),
        P(("dp", "tensor"), None),
    )
    out_specs = (
        P(("dp", "tensor"), None),
        P("dp", "tensor", None, None),
        P(("dp", "tensor"), None),
        P(),
        P("dp", "tensor"),
        P("dp", "tensor"),
        P("dp", "tensor"),
        P("dp", "tensor"),
        P("dp", "tensor"),
        P("dp", "tensor"),
        P(None, "tensor"),
        P(None, "tensor"),
        P(None, "tensor"),
        P("tensor"),
        P("tensor"),
        P(),
        P("tensor", "dp"),
        P(),
        P("dp", "tensor"),
        P("dp", "tensor"),
        P("tensor", "dp"),
    )
    return jax.shard_map(
        per_device, mesh=mesh, in_specs=in_specs, out_specs=out_specs, check_vma=False
    )
```

```python
import jax
import jax.numpy as jnp
from jax import lax
from jax.experimental import pallas as pl
from jax.experimental.pallas import tpu as pltpu
from jax.sharding import PartitionSpec as P

BLOCK = 64

CHUNK = 128
LITTLE = pl.CostEstimate(flops=1, bytes_accessed=1, transcendentals=0)
f32 = jnp.float32
bf16 = jnp.bfloat16


def mm(left, right):
    return lax.dot_general(
        left.astype(bf16), right.astype(bf16), (((1,), (0,)), ((), ())), preferred_element_type=f32
    )


def mm_nt(left, right):
    return lax.dot_general(
        left.astype(bf16), right.astype(bf16), (((1,), (1,)), ((), ())), preferred_element_type=f32
    )


def mm_tn(left, right):
    return lax.dot_general(
        left.astype(bf16), right.astype(bf16), (((0,), (0,)), ((), ())), preferred_element_type=f32
    )


def conv_rows(rows, before, taps):
    count = rows.shape[0]
    longer = jnp.concatenate([before, rows], axis=0)
    total = rows * taps[3:4]
    for tap in range(3):
        total = total + longer[5 + tap : 5 + tap + count] * taps[tap : tap + 1]
    return total


def sigmoid(value):
    return 1.0 / (1.0 + jnp.exp(-value))


def unit_factor(rows):
    return lax.rsqrt(jnp.sum(rows * rows, axis=-1, keepdims=True) + 1e-06)


def chunk_masks():
    down = lax.broadcasted_iota(jnp.int32, (CHUNK, CHUNK), 0)
    across = lax.broadcasted_iota(jnp.int32, (CHUNK, CHUNK), 1)
    return down, across


def softplus(value):
    return jnp.maximum(value, 0.0) + jnp.log1p(jnp.exp(-jnp.abs(value)))


def exact(left, right):
    return jnp.dot(left, right, preferred_element_type=f32, precision=lax.Precision.HIGHEST)


def block_place(chunk, place, per):
    return ((chunk // per) ^ place) * per + chunk % per


def decay_terms(small, log_scale, bias, valid, tri):
    heads = log_scale.shape[1]
    decays = -jnp.exp(log_scale) * softplus(small[:, :heads] + bias) * valid
    running = exact(tri, decays)
    strength = sigmoid(small[:, heads:]) * valid
    cols = jnp.concatenate([running, strength], axis=1)
    wide = jnp.concatenate([cols, jnp.zeros((CHUNK, CHUNK - 2 * heads), f32)], axis=1)
    return cols, jnp.transpose(wide)[: 2 * heads]


def mixer_forward_kernel(
    scal, pq, pk, pv, pg, small, cq, ck, cv, dlog, dbias, gain, s0,
    gated_out, final_out, o_out, delta_out, s_out, tt_out,
    state, tq, tk, tv,
):
    chunk = pl.program_id(0)
    heads = s0.shape[0]
    dk, dv = s0.shape[1], s0.shape[2]
    every = range(heads)

    @pl.when(chunk == 0)
    def _():
        state[...] = s0[...]
        tq[...] = jnp.zeros_like(tq)
        tk[...] = jnp.zeros_like(tk)
        tv[...] = jnp.zeros_like(tv)

    down, across = chunk_masks()
    lower = down > across
    full = down >= across
    level = jnp.where(lower, down ^ across, 0)
    eye = jnp.where(down == across, 1.0, 0.0)
    eye_low = eye.astype(bf16)
    kslice = [slice(h * dk, (h + 1) * dk) for h in every]
    vslice = [slice(h * dv, (h + 1) * dv) for h in every]

    row_at = chunk * CHUNK + lax.broadcasted_iota(jnp.int32, (CHUNK, 1), 0)
    valid = jnp.where(row_at < scal[0], 1.0, 0.0)
    tri = jnp.where(full, 1.0, 0.0)
    gcol, grow = decay_terms(small[...], dlog[...], dbias[...], valid, tri)

    def activated(ref, tail, taps, where):
        pre = conv_rows(ref[:, where].astype(f32), tail[:, where], taps[:, where])
        return pre * sigmoid(pre)

    keys, queries, values = [], [], []
    for h in every:
        u = activated(pk, tk, ck, kslice[h])
        keys.append((u * unit_factor(u)).astype(bf16))
    for h in every:
        u = activated(pq, tq, cq, kslice[h])
        queries.append((u * (unit_factor(u) * dk ** (-0.5))).astype(bf16))
    gc = [gcol[:, h : h + 1] for h in every]
    bc = [gcol[:, heads + h : heads + h + 1] for h in every]
    products = [mm_nt(jnp.concatenate([keys[h], queries[h]], axis=0), keys[h]) for h in every]
    gam = [jnp.exp(jnp.where(full, gc[h] - grow[h : h + 1, :], -1e30)) for h in every]
    system = [jnp.where(lower, products[h][:CHUNK] * gam[h] * bc[h], 0.0) for h in every]
    attend = [(products[h][CHUNK:] * gam[h]).astype(bf16) for h in every]
    system_low = [system[h].astype(bf16) for h in every]
    first = jnp.where(level == 1, 1.0, 0.0).astype(bf16)
    inverse = [eye_low - system_low[h] * first for h in every]
    size = 2
    while size < CHUNK:
        mask = jnp.where((level >= size) & (level < 2 * size), 1.0, 0.0).astype(bf16)
        inner = [mm(system_low[h] * mask, inverse[h]).astype(bf16) for h in every]
        inverse = [inverse[h] - mm(inverse[h], inner[h]).astype(bf16) for h in every]
        size *= 2
    left_over = [
        (eye - inverse[h].astype(f32))
        - mm(system_low[h], inverse[h])
        - mm((system[h] - system_low[h].astype(f32)).astype(bf16), inverse[h])
        for h in every
    ]
    inverse = [(inverse[h].astype(f32) + mm(inverse[h], left_over[h])) for h in every]
    for h in every:
        tt_out[0, h] = jnp.transpose(inverse[h]).astype(bf16)
    inverse = [inverse[h].astype(bf16) for h in every]
    for h in every:
        values.append(activated(pv, tv, cv, vslice[h]))
    for ref, tail in ((pq, tq), (pk, tk), (pv, tv)):
        tail[...] = ref[CHUNK - 16 :, :].astype(f32)[8:]
    growth = [jnp.exp(gc[h]) for h in every]
    keys_f = [keys[h].astype(f32) for h in every]
    pair = [
        jnp.concatenate(
            [(keys_f[h] * growth[h]).astype(bf16), (queries[h].astype(f32) * growth[h]).astype(bf16)], axis=0
        )
        for h in every
    ]
    for h in every:
        s_out[0, h] = state[h].astype(bf16)
    carried = [mm(pair[h], state[h]) for h in every]
    delta = [
        mm(inverse[h], bc[h] * (values[h] - carried[h][:CHUNK])).astype(bf16) for h in every
    ]
    out = [carried[h][CHUNK:] + mm(attend[h], delta[h]) for h in every]
    for h in every:
        last = gc[h][CHUNK - 1 : CHUNK]
        late = (keys_f[h] * jnp.exp(last - gc[h])).astype(bf16)
        state[h] = jnp.exp(last) * state[h] + mm_tn(late, delta[h])
    for h in every:
        delta_out[:, vslice[h]] = delta[h]
        o_out[:, vslice[h]] = out[h].astype(bf16)
        inv = lax.rsqrt(jnp.mean(out[h] * out[h], axis=-1, keepdims=True) + 1e-05)
        gate = pg[:, vslice[h]].astype(f32)
        gated_out[:, vslice[h]] = (
            out[h] * (inv * valid) * gain[...] * (gate * sigmoid(gate))
        ).astype(bf16)

    @pl.when(chunk == pl.num_programs(0) - 1)
    def _():
        final_out[...] = state[...]


def mixer_forward(scal, pq, pk, pv, pg, small, cq, ck, cv, dlog, dbias, gain, s0):
    rows = pq.shape[0]
    heads, dk, dv = s0.shape
    chunks = rows // CHUNK
    per = chunks // 4

    def by_rows(width):
        return pl.BlockSpec((CHUNK, width), lambda c, s: (block_place(c, s[1], per), 0))

    def whole(*shape):
        return pl.BlockSpec(shape, lambda c, s: (0,) * len(shape))

    def by_chunk(*shape):
        return pl.BlockSpec((1,) + shape, lambda c, s: (c,) + (0,) * len(shape))

    kw, vw = heads * dk, heads * dv
    return pl.pallas_call(
        mixer_forward_kernel,
        grid_spec=pltpu.PrefetchScalarGridSpec(
            num_scalar_prefetch=1,
            grid=(chunks,),
            in_specs=[
                by_rows(kw), by_rows(kw), by_rows(vw), by_rows(vw), by_rows(2 * heads),
                whole(4, kw), whole(4, kw), whole(4, vw), whole(1, heads), whole(1, heads),
                whole(1, dv), whole(heads, dk, dv),
            ],
            out_specs=[
                by_rows(vw), whole(heads, dk, dv), by_rows(vw), by_rows(vw),
                by_chunk(heads, dk, dv), by_chunk(heads, CHUNK, CHUNK),
            ],
            scratch_shapes=[
                pltpu.VMEM((heads, dk, dv), f32),
                pltpu.VMEM((8, kw), f32), pltpu.VMEM((8, kw), f32), pltpu.VMEM((8, vw), f32),
            ],
        ),
        out_shape=[
            jax.ShapeDtypeStruct((rows, vw), bf16),
            jax.ShapeDtypeStruct((heads, dk, dv), f32),
            jax.ShapeDtypeStruct((rows, vw), bf16),
            jax.ShapeDtypeStruct((rows, vw), bf16),
            jax.ShapeDtypeStruct((chunks, heads, dk, dv), bf16),
            jax.ShapeDtypeStruct((chunks, heads, CHUNK, CHUNK), bf16),
        ],
        compiler_params=pltpu.CompilerParams(vmem_limit_bytes=56 * 1024 * 1024),
        cost_estimate=LITTLE,
        name="mixer_forward",
    )(scal, pq, pk, pv, pg, small, cq, ck, cv, dlog, dbias, gain, s0)


def mixer_backward_kernel(
    scal, pq, pk, pv, pq16, pk16, pv16, small, do_in, delta_in, s_in, tt_in,
    cq, ck, cv, dlog_in, dbias_in, left_one, right_one, left_two, right_two, left_three, right_three,
    dpqk, dpv, dsmall, dcq, dck, dcv, ddecay, product_one, product_two, product_three,
    dstate, nq, nk, nv,
):
    step = pl.program_id(0)
    chunk = pl.num_programs(0) - 1 - step
    heads, dk, dv = dstate.shape
    every = range(heads)

    @pl.when(step == 0)
    def _():
        for ref in (dstate, nq, nk, nv, dcq, dck, dcv, ddecay):
            ref[...] = jnp.zeros_like(ref)

    product_one[...] = mm_tn(left_one[...], right_one[...]).astype(bf16)
    product_two[...] = mm_tn(left_two[...], right_two[...]).astype(bf16)
    product_three[...] = mm(left_three[...], right_three[...]).astype(bf16)
    down, across = chunk_masks()
    lower = down > across
    full = down >= across
    upper = down < across
    ufull = down <= across
    kslice = [slice(h * dk, (h + 1) * dk) for h in every]
    vslice = [slice(h * dv, (h + 1) * dv) for h in every]
    has_before = jnp.where(chunk > 0, 1.0, 0.0)

    def preact(ref, ref16, taps, where):
        pre = conv_rows(
            ref[:, where].astype(f32), ref16[:, where].astype(f32)[8:] * has_before, taps[:, where]
        )
        sig = sigmoid(pre)
        return pre, sig

    def conv_back(dpre, ref, ref16, taps, where, later, dtaps, dref, base=0):
        rows = ref[:, where].astype(f32)
        longer = jnp.concatenate([ref16[:, where].astype(f32)[8:] * has_before, rows], axis=0)
        after = jnp.concatenate([dpre, later[:, where]], axis=0)
        total = dpre * taps[3:4, where]
        sums = [jnp.sum(dpre * longer[5 + tap : 5 + tap + CHUNK], axis=0, keepdims=True) for tap in range(3)]
        sums.append(jnp.sum(dpre * rows, axis=0, keepdims=True))
        for tap in range(3):
            total = total + after[3 - tap : 3 - tap + CHUNK] * taps[tap : tap + 1, where]
        dtaps[:, where] += jnp.concatenate(sums, axis=0)
        later[:, where] = dpre[:8]
        dref[:, where.start + base : where.stop + base] = total.astype(bf16)

    row_at = chunk * CHUNK + lax.broadcasted_iota(jnp.int32, (CHUNK, 1), 0)
    valid = jnp.where(row_at < scal[0], 1.0, 0.0)
    tri = jnp.where(full, 1.0, 0.0)
    gcol, grow = decay_terms(small[...], dlog_in[...], dbias_in[...], valid, tri)
    last_row = lax.broadcasted_iota(jnp.int32, (CHUNK, 1), 0) == CHUNK - 1
    kpre, ksig, kinv, kunit, keys = [], [], [], [], []
    qpre, qsig, qinv, qunit, queries = [], [], [], [], []
    for h in every:
        pre, sig = preact(pk, pk16, ck, kslice[h])
        u = pre * sig
        inv = unit_factor(u)
        kpre.append(pre), ksig.append(sig), kinv.append(inv), kunit.append(u * inv)
        keys.append(kunit[h].astype(bf16))
    for h in every:
        pre, sig = preact(pq, pq16, cq, kslice[h])
        u = pre * sig
        inv = unit_factor(u)
        qpre.append(pre), qsig.append(sig), qinv.append(inv), qunit.append(u * inv)
        queries.append((qunit[h] * dk ** (-0.5)).astype(bf16))
    gc = [gcol[:, h : h + 1] for h in every]
    gr = [grow[h : h + 1, :] for h in every]
    bc = [gcol[:, heads + h : heads + h + 1] for h in every]
    br = [grow[heads + h : heads + h + 1, :] for h in every]
    do = [do_in[:, vslice[h]] for h in every]
    delta = [delta_in[:, vslice[h]] for h in every]
    dnext = [dstate[h].astype(bf16) for h in every]
    growth = [jnp.exp(gc[h]) for h in every]
    ending = [jnp.exp(gc[h][CHUNK - 1 : CHUNK] - gc[h]) for h in every]
    final = [jnp.exp(gc[h][CHUNK - 1 : CHUNK]) for h in every]
    gamma = [jnp.exp(jnp.where(full, gc[h] - gr[h], -1e30)) for h in every]
    gamma_t = [jnp.exp(jnp.where(ufull, gr[h] - gc[h], -1e30)) for h in every]
    kq = [mm_nt(keys[h], queries[h]) for h in every]
    keys_late = [(keys[h].astype(f32) * ending[h]).astype(bf16) for h in every]
    d_delta = [
        mm(
            jnp.concatenate([(kq[h] * gamma_t[h]).astype(bf16), keys_late[h]], axis=1),
            jnp.concatenate([do[h], dnext[h]], axis=0),
        ).astype(bf16)
        for h in every
    ]
    dr = [mm(tt_in[0, h], d_delta[h]) for h in every]
    dr_low = [dr[h].astype(bf16) for h in every]
    both = [jnp.concatenate([do[h], dr_low[h]], axis=0) for h in every]
    pair = [
        jnp.concatenate(
            [
                (queries[h].astype(f32) * growth[h]).astype(bf16),
                (keys[h].astype(f32) * (-growth[h] * bc[h])).astype(bf16),
            ],
            axis=0,
        )
        for h in every
    ]
    state = [s_in[0, h] for h in every]
    new_dstate = [final[h] * dstate[h] + mm_tn(pair[h], both[h]) for h in every]
    dgamma_end = [
        jnp.sum(jnp.sum(state[h].astype(f32) * dstate[h], axis=0, keepdims=True), axis=1, keepdims=True)
        * final[h]
        for h in every
    ]
    d_keys_late = [mm_nt(delta[h], dnext[h]) * ending[h] for h in every]
    for h in every:
        dstate[h] = new_dstate[h]
    strict = [jnp.where(lower, gamma[h] * bc[h], 0.0) for h in every]
    strict_t = [jnp.where(upper, gamma_t[h] * br[h], 0.0) for h in every]
    outer = [mm_nt(both[h], delta[h]) for h in every]
    outer_t = [mm_nt(delta[h], both[h]) for h in every]
    inner = [
        jnp.concatenate(
            [(outer[h][:CHUNK] * gamma[h]).astype(bf16), (-outer[h][CHUNK:] * strict[h]).astype(bf16)], axis=0
        )
        for h in every
    ]
    inner_t = [
        jnp.concatenate(
            [
                (outer_t[h][:, :CHUNK] * gamma_t[h]).astype(bf16),
                (-outer_t[h][:, CHUNK:] * strict_t[h]).astype(bf16),
            ],
            axis=1,
        )
        for h in every
    ]
    by_state = [mm_nt(both[h], state[h]) for h in every]
    by_key = [mm(inner[h], keys[h]) for h in every]
    d_col = [
        mm(inner_t[h], jnp.concatenate([queries[h], keys[h]], axis=0)) + d_keys_late[h] for h in every
    ]
    scal_cols = []
    dbs = []
    for h in every:
        dq = by_key[h][:CHUNK] + by_state[h][:CHUNK] * growth[h]
        d_row = by_key[h][CHUNK:] - by_state[h][CHUNK:] * (growth[h] * bc[h])
        key_f = keys[h].astype(f32)
        q_along = jnp.sum(queries[h].astype(f32) * dq, axis=-1, keepdims=True)
        row_along = jnp.sum(key_f * d_row, axis=-1, keepdims=True)
        col_along = jnp.sum(key_f * d_col[h], axis=-1, keepdims=True)
        late_along = jnp.sum(key_f * d_keys_late[h], axis=-1, keepdims=True)
        at_end = dgamma_end[h] + jnp.sum(late_along, axis=0, keepdims=True)
        scal_cols.append(q_along + row_along - col_along + jnp.where(last_row, at_end, 0.0))
        dbs.append(jnp.sum(dr[h] * delta[h].astype(f32), axis=-1, keepdims=True))
        du = qinv[h] * (dq * dk ** (-0.5) - qunit[h] * q_along)
        dpre = du * (qsig[h] * (1.0 + qpre[h] * (1.0 - qsig[h])))
        conv_back(dpre, pq, pq16, cq, kslice[h], nq, dcq, dpqk)
        du = kinv[h] * (d_row + d_col[h] - kunit[h] * (row_along + col_along))
        dpre = du * (ksig[h] * (1.0 + kpre[h] * (1.0 - ksig[h])))
        conv_back(dpre, pk, pk16, ck, kslice[h], nk, dck, dpqk, heads * dk)
        pre, sig = preact(pv, pv16, cv, vslice[h])
        dpre = dr[h] * bc[h] * (sig * (1.0 + pre * (1.0 - sig)))
        conv_back(dpre, pv, pv16, cv, vslice[h], nv, dcv, dpv)
    da = exact(jnp.where(ufull, 1.0, 0.0), jnp.concatenate(scal_cols, axis=1))
    log_scale, shifted = dlog_in[...], small[:, :heads] + dbias_in[...]
    scale = -jnp.exp(log_scale) * valid
    dpa = da * scale * sigmoid(shifted)
    dpb = jnp.concatenate(dbs, axis=1) * sigmoid(-small[:, heads:])
    dsmall[...] = jnp.concatenate([dpa, dpb], axis=1).astype(bf16)
    along = jnp.concatenate([da * scale * softplus(shifted), dpa], axis=1)
    ddecay[...] += jnp.sum(along, axis=0, keepdims=True)


def mixer_backward(scal, pq, pk, pv, small, do, delta, s, tt, cq, ck, cv, dlog, dbias, one, two, three):
    rows = pq.shape[0]
    chunks, heads, dk, dv = s.shape
    kw, vw = heads * dk, heads * dv
    per = chunks // 4
    fine = CHUNK // 16
    (left_one, right_one), (left_two, right_two), (left_three, right_three) = one, two, three
    width = left_one.shape[1]
    each_one, each_two = width // chunks, width // 2 // chunks

    def by_rows(width):
        return pl.BlockSpec((CHUNK, width), lambda c, s: (block_place(chunks - 1 - c, s[1], per), 0))

    def before(width):
        def place(c, s):
            earlier = jnp.maximum(chunks - 2 - c, 0)
            return (block_place(earlier, s[1], per) * fine + fine - 1, 0)

        return pl.BlockSpec((16, width), place)

    def whole(*shape):
        return pl.BlockSpec(shape, lambda c, s: (0,) * len(shape))

    def by_chunk(*shape):
        return pl.BlockSpec((1,) + shape, lambda c, s: (chunks - 1 - c,) + (0,) * len(shape))

    return pl.pallas_call(
        mixer_backward_kernel,
        grid_spec=pltpu.PrefetchScalarGridSpec(
            num_scalar_prefetch=1,
            grid=(chunks,),
            in_specs=[
                by_rows(kw), by_rows(kw), by_rows(vw),
                before(kw), before(kw), before(vw),
                by_rows(2 * heads), by_rows(vw), by_rows(vw),
                by_chunk(heads, dk, dv), by_chunk(heads, CHUNK, CHUNK),
                whole(4, kw), whole(4, kw), whole(4, vw), whole(1, heads), whole(1, heads),
                pl.BlockSpec((rows, each_one), lambda c, s: (0, c)), whole(*right_one.shape),
                pl.BlockSpec((rows, each_two), lambda c, s: (0, chunks + c)), whole(*right_two.shape),
                pl.BlockSpec((CHUNK, left_three.shape[1]), lambda c, s: (c, 0)), whole(*right_three.shape),
            ],
            out_specs=[
                by_rows(2 * kw), by_rows(vw), by_rows(2 * heads),
                whole(4, kw), whole(4, kw), whole(4, vw), whole(1, 2 * heads),
                pl.BlockSpec((each_one, right_one.shape[1]), lambda c, s: (c, 0)),
                pl.BlockSpec((each_two, right_two.shape[1]), lambda c, s: (c, 0)),
                pl.BlockSpec((CHUNK, right_three.shape[1]), lambda c, s: (c, 0)),
            ],
            scratch_shapes=[
                pltpu.VMEM((heads, dk, dv), f32),
                pltpu.VMEM((8, kw), f32), pltpu.VMEM((8, kw), f32), pltpu.VMEM((8, vw), f32),
            ],
        ),
        out_shape=[
            jax.ShapeDtypeStruct((rows, 2 * kw), bf16),
            jax.ShapeDtypeStruct((rows, vw), bf16),
            jax.ShapeDtypeStruct((rows, 2 * heads), bf16),
            jax.ShapeDtypeStruct((4, kw), f32),
            jax.ShapeDtypeStruct((4, kw), f32),
            jax.ShapeDtypeStruct((4, vw), f32),
            jax.ShapeDtypeStruct((1, 2 * heads), f32),
            jax.ShapeDtypeStruct((width, right_one.shape[1]), bf16),
            jax.ShapeDtypeStruct((width // 2, right_two.shape[1]), bf16),
            jax.ShapeDtypeStruct((rows, right_three.shape[1]), bf16),
        ],
        compiler_params=pltpu.CompilerParams(vmem_limit_bytes=56 * 1024 * 1024),
        cost_estimate=LITTLE,
        name="mixer_backward",
    )(
        scal, pq, pk, pv, pq, pk, pv, small, do, delta, s, tt, cq, ck, cv, dlog, dbias,
        left_one, right_one, left_two, right_two, left_three, right_three,
    )


def product_tn(left, right):
    return lax.dot_general(
        left, right, (((0,), (0,)), ((), ())), preferred_element_type=jnp.float32
    )


def product_nt(left, right):
    return lax.dot_general(
        left, right, (((1,), (1,)), ((), ())), preferred_element_type=jnp.float32
    )


def row_stats(rows):
    inverse = lax.rsqrt(jnp.mean(rows * rows, axis=-1, keepdims=True) + 1e-05)
    return (rows * inverse, inverse)


def norm_back(scaled, inverse, gain, upstream):
    along = upstream * gain
    inner = jnp.mean(along * scaled, axis=-1, keepdims=True)
    return (inverse * (along - scaled * inner), jnp.sum(upstream * scaled, axis=0))


VMEM_MOST = 56 * 1024 * 1024
COLUMNS = 512
MESH = pl.DeviceIdType.MESH


def flipped(place, mask, count):
    out, bit = 0, 1
    while bit < count:
        here = (place // bit) % 2
        out = out + bit * ((1 - here) if mask & bit else here)
        bit *= 2
    return out


def group_order(groups):
    order, bit = [0], groups // 2
    while bit >= 1:
        order = order + [place | bit for place in order]
        bit //= 2
    return order


def split_order(groups, place):
    half = groups // 2
    bit = place % 2
    return [2 * at + bit for at in range(half)] + [2 * at + 1 - bit for at in range(half)]


def column_order(kind, groups, place):
    if kind == "split":
        return split_order(groups, place)
    return [flipped(place, mask, groups) for mask in group_order(groups)]


def take_columns(array, kind):
    groups = lax.axis_size("dp")
    order = jnp.stack([jnp.asarray(at, jnp.int32) for at in column_order(kind, groups, lax.axis_index("dp"))])
    parts = array.reshape(array.shape[0], groups, array.shape[1] // groups)
    return jnp.take(parts, order, axis=1).reshape(array.shape)


def column_copies(kind, groups, source, target, sems):
    each = source.shape[1] // groups
    found = []
    for at, chunk in enumerate(column_order(kind, groups, lax.axis_index("dp"))):
        start = pl.multiple_of(chunk * each, each)
        found.append(
            pltpu.make_async_copy(
                source.at[:, pl.ds(start, each)], target.at[:, pl.ds(at * each, each)], sems.at[at]
            )
        )
    return found


class Gather:
    def __init__(self, own, held, whole, send_sem, recv_sem, out_sem, groups, kind):
        self.kind = kind
        self.own, self.held, self.whole, self.groups = own, held, whole, groups
        self.send_sem, self.recv_sem, self.out_sem = send_sem, recv_sem, out_sem
        place = lax.axis_index("tensor")
        self.beside = flipped(place, 1, 4)
        self.across = flipped(place, 2, 4)

    def copy(self, source, slot, to):
        rows = self.own.shape[0]
        return pltpu.make_async_remote_copy(
            src_ref=self.held.at[pl.ds(source * rows, rows)],
            dst_ref=self.held.at[pl.ds(slot * rows, rows)],
            send_sem=self.send_sem.at[slot - 1],
            recv_sem=self.recv_sem.at[slot - 1],
            device_id={"tensor": to},
            device_id_type=MESH,
        )

    def copies(self):
        return self.copy(0, 1, self.beside), self.copy(0, 2, self.across), self.copy(2, 3, self.beside)

    def outward(self):
        if self.groups == 1:
            return [pltpu.make_async_copy(self.held, self.whole, self.out_sem.at[0])]
        return column_copies(self.kind, self.groups, self.held, self.whole, self.out_sem)

    def begin(self):
        self.held[pl.ds(0, self.own.shape[0]), :] = self.own[...]
        barrier = pltpu.get_barrier_semaphore()
        for other in (self.beside, self.across):
            pl.semaphore_signal(barrier, inc=1, device_id={"tensor": other}, device_id_type=MESH)
        pl.semaphore_wait(barrier, 2)
        to_beside, to_across, _ = self.copies()
        to_across.start()
        to_beside.start()

    def near(self):
        self.copies()[0].wait_recv()

    def second(self):
        _, to_across, forward = self.copies()
        to_across.wait_recv()
        forward.start()
        forward.wait_recv()
        for copy in self.outward():
            copy.start()

    def end(self):
        for copy in self.copies():
            copy.wait_send()
        for copy in self.outward():
            copy.wait()

    def at(self, step, steps):
        @pl.when(step == 0)
        def _():
            self.begin()
            self.near()

        pl.when(step == steps // 2)(self.second)

    def rows(self, half):
        count = 2 * self.own.shape[0]
        return self.held[pl.ds(pl.multiple_of(half * count, count), count), :]


def column_groups(width):
    groups = lax.axis_size("dp")
    return 1 if (width // groups) % 128 else groups


def gather_call(kernel, name, collective, own, operands, in_specs, out_specs, out_shape, cost, kind, more=(), grid=None):
    rows, width = own.shape
    groups = column_groups(width)
    count, made = len(operands), len(out_shape)

    def body(own_ref, *refs):
        outs = refs[count : count + made]
        whole, held, send_sem, recv_sem, out_sem = refs[count + made : count + made + 5]
        gather = Gather(own_ref, held, whole, send_sem, recv_sem, out_sem, groups, kind)
        rest = refs[count + made + 5 :]
        if grid is None:
            kernel(gather, *refs[:count], *outs, *rest)
            return
        step = pl.program_id(0)
        gather.at(step, grid)
        kernel(step, gather, *refs[:count], *outs, *rest)
        pl.when(step == grid - 1)(gather.end)

    own_spec = pl.BlockSpec(memory_space=pltpu.VMEM)
    if grid is not None:
        own_spec = pl.BlockSpec((rows, width), lambda j: (0, 0))
    outs = pl.pallas_call(
        body,
        name=name,
        grid=() if grid is None else (grid,),
        in_specs=[own_spec] + in_specs,
        out_specs=out_specs + [pl.BlockSpec(memory_space=pl.ANY)],
        out_shape=out_shape + [jax.ShapeDtypeStruct((4 * rows, width), own.dtype)],
        scratch_shapes=[
            pltpu.VMEM((4 * rows, width), own.dtype),
            pltpu.SemaphoreType.DMA((3,)),
            pltpu.SemaphoreType.DMA((3,)),
            pltpu.SemaphoreType.DMA((groups,)),
        ]
        + list(more),
        compiler_params=pltpu.CompilerParams(
            vmem_limit_bytes=VMEM_MOST, collective_id=collective, has_side_effects=True
        ),
        cost_estimate=LITTLE,
    )(own, *operands)
    if kind is not None and groups == 1:
        outs = list(outs[:-1]) + [take_columns(outs[-1], kind)]
    return outs


def project_kernel(gather, wq, wk, wv, wg, ws, pq, pk, pv, pg, small, held_w, stage, w_sem, o_sem):
    pair = 2 * gather.own.shape[0]
    pieces = []
    for weight, out in ((wq, pq), (wk, pk), (wv, pv), (wg, pg)):
        for start in range(0, weight.shape[1], COLUMNS):
            pieces.append((weight, out, start))

    def block(at):
        return pl.ds(at * COLUMNS, COLUMNS)

    def load(at):
        weight, _, start = pieces[at]
        return pltpu.make_async_copy(
            weight.at[:, pl.ds(start, COLUMNS)], held_w.at[:, block(at)], w_sem.at[at]
        )

    def store(half, at):
        _, out, start = pieces[at]
        rows = pl.ds(half * pair, pair)
        return pltpu.make_async_copy(
            stage.at[rows, block(at)], out.at[rows, pl.ds(start, COLUMNS)], o_sem.at[half * len(pieces) + at]
        )

    load(0).start()
    gather.begin()
    for at in range(1, len(pieces)):
        load(at).start()
    gather.near()
    for half in range(2):
        if half:
            gather.second()
        rows = pl.ds(half * pair, pair)
        for at in range(len(pieces)):
            if half == 0:
                load(at).wait()
            stage[rows, block(at)] = mm(gather.held[rows, :], held_w[:, block(at)]).astype(bf16)
            store(half, at).start()
        small[rows, :] = mm_nt(gather.held[rows, :], ws[...])
    for half in range(2):
        for at in range(len(pieces)):
            store(half, at).wait()
    gather.end()


def project(own, weights):
    rows, width = own.shape
    total = sum(weight.shape[1] for weight in weights[:4])
    blocks = total // COLUMNS
    hbm, vmem = pl.BlockSpec(memory_space=pl.ANY), pl.BlockSpec(memory_space=pltpu.VMEM)
    out_shape = [jax.ShapeDtypeStruct((4 * rows, weight.shape[1]), bf16) for weight in weights[:4]]
    out_shape.append(jax.ShapeDtypeStruct((4 * rows, weights[4].shape[0]), f32))
    return gather_call(
        project_kernel, "project", 0, own, weights, [hbm] * 4 + [vmem], [hbm] * 4 + [vmem], out_shape,
        (40_000_000_000, 40_000_000), "flip",
        [
            pltpu.VMEM((width, total), bf16),
            pltpu.VMEM((4 * rows, total), bf16),
            pltpu.SemaphoreType.DMA((blocks,)),
            pltpu.SemaphoreType.DMA((2 * blocks,)),
        ],
    )


def feed_kernel(
    gather, e0, e1, e2, e3, wg, wu, wd, hidden, d_gate, d_up, e_out,
    e, held_g, held_u, held_d, stage, e_sem, w_sem, o_sem,
):
    count = gather.own.shape[0]
    pair = 2 * count
    units = wg.shape[0]
    blocks = [(start, min(COLUMNS, units - start)) for start in range(0, units, COLUMNS)]
    outs = (hidden, d_gate, d_up)

    def load_rows(at):
        return pltpu.make_async_copy((e0, e1, e2, e3)[at], e.at[pl.ds(at * count, count)], e_sem.at[at])

    def save_rows():
        return pltpu.make_async_copy(e, e_out, e_sem.at[4])

    def load(at, which):
        where = pl.ds(*blocks[at])
        return pltpu.make_async_copy(
            (wg, wu, wd)[which].at[where], (held_g, held_u, held_d)[which].at[where], w_sem.at[3 * at + which]
        )

    def store(half, which):
        rows = pl.ds(half * pair, pair)
        return pltpu.make_async_copy(stage.at[which, rows], outs[which].at[rows], o_sem.at[3 * half + which])

    load(0, 0).start()
    gather.begin()
    for at in range(len(blocks)):
        for which in range(3):
            if at or which:
                load(at, which).start()
        if at == 0:
            for part in range(4):
                load_rows(part).start()
    gather.near()
    for part in range(4):
        load_rows(part).wait()
    save_rows().start()
    for half in range(2):
        if half:
            gather.second()
        rows = pl.ds(half * pair, pair)
        for at, (start, size) in enumerate(blocks):
            where = pl.ds(start, size)
            if half == 0:
                for which in range(3):
                    load(at, which).wait()
            gate = mm_nt(gather.held[rows, :], held_g[where, :])
            up = mm_nt(gather.held[rows, :], held_u[where, :])
            back = mm_nt(e[rows, :], held_d[where, :])
            sig = sigmoid(gate)
            act = gate * sig
            stage[0, rows, where] = (act * up).astype(bf16)
            stage[1, rows, where] = (back * up * (sig + act * (1.0 - sig))).astype(bf16)
            stage[2, rows, where] = (back * act).astype(bf16)
        for which in range(3):
            store(half, which).start()
    for half in range(2):
        for which in range(3):
            store(half, which).wait()
    save_rows().wait()
    gather.end()


def feed(own, e_blocks, wg, wu, wd):
    rows, width = own.shape
    units = wd.shape[0]
    blocks = pl.cdiv(units, COLUMNS)
    hbm = pl.BlockSpec(memory_space=pl.ANY)
    return gather_call(
        feed_kernel, "feed", 1, own, list(e_blocks) + [wg, wu, wd], [hbm] * 7, [hbm] * 4,
        [jax.ShapeDtypeStruct((4 * rows, units), bf16)] * 3
        + [jax.ShapeDtypeStruct((4 * rows, width), bf16)],
        (40_000_000_000, 40_000_000), "split",
        [pltpu.VMEM((4 * rows, width), bf16)]
        + [pltpu.VMEM((units, width), bf16)] * 3
        + [
            pltpu.VMEM((3, 4 * rows, units), bf16),
            pltpu.SemaphoreType.DMA((5,)),
            pltpu.SemaphoreType.DMA((3 * blocks,)),
            pltpu.SemaphoreType.DMA((6,)),
        ],
    )


def gate_back_kernel(heads, step, gather, length, w, pg, o_in, gain, left, right, dpg, do, dgain, leave):
    pair = 2 * gather.own.shape[0]
    each = pair // 2
    dv = gain.shape[1]
    half = step // 2

    @pl.when(step == 0)
    def _():
        dgain[...] = jnp.zeros_like(dgain)

    at = half * pair + lax.broadcasted_iota(jnp.int32, (pair, 1), 0)
    at = (at // each ^ lax.axis_index("tensor").astype(jnp.int32)) * each + at % each
    valid = jnp.where(at < length[0], 1.0, 0.0)
    upstream = mm_nt(gather.rows(half), w[...]) * valid
    for head in range(heads):
        where = slice(head * dv, (head + 1) * dv)
        dg = upstream[:, where]
        gate = pg[:, where].astype(f32)
        sig = sigmoid(gate)
        act = gate * sig
        o = o_in[:, where].astype(f32)
        inv = lax.rsqrt(jnp.mean(o * o, axis=-1, keepdims=True) + 1e-05)
        norm = o * inv
        through = dg * norm
        dgain[...] += jnp.sum(through * act, axis=0, keepdims=True)
        dpg[:, where] = (through * gain[...] * (sig + act * (1.0 - sig))).astype(bf16)
        dn = dg * gain[...] * act
        do[:, where] = (inv * (dn - norm * jnp.mean(dn * norm, axis=-1, keepdims=True))).astype(bf16)

    @pl.when(step == 1)
    def _():
        units = leave.shape[0]
        for start in range(0, units, COLUMNS):
            where = slice(start, min(start + COLUMNS, units))
            leave[where, :] = mm_tn(left[:, where], right[...]).astype(bf16)


def gate_back(own, length, w_out, pg, o, gain, left, right):
    rows, width = own.shape
    pair = 2 * rows
    dv = gain.shape[1]
    heads = w_out.shape[0] // dv // 2
    by_head = pl.BlockSpec((pair, heads * dv), lambda j: (j // 2, j % 2))
    return gather_call(
        lambda *refs: gate_back_kernel(heads, *refs), "gate_back", 2, own, [length, w_out, pg, o, gain, left, right],
        [
            pl.BlockSpec(memory_space=pltpu.SMEM),
            pl.BlockSpec((heads * dv, width), lambda j: (j % 2, 0)),
            by_head, by_head,
            pl.BlockSpec((1, dv), lambda j: (0, 0)),
            pl.BlockSpec(left.shape, lambda j: (0, 0)),
            pl.BlockSpec((right.shape[0], right.shape[1] // 2), lambda j: (0, 1)),
        ],
        [
            by_head, by_head,
            pl.BlockSpec((1, dv), lambda j: (0, 0)),
            pl.BlockSpec((left.shape[1], right.shape[1] // 2), lambda j: (0, 0)),
        ],
        [
            jax.ShapeDtypeStruct(pg.shape, bf16),
            jax.ShapeDtypeStruct(pg.shape, bf16),
            jax.ShapeDtypeStruct((1, dv), f32),
            jax.ShapeDtypeStruct((left.shape[1], right.shape[1] // 2), bf16),
        ],
        (30_000_000_000, 30_000_000), "flip", grid=4,
    )


def scatter_kernel(turned, count, filled, *refs):
    lefts, rights, refs = refs[:count], refs[count : 2 * count], refs[2 * count :]
    if filled:
        (fill_left, fill_right, out, fill), refs = refs[:4], refs[4:]
    else:
        out, refs = refs[0], refs[1:]
    far_own, leave, other, send_sem, recv_sem = refs
    step = pl.program_id(0)
    parts = pl.num_programs(0) // 2
    rows = out.shape[0]
    place = lax.axis_index("tensor")
    beside, across = flipped(place, 1, 4), flipped(place, 2, 4)
    multiply = mm_nt if turned else mm
    CORNER, NEAR, ACROSS = 0, 1, 2

    def columns(part):
        return pl.ds(pl.multiple_of(part * COLUMNS, COLUMNS), COLUMNS)

    def copy(kind, part):
        return pltpu.make_async_remote_copy(
            src_ref=leave.at[kind, :, columns(part)],
            dst_ref=other.at[kind, :, columns(part)],
            send_sem=send_sem.at[kind, part],
            recv_sem=recv_sem.at[kind, part],
            device_id={"tensor": across if kind == ACROSS else beside},
            device_id_type=MESH,
        )

    def product():
        total = multiply(lefts[0][...], rights[0][...])
        for at in range(1, count):
            total = total + multiply(lefts[at][...], rights[at][...])
        return total

    def pass_on(part):
        copy(CORNER, part).wait_recv()
        both = far_own[:, columns(part)] + other[CORNER, :, columns(part)].astype(f32)
        leave[ACROSS, :, columns(part)] = both.astype(bf16)
        copy(ACROSS, part).start()

    @pl.when(step == 0)
    def _():
        barrier = pltpu.get_barrier_semaphore()
        for to in (beside, across):
            pl.semaphore_signal(barrier, inc=1, device_id={"tensor": to}, device_id_type=MESH)
        pl.semaphore_wait(barrier, 2)

    part = step % parts

    @pl.when(step < parts)
    def _():
        total = product()
        far_own[:, columns(part)] = total[:rows]
        leave[CORNER, :, columns(part)] = total[rows:].astype(bf16)
        copy(CORNER, part).start()

        @pl.when(step > 0)
        def _():
            pass_on(part - 1)

    @pl.when(step >= parts)
    def _():
        @pl.when(step == parts)
        def _():
            pass_on(parts - 1)

        total = product()
        out[:, columns(part)] = total[:rows]
        leave[NEAR, :, columns(part)] = total[rows:].astype(bf16)
        copy(NEAR, part).start()

    @pl.when(step == 2 * parts - 1)
    def _():
        if filled:
            for start in range(0, fill.shape[0], COLUMNS):
                where = slice(start, start + COLUMNS)
                fill[where, :] = mm_tn(fill_left[:, where], fill_right[...]).astype(bf16)

        def finish(part, carry):
            copy(NEAR, part).wait_recv()
            copy(ACROSS, part).wait_recv()
            where = columns(part)
            out[:, where] = (
                out[:, where] + other[NEAR, :, where].astype(f32) + other[ACROSS, :, where].astype(f32)
            )
            for kind in (CORNER, NEAR, ACROSS):
                copy(kind, part).wait_send()
            return carry

        lax.fori_loop(0, parts, finish, 0)


def scatter_products(lefts, rights, turned, collective, fill=None):
    lefts = [left if isinstance(left, tuple) else (left, 0, left.shape[1]) for left in lefts]
    rows = lefts[0][0].shape[0] // 4
    width = rights[0].shape[0 if turned else 1]
    parts = width // COLUMNS
    total = sum(left[2] for left in lefts)
    flops = 8 * rows * width * total

    def left_spec(block, size):
        return pl.BlockSpec((2 * rows, size), lambda j: (1 - j // parts, block))

    def right_spec(right):
        if turned:
            return pl.BlockSpec((COLUMNS, right.shape[1]), lambda j: (j % parts, 0))
        return pl.BlockSpec((right.shape[0], COLUMNS), lambda j: (0, j % parts))

    in_specs = [left_spec(block, size) for _, block, size in lefts] + [right_spec(right) for right in rights]
    out_specs = [pl.BlockSpec((rows, width), lambda j: (0, 0))]
    out_shape = [jax.ShapeDtypeStruct((rows, width), f32)]
    if fill is not None:
        made = (fill[0].shape[1], fill[1].shape[1])
        in_specs += [pl.BlockSpec(part.shape, lambda j: (0, 0)) for part in fill]
        out_specs.append(pl.BlockSpec(made, lambda j: (0, 0)))
        out_shape.append(jax.ShapeDtypeStruct(made, bf16))
    outs = pl.pallas_call(
        lambda *refs: scatter_kernel(turned, len(lefts), fill is not None, *refs),
        name="scatter_products",
        grid=(2 * parts,),
        in_specs=in_specs,
        out_specs=out_specs,
        out_shape=out_shape,
        scratch_shapes=[
            pltpu.VMEM((rows, width), f32),
            pltpu.VMEM((3, rows, width), bf16),
            pltpu.VMEM((3, rows, width), bf16),
            pltpu.SemaphoreType.DMA((3, parts)),
            pltpu.SemaphoreType.DMA((3, parts)),
        ],
        compiler_params=pltpu.CompilerParams(
            vmem_limit_bytes=VMEM_MOST, collective_id=collective, has_side_effects=True
        ),
        cost_estimate=LITTLE,
    )(*[left[0] for left in lefts], *rights, *(fill or ()))
    return outs[0] if fill is None else outs


def turned_kernel(added, left, right, *refs):
    total = mm_tn(left[...], right[...])
    if added:
        total = total + refs[0][...].astype(f32)
    refs[-1][...] = total.astype(bf16)


def turned_product(left, right, left_half=None, right_half=None, other=None):
    rows = left.shape[0]
    count = left.shape[1] if left_half is None else left.shape[1] // 2
    width = right.shape[1] if right_half is None else right.shape[1] // 2
    skip = (left_half or 0) * (count // COLUMNS)
    out = pl.BlockSpec((COLUMNS, width), lambda j: (j, 0))
    more = [] if other is None else [other]
    return pl.pallas_call(
        lambda *refs: turned_kernel(len(more), *refs),
        name="turned_product",
        grid=(pl.cdiv(count, COLUMNS),),
        in_specs=[
            pl.BlockSpec((rows, COLUMNS), lambda j: (0, skip + j)),
            pl.BlockSpec((rows, width), lambda j: (0, right_half or 0)),
        ]
        + [out] * len(more),
        out_specs=out,
        out_shape=jax.ShapeDtypeStruct((count, width), bf16),
        compiler_params=pltpu.CompilerParams(vmem_limit_bytes=VMEM_MOST),
        cost_estimate=LITTLE,
    )(left, right, *more)


def low_bit(chunk, groups):
    return groups if chunk == 0 else chunk & -chunk


def reduce_plan(groups, early, late):
    chunks = [chunk for chunk in group_order(groups) if chunk % 2 == 0]
    chunks.sort(key=lambda chunk: low_bit(chunk, groups))
    levels = max(groups.bit_length() - 2, 1)
    plan = []
    for at, tensor in enumerate(late):
        for position, chunk in enumerate(chunks):
            level = low_bit(chunk, groups).bit_length() - 2
            lag = LAST * level / levels if chunk == 0 else NEXT * level
            plan.append((at * len(chunks) + position + lag, tensor, chunk))
    for at, tensor in enumerate(early):
        for position, chunk in enumerate(chunks):
            level = low_bit(chunk, groups).bit_length() - 2
            plan.append((EARLY[0] * at - 1 + EARLY[1] * level + 0.01 * position, tensor, chunk))
    return [step[1:] for step in sorted(plan)], chunks


PARTS = 2
AHEAD = 4
EARLY = (2, 6)
LAST, NEXT = 2.5, 0.5


def reduce_kernel(groups, early, shapes, *refs):
    count = len(shapes)
    late = list(range(len(early), count))
    leaves, refs = refs[:count], refs[count:]
    (taps_q, taps_k, taps_v, decay, thin, gain_one, gain_two, gain_head, partial_in, resid), refs = (
        refs[:10], refs[10:],
    )
    outs = []
    for shape in shapes:
        outs.append(refs[: len(shape)])
        refs = refs[len(shape) :]
    (out_q, out_k, out_v, out_decay, out_thin, out_one, out_two, out_head, mixed), refs = refs[:9], refs[9:]
    lands, refs = refs[:count], refs[count:]
    sends, refs = refs[:count], refs[count:]
    keeps, refs = refs[:count], refs[count:]
    small_land, gains_land, gains_first, rows_leave, rows_land, partial = refs[:6]
    send_sem, recv_sem, sum_send, sum_recv, rows_send, rows_recv, keep_sem, load_sem = refs[6:]
    place = lax.axis_index("dp")
    beside = lax.axis_index("tensor")
    order = group_order(groups)
    position = {chunk: at for at, chunk in enumerate(order)}
    bits = [1 << at for at in range(groups.bit_length() - 1)]
    each = sends[0].shape[0] // (groups // 2 - 1)
    across_core = {"tensor": flipped(beside, 1, 4)}
    across_chip = {"tensor": flipped(beside, 2, 4)}

    size = each // PARTS

    def rows(at, part):
        return pl.ds(at * each + part * size, size)

    def slot(unit, chunk):
        tensor, part = unit
        return rows(chunk // 2 - 1 if tensor in early else chunk - 1, part)

    def copy(unit, chunk):
        tensor, part = unit
        if chunk % 2:
            source = leaves[tensor].at[rows(position[chunk], part)]
        else:
            source = sends[tensor].at[rows(chunk // 2 - 1, part)]
        at = (tensor * PARTS + part) * groups + chunk
        return pltpu.make_async_remote_copy(
            src_ref=source,
            dst_ref=lands[tensor].at[slot(unit, chunk)],
            send_sem=send_sem.at[at],
            recv_sem=recv_sem.at[at],
            device_id={"dp": flipped(place, low_bit(chunk, groups), groups)},
            device_id_type=MESH,
        )

    def keep_copy(tensor):
        return pltpu.make_async_copy(
            leaves[tensor].at[pl.ds(0, keeps[tensor].shape[0])], keeps[tensor], keep_sem.at[tensor]
        )

    for tensor in range(count):
        keep_copy(tensor).start()
    kept = set()
    partners = [{"dp": flipped(place, bit, groups)} for bit in bits] + [across_core, across_chip]
    barrier = pltpu.get_barrier_semaphore()
    for partner in partners:
        pl.semaphore_signal(barrier, inc=1, device_id=partner, device_id_type=MESH)
    pl.semaphore_wait(barrier, len(partners))

    early_units = [(tensor, part) for tensor in early for part in range(PARTS)]
    late_units = [(tensor, part) for tensor in late for part in range(PARTS)]
    plan, chunks = reduce_plan(groups, early_units, late_units)
    pieces = [(unit, chunk + 1) for unit in late_units for chunk in chunks]
    started = []

    def send_piece():
        if len(started) < len(pieces):
            copy(*pieces[len(started)]).start()
            started.append(1)

    for _ in range(AHEAD):
        send_piece()

    def plain_copy(source, land, sems, at, partner):
        return pltpu.make_async_remote_copy(
            src_ref=source, dst_ref=land, send_sem=sems[0].at[at], recv_sem=sems[1].at[at],
            device_id=partner, device_id_type=MESH,
        )

    quarter = mixed.shape[0]
    blocks = [pl.ds(at * quarter, quarter) for at in range(4)]
    row_sems = (rows_send, rows_recv)
    corner = plain_copy(partial.at[blocks[3]], rows_land.at[0], row_sems, 0, across_core)
    near = plain_copy(partial.at[blocks[1]], rows_land.at[1], row_sems, 1, across_core)
    far = plain_copy(rows_leave, rows_land.at[2], row_sems, 2, across_chip)
    load = pltpu.make_async_copy(partial_in, partial, load_sem.at[0])
    load.start()

    kw, line = taps_q.shape[1], taps_v.shape[1]
    lines = gain_one.shape[1] // line
    gains_first[0] = jnp.zeros(gains_first.shape[1:], f32)
    small_land[0] = jnp.zeros(small_land.shape[1:], f32)
    small_land[0, 0:4, :] = taps_v[...]
    small_land[0, 4:8, :kw] = taps_q[...]
    small_land[0, 4:8, kw:] = taps_k[...]
    for at in range(lines):
        where = slice(at * line, (at + 1) * line)
        small_land[0, 8 + 8 * at : 16 + 8 * at, :] = thin[:, where]
        gains_first[0, at : at + 1, :] = gain_one[:, where]
        gains_first[0, lines + at : lines + at + 1, :] = gain_two[:, where]
    small_land[0, 8 + 8 * lines : 9 + 8 * lines, : decay.shape[1]] = decay[...]
    gains_first[0, 2 * lines : 2 * lines + 1, : gain_head.shape[1]] = gain_head[...]
    sum_sems = (sum_send, sum_recv)
    hops = [across_core, across_chip] + [{"dp": flipped(place, bit, groups)} for bit in bits]
    gains_copies = [
        plain_copy(gains_first.at[at], gains_land.at[at], sum_sems, at, partner)
        for at, partner in enumerate(hops)
    ]
    small_copies = [
        plain_copy(small_land.at[2 * at], small_land.at[2 * at + 1], sum_sems, len(hops) + at, partner)
        for at, partner in enumerate(hops[2:])
    ]
    gains_copies[0].start()
    small_copies[0].start()
    done = {"gains": 0, "small": 0}

    def next_sum():
        at = done["gains"]
        if at < len(gains_copies):
            gains_copies[at].wait_recv()
            total = gains_first[at] + gains_land[at]
            if at + 1 < len(gains_copies):
                gains_first[at + 1] = total
                gains_copies[at + 1].start()
            else:
                for row in range(lines):
                    where = slice(row * line, (row + 1) * line)
                    out_one[:, where] = total[row : row + 1, :]
                    out_two[:, where] = total[lines + row : lines + row + 1, :]
                out_head[...] = total[2 * lines : 2 * lines + 1, : gain_head.shape[1]]
            done["gains"] += 1
        at = done["small"]
        if at < len(small_copies):
            small_copies[at].wait_recv()
            total = small_land[2 * at] + small_land[2 * at + 1]
            if at + 1 < len(small_copies):
                small_land[2 * at + 2] = total
                small_copies[at + 1].start()
            else:
                out_v[...] = total[0:4]
                out_q[...] = total[4:8, :kw]
                out_k[...] = total[4:8, kw:]
                for row in range(lines):
                    out_thin[:, row * line : (row + 1) * line] = total[8 + 8 * row : 16 + 8 * row]
                out_decay[...] = total[8 + 8 * lines : 9 + 8 * lines, : decay.shape[1]]
            done["small"] += 1

    def finish(tensor, part, total):
        where = slice(part * size, (part + 1) * size)
        for out, (start, count, turned) in zip(outs[tensor], shapes[tensor]):
            piece = total[:, start : start + count]
            if turned:
                out[:, where] = jnp.transpose(piece)
            else:
                out[where, :] = piece

    for index, (unit, chunk) in enumerate(plan):
        tensor, part = unit
        if index == 8:
            load.wait()
            corner.start()
            near.start()
        if index == 8:
            corner.wait_recv()
            rows_leave[...] = (
                partial[blocks[2], :].astype(f32) + rows_land[0].astype(f32)
            ).astype(bf16)
            far.start()
        if tensor not in kept:
            keep_copy(tensor).wait()
            kept.add(tensor)
        total = keeps[tensor][rows(position[chunk], part), :].astype(f32)
        for bit in bits:
            if bit >= low_bit(chunk, groups):
                break
            if bit == 1 and tensor in early:
                continue
            copy(unit, chunk + bit).wait_recv()
            if bit == 1:
                send_piece()
            total = total + lands[tensor][slot(unit, chunk + bit), :].astype(f32)
        if chunk:
            sends[tensor][rows(chunk // 2 - 1, part), :] = total.astype(bf16)
            copy(unit, chunk).start()
        else:
            finish(tensor, part, total)
        if index >= 4 and index % 4 == 0:
            next_sum()
        if index == 20:
            near.wait_recv()
            far.wait_recv()
            mixed[...] = (
                resid[...]
                + partial[blocks[0], :].astype(f32)
                + rows_land[1].astype(f32)
                + rows_land[2].astype(f32)
            ).astype(bf16)
    while done["gains"] < len(gains_copies):
        next_sum()
    for unit in early_units + late_units:
        for chunk in range(1, groups):
            if chunk % 2 == 0 or unit[0] in late:
                copy(unit, chunk).wait_send()
    for sent in gains_copies + small_copies + [corner, near, far]:
        sent.wait_send()


def reduce_groups(early_grads, late_grads, shapes, small, partial, resid, collective):
    grads = list(early_grads) + list(late_grads)
    early = list(range(len(early_grads)))
    groups = lax.axis_size("dp")
    bits = groups.bit_length() - 1
    each = late_grads[0].shape[0] // groups
    rows, width = resid.shape
    widths = [grad.shape[1] for grad in grads]
    vmem = pl.BlockSpec(memory_space=pltpu.VMEM)
    out_shape = []
    for shape in shapes:
        for _, size, turned in shape:
            out_shape.append(jax.ShapeDtypeStruct((size, each) if turned else (each, size), f32))
    out_shape += [jax.ShapeDtypeStruct(part.shape, f32) for part in small]
    out_shape += [jax.ShapeDtypeStruct((rows, width), bf16)]
    line = small[2].shape[1]
    lines = width // line
    small_shape, gains_shape = (16 + 8 * lines, line), (8 * pl.cdiv(2 * lines + 1, 8), line)
    landed = [(groups // 2 if at in early else groups) - 1 for at in range(len(grads))]
    return pl.pallas_call(
        lambda *refs: reduce_kernel(groups, early, shapes, *refs),
        name="reduce_groups",
        in_specs=[pl.BlockSpec(memory_space=pl.ANY)] * len(grads) + [vmem] * len(small)
        + [pl.BlockSpec(memory_space=pl.ANY), vmem],
        out_specs=[vmem] * len(out_shape),
        out_shape=out_shape,
        scratch_shapes=[pltpu.VMEM((chunks * each, size), bf16) for chunks, size in zip(landed, widths)]
        + [pltpu.VMEM(((groups // 2 - 1) * each, size), bf16) for size in widths]
        + [pltpu.VMEM((groups // 2 * each, size), bf16) for size in widths]
        + [
            pltpu.VMEM((2 * bits,) + small_shape, f32),
            pltpu.VMEM((bits + 2,) + gains_shape, f32),
            pltpu.VMEM((bits + 2,) + gains_shape, f32),
            pltpu.VMEM((rows, width), bf16),
            pltpu.VMEM((3, rows, width), bf16),
            pltpu.VMEM((4 * rows, width), bf16),
            pltpu.SemaphoreType.DMA((len(grads) * PARTS * groups,)),
            pltpu.SemaphoreType.DMA((len(grads) * PARTS * groups,)),
            pltpu.SemaphoreType.DMA((2 * bits + 2,)),
            pltpu.SemaphoreType.DMA((2 * bits + 2,)),
            pltpu.SemaphoreType.DMA((3,)),
            pltpu.SemaphoreType.DMA((3,)),
            pltpu.SemaphoreType.DMA((len(grads),)),
            pltpu.SemaphoreType.DMA((1,)),
        ],
        compiler_params=pltpu.CompilerParams(
            vmem_limit_bytes=VMEM_MOST, collective_id=collective, has_side_effects=True
        ),
        cost_estimate=LITTLE,
    )(*grads, *small, partial, resid)


def product_nn(left, right):
    return jnp.dot(left, right, preferred_element_type=jnp.float32)


def tie(value, after):
    return lax.optimization_barrier((value, after))[0]


def together(*values):
    return lax.optimization_barrier(values)


def flip(array, axis, bit):
    size = lax.axis_size(axis)
    return lax.ppermute(array, axis, [(place, place ^ bit) for place in range(size)])


def in_order(array):
    groups = lax.axis_size("dp")
    place = lax.axis_index("dp").astype(jnp.int32)
    found = jnp.array(group_order(groups), jnp.int32)[jnp.arange(groups, dtype=jnp.int32) ^ place]
    return jnp.take(array.reshape(array.shape[0], groups, -1), found, axis=1)


def scatter_far(total):
    groups = lax.axis_size("dp")
    alike = [[place for place in range(groups) if place % 2 == bit] for bit in (0, 1)]
    return lax.psum_scatter(
        total, "dp", scatter_dimension=1, axis_index_groups=alike, tiled=True
    ).astype(jnp.float32)


def per_device(
    tokens,
    norm1_gain,
    w_query,
    w_key,
    w_value,
    w_gate_out,
    w_decay,
    w_beta,
    conv_query,
    conv_key,
    conv_value,
    decay_log,
    decay_bias,
    head_gain,
    w_out,
    norm2_gain,
    w_gate,
    w_up,
    w_down,
    state_in,
    seq_blocks,
    seq_tail,
    cotangent,
):
    width = tokens.shape[1]
    heads = decay_log.shape[0]
    rows_in = tokens.astype(jnp.float32)
    scaled1, inverse1 = row_stats(rows_in)
    normed1 = (scaled1 * norm1_gain).astype(jnp.bfloat16)
    seq_length = (BLOCK * (seq_blocks - 1) + seq_tail).astype(jnp.int32)
    place = lax.axis_index("tensor").astype(jnp.int32)
    scal = jnp.stack([seq_length[0], place])
    gain_row, log_row, bias_row = head_gain[None], decay_log[None], decay_bias[None]
    w_small = jnp.concatenate([w_decay.T, w_beta.T], axis=0)
    weights1 = (w_query, w_key, w_value, w_gate_out, w_small)
    p_query, p_key, p_value, p_gate, p_small, gathered1 = project(normed1, weights1)
    cotangent = tie(cotangent, p_small)
    e_beside, e_across = flip(cotangent, "tensor", 1), flip(cotangent, "tensor", 2)
    gated, final, mixer_out, delta, states, inverse_t = mixer_forward(
        scal, p_query, p_key, p_value, p_gate, p_small,
        conv_query, conv_key, conv_value, log_row, bias_row, gain_row, state_in[0],
    )
    gated, e_across = together(gated, e_across)
    e_corner = flip(e_across, "tensor", 1)
    resid = rows_in + scatter_products([gated], [w_out], False, 3)
    scaled2, inverse2 = row_stats(resid)
    normed2 = (scaled2 * norm2_gain).astype(jnp.bfloat16)
    hidden, d_gate, d_up, cot_full, split2 = feed(
        normed2, (cotangent, e_beside, e_across, e_corner), w_gate.T, w_up.T, w_down
    )
    grad_down = product_tn(hidden, cot_full).astype(jnp.bfloat16)
    half = width // 2
    up_other = product_tn(d_up, split2[:, half:]).astype(jnp.bfloat16)
    d_gate, d_up, grad_down, up_other = together(d_gate, d_up, grad_down, up_other)
    grad_down = lax.psum_scatter(grad_down, "dp", scatter_dimension=1, tiled=True).astype(jnp.float32)
    up_other = flip(up_other, "dp", 1)
    d_normed2 = scatter_products([d_gate, d_up], [w_gate.T, w_up.T], False, 4)
    d_resid_part, grad_norm2 = norm_back(scaled2, inverse2, norm2_gain, d_normed2)
    d_resid = (cotangent.astype(jnp.float32) + d_resid_part).astype(jnp.bfloat16)
    dp_gate, do, dgain, gate_other, resid_full = gate_back(
        d_resid, seq_length, w_out, p_gate, mixer_out, gain_row, d_gate, split2
    )
    do, dp_gate, dgain, resid_full, gate_other, up_other = together(
        do, dp_gate, dgain, resid_full, gate_other, up_other
    )
    gate_other = flip(gate_other, "dp", 1)
    up_kept = turned_product(d_up, split2, right_half=0, other=up_other)
    do, up_kept = together(do, up_kept)
    grad_up = scatter_far(up_kept)
    mixer_grads = mixer_backward(
        scal, p_query, p_key, p_value, p_small, do, delta, states, inverse_t,
        conv_query, conv_key, conv_value, log_row, bias_row, (gathered1, dp_gate), (resid_full, gated),
        (hidden, w_down),
    )
    (
        dp_pair, dp_value, dp_small, dc_query, dc_key, dc_value, ddecay, grad_gate_out, out_other, partial,
        grad_down, gate_other,
    ) = together(*mixer_grads, grad_down, gate_other)
    out_other = flip(out_other, "dp", 1)
    grad_gate = scatter_far(turned_product(d_gate, split2, right_half=0, other=gate_other))
    grad_value = turned_product(gathered1, dp_value)
    dp_value, grad_value = together(dp_value, grad_value)
    key_width = w_query.shape[1]
    d_normed1, grad_pair = scatter_products(
        [(dp_pair, 0, key_width), (dp_pair, 1, key_width), dp_value, dp_gate, dp_small],
        weights1[:4] + (w_small.T,), True, 5, (gathered1, dp_pair),
    )
    d_normed1, out_other = together(d_normed1, out_other)
    out_keep = turned_product(resid_full, gated, left_half=0, other=out_other)
    grad_small = in_order(product_tn(dp_small, gathered1))
    d_tokens_part, grad_norm1 = norm_back(scaled1, inverse1, norm1_gain, d_normed1)
    tokens_grad = (d_resid.astype(jnp.float32) + d_tokens_part).astype(jnp.bfloat16)
    value_width = w_value.shape[1]
    turn = (width // lax.axis_size("dp")) % 128 == 0
    thin = grad_small.reshape(grad_small.shape[0], width)
    small = [dc_query, dc_key, dc_value, ddecay, thin, grad_norm1[None], grad_norm2[None], dgain]
    (
        grad_out, grad_gate_out, grad_value, grad_query, grad_key,
        dc_query, dc_key, dc_value, ddecay, thin, grad_norm1, grad_norm2, dgain, mixed,
    ) = reduce_groups(
        [out_keep], [grad_gate_out, grad_value, grad_pair],
        [
            [(0, value_width, turn)],
            [(0, value_width, False)],
            [(0, value_width, False)],
            [(0, key_width, False), (key_width, key_width, False)],
        ],
        small, partial, resid, 6,
    )
    each = width // lax.axis_size("dp")
    grad_small = lax.dynamic_slice_in_dim(thin, lax.axis_index("dp") * each, each, 1).T
    return (
        mixed,
        final[None],
        tokens_grad,
        grad_norm1[0],
        grad_query,
        grad_key,
        grad_value,
        grad_gate_out,
        grad_small[:, :heads],
        grad_small[:, heads:],
        dc_query,
        dc_key,
        dc_value,
        ddecay[0, :heads],
        ddecay[0, heads:],
        dgain[0],
        grad_out if turn else grad_out.T,
        grad_norm2[0],
        grad_gate.T,
        grad_up.T,
        grad_down,
    )


def solution(mesh):
    in_specs = (
        P(("dp", "tensor"), None),
        P(),
        P(None, "tensor"),
        P(None, "tensor"),
        P(None, "tensor"),
        P(None, "tensor"),
        P(None, "tensor"),
        P(None, "tensor"),
        P(None, "tensor"),
        P(None, "tensor"),
        P(None, "tensor"),
        P("tensor"),
        P("tensor"),
        P(),
        P("tensor", None),
        P(),
        P(None, "tensor"),
        P(None, "tensor"),
        P("tensor", None),
        P("dp", "tensor", None, None),
        P("dp"),
        P("dp"),
        P(("dp", "tensor"), None),
    )
    out_specs = (
        P(("dp", "tensor"), None),
        P("dp", "tensor", None, None),
        P(("dp", "tensor"), None),
        P(),
        P("dp", "tensor"),
        P("dp", "tensor"),
        P("dp", "tensor"),
        P("dp", "tensor"),
        P("dp", "tensor"),
        P("dp", "tensor"),
        P(None, "tensor"),
        P(None, "tensor"),
        P(None, "tensor"),
        P("tensor"),
        P("tensor"),
        P(),
        P("tensor", "dp"),
        P(),
        P("dp", "tensor"),
        P("dp", "tensor"),
        P("tensor", "dp"),
    )
    return jax.shard_map(
        per_device, mesh=mesh, in_specs=in_specs, out_specs=out_specs, check_vma=False
    )
```

```python
import jax
import jax.numpy as jnp
from jax import lax
from jax.experimental import pallas as pl
from jax.experimental.pallas import tpu as pltpu
from jax.sharding import PartitionSpec as P

BLOCK = 64

CHUNK = 128
LITTLE = pl.CostEstimate(flops=1, bytes_accessed=1, transcendentals=0)
f32 = jnp.float32
bf16 = jnp.bfloat16


def mm(left, right):
    return lax.dot_general(
        left.astype(bf16), right.astype(bf16), (((1,), (0,)), ((), ())), preferred_element_type=f32
    )


def mm_nt(left, right):
    return lax.dot_general(
        left.astype(bf16), right.astype(bf16), (((1,), (1,)), ((), ())), preferred_element_type=f32
    )


def mm_tn(left, right):
    return lax.dot_general(
        left.astype(bf16), right.astype(bf16), (((0,), (0,)), ((), ())), preferred_element_type=f32
    )


def conv_rows(rows, before, taps):
    count = rows.shape[0]
    longer = jnp.concatenate([before, rows], axis=0)
    total = rows * taps[3:4]
    for tap in range(3):
        total = total + longer[5 + tap : 5 + tap + count] * taps[tap : tap + 1]
    return total


def sigmoid(value):
    return 1.0 / (1.0 + jnp.exp(-value))


def unit_factor(rows):
    return lax.rsqrt(jnp.sum(rows * rows, axis=-1, keepdims=True) + 1e-06)


def chunk_masks():
    down = lax.broadcasted_iota(jnp.int32, (CHUNK, CHUNK), 0)
    across = lax.broadcasted_iota(jnp.int32, (CHUNK, CHUNK), 1)
    return down, across


def softplus(value):
    return jnp.maximum(value, 0.0) + jnp.log1p(jnp.exp(-jnp.abs(value)))


def exact(left, right):
    return jnp.dot(left, right, preferred_element_type=f32, precision=lax.Precision.HIGHEST)


def block_place(chunk, place, per):
    return ((chunk // per) ^ place) * per + chunk % per


def decay_terms(small, log_scale, bias, valid, tri):
    heads = log_scale.shape[1]
    decays = -jnp.exp(log_scale) * softplus(small[:, :heads] + bias) * valid
    running = exact(tri, decays)
    strength = sigmoid(small[:, heads:]) * valid
    cols = jnp.concatenate([running, strength], axis=1)
    wide = jnp.concatenate([cols, jnp.zeros((CHUNK, CHUNK - 2 * heads), f32)], axis=1)
    return cols, jnp.transpose(wide)[: 2 * heads]


def mixer_forward_kernel(
    scal, pq, pk, pv, pg, small, cq, ck, cv, dlog, dbias, gain, s0,
    gated_out, final_out, o_out, delta_out, s_out, tt_out,
    state, tq, tk, tv,
):
    chunk = pl.program_id(0)
    heads = s0.shape[0]
    dk, dv = s0.shape[1], s0.shape[2]
    every = range(heads)

    @pl.when(chunk == 0)
    def _():
        state[...] = s0[...]
        tq[...] = jnp.zeros_like(tq)
        tk[...] = jnp.zeros_like(tk)
        tv[...] = jnp.zeros_like(tv)

    down, across = chunk_masks()
    lower = down > across
    full = down >= across
    level = jnp.where(lower, down ^ across, 0)
    eye = jnp.where(down == across, 1.0, 0.0)
    eye_low = eye.astype(bf16)
    kslice = [slice(h * dk, (h + 1) * dk) for h in every]
    vslice = [slice(h * dv, (h + 1) * dv) for h in every]

    subs = range(pq.shape[0] // CHUNK)
    units = [(sub, h) for sub in subs for h in every]
    parts = range(len(units))
    tri = jnp.where(full, 1.0, 0.0)
    valid, gcol, grow = [], [], []
    for sub in subs:
        row_at = (chunk * len(subs) + sub) * CHUNK + lax.broadcasted_iota(jnp.int32, (CHUNK, 1), 0)
        valid.append(jnp.where(row_at < scal[0], 1.0, 0.0))
        cols, rows = decay_terms(
            small[sub * CHUNK : (sub + 1) * CHUNK, :], dlog[...], dbias[...], valid[sub], tri
        )
        gcol.append(cols)
        grow.append(rows)

    def activated(ref, tail, taps, where):
        pre = conv_rows(ref[:, where].astype(f32), tail[:, where], taps[:, where])
        return pre * sigmoid(pre)

    def cut(array, sub):
        return array[sub * CHUNK : (sub + 1) * CHUNK]

    all_keys, all_queries, all_values = [], [], []
    for h in every:
        u = activated(pk, tk, ck, kslice[h])
        all_keys.append((u * unit_factor(u)).astype(bf16))
    for h in every:
        u = activated(pq, tq, cq, kslice[h])
        all_queries.append((u * (unit_factor(u) * dk ** (-0.5))).astype(bf16))
    keys = [cut(all_keys[h], sub) for sub, h in units]
    queries = [cut(all_queries[h], sub) for sub, h in units]
    gc = [gcol[sub][:, h : h + 1] for sub, h in units]
    bc = [gcol[sub][:, heads + h : heads + h + 1] for sub, h in units]
    products = [mm_nt(jnp.concatenate([keys[u], queries[u]], axis=0), keys[u]) for u in parts]
    gam = [
        jnp.exp(jnp.where(full, gc[u] - grow[sub][h : h + 1, :], -1e30))
        for u, (sub, h) in enumerate(units)
    ]
    system = [jnp.where(lower, products[u][:CHUNK] * gam[u] * bc[u], 0.0) for u in parts]
    attend = [(products[u][CHUNK:] * gam[u]).astype(bf16) for u in parts]
    system_low = [system[u].astype(bf16) for u in parts]
    first = jnp.where(level == 1, 1.0, 0.0).astype(bf16)
    inverse = [eye_low - system_low[u] * first for u in parts]
    size = 2
    while size < CHUNK:
        mask = jnp.where((level >= size) & (level < 2 * size), 1.0, 0.0).astype(bf16)
        inner = [mm(system_low[u] * mask, inverse[u]).astype(bf16) for u in parts]
        inverse = [inverse[u] - mm(inverse[u], inner[u]).astype(bf16) for u in parts]
        size *= 2
    left_over = [
        (eye - inverse[u].astype(f32))
        - mm(system_low[u], inverse[u])
        - mm((system[u] - system_low[u].astype(f32)).astype(bf16), inverse[u])
        for u in parts
    ]
    inverse = [(inverse[u].astype(f32) + mm(inverse[u], left_over[u])) for u in parts]
    for u, (sub, h) in enumerate(units):
        tt_out[sub, h] = jnp.transpose(inverse[u]).astype(bf16)
    inverse = [inverse[u].astype(bf16) for u in parts]
    for h in every:
        all_values.append(activated(pv, tv, cv, vslice[h]))
    for ref, tail in ((pq, tq), (pk, tk), (pv, tv)):
        tail[...] = ref[ref.shape[0] - 16 :, :].astype(f32)[8:]
    growth = [jnp.exp(gc[u]) for u in parts]
    keys_f = [keys[u].astype(f32) for u in parts]
    pair = [
        jnp.concatenate(
            [(keys_f[u] * growth[u]).astype(bf16), (queries[u].astype(f32) * growth[u]).astype(bf16)], axis=0
        )
        for u in parts
    ]
    now = [state[h] for h in every]
    for sub in subs:
        mine = [sub * heads + h for h in every]
        for h in every:
            s_out[sub, h] = now[h].astype(bf16)
        carried = [mm(pair[u], now[h]) for h, u in enumerate(mine)]
        delta = [
            mm(inverse[u], bc[u] * (cut(all_values[h], sub) - carried[h][:CHUNK])).astype(bf16)
            for h, u in enumerate(mine)
        ]
        out = [carried[h][CHUNK:] + mm(attend[u], delta[h]) for h, u in enumerate(mine)]
        for h, u in enumerate(mine):
            last = gc[u][CHUNK - 1 : CHUNK]
            late = (keys_f[u] * jnp.exp(last - gc[u])).astype(bf16)
            now[h] = jnp.exp(last) * now[h] + mm_tn(late, delta[h])
        here = slice(sub * CHUNK, (sub + 1) * CHUNK)
        for h in every:
            delta_out[here, vslice[h]] = delta[h]
            o_out[here, vslice[h]] = out[h].astype(bf16)
            inv = lax.rsqrt(jnp.mean(out[h] * out[h], axis=-1, keepdims=True) + 1e-05)
            gate = pg[here, vslice[h]].astype(f32)
            gated_out[here, vslice[h]] = (
                out[h] * (inv * valid[sub]) * gain[...] * (gate * sigmoid(gate))
            ).astype(bf16)
    for h in every:
        state[h] = now[h]

    @pl.when(chunk == pl.num_programs(0) - 1)
    def _():
        final_out[...] = state[...]


def mixer_forward(scal, pq, pk, pv, pg, small, cq, ck, cv, dlog, dbias, gain, s0):
    rows = pq.shape[0]
    heads, dk, dv = s0.shape
    chunks = rows // CHUNK
    per = chunks // 4
    joined = 2 if per % 2 == 0 else 1

    def by_rows(width):
        return pl.BlockSpec(
            (joined * CHUNK, width), lambda c, s: (block_place(c, s[1], per // joined), 0)
        )

    def whole(*shape):
        return pl.BlockSpec(shape, lambda c, s: (0,) * len(shape))

    def by_chunk(*shape):
        return pl.BlockSpec((joined,) + shape, lambda c, s: (c,) + (0,) * len(shape))

    kw, vw = heads * dk, heads * dv
    return pl.pallas_call(
        mixer_forward_kernel,
        grid_spec=pltpu.PrefetchScalarGridSpec(
            num_scalar_prefetch=1,
            grid=(chunks // joined,),
            in_specs=[
                by_rows(kw), by_rows(kw), by_rows(vw), by_rows(vw), by_rows(2 * heads),
                whole(4, kw), whole(4, kw), whole(4, vw), whole(1, heads), whole(1, heads),
                whole(1, dv), whole(heads, dk, dv),
            ],
            out_specs=[
                by_rows(vw), whole(heads, dk, dv), by_rows(vw), by_rows(vw),
                by_chunk(heads, dk, dv), by_chunk(heads, CHUNK, CHUNK),
            ],
            scratch_shapes=[
                pltpu.VMEM((heads, dk, dv), f32),
                pltpu.VMEM((8, kw), f32), pltpu.VMEM((8, kw), f32), pltpu.VMEM((8, vw), f32),
            ],
        ),
        out_shape=[
            jax.ShapeDtypeStruct((rows, vw), bf16),
            jax.ShapeDtypeStruct((heads, dk, dv), f32),
            jax.ShapeDtypeStruct((rows, vw), bf16),
            jax.ShapeDtypeStruct((rows, vw), bf16),
            jax.ShapeDtypeStruct((chunks, heads, dk, dv), bf16),
            jax.ShapeDtypeStruct((chunks, heads, CHUNK, CHUNK), bf16),
        ],
        compiler_params=pltpu.CompilerParams(vmem_limit_bytes=56 * 1024 * 1024),
        cost_estimate=LITTLE,
        name="mixer_forward",
    )(scal, pq, pk, pv, pg, small, cq, ck, cv, dlog, dbias, gain, s0)


def mixer_backward_kernel(
    pieces, scal, pq, pk, pv, pq16, pk16, pv16, small, do_in, delta_in, s_in, tt_in,
    cq, ck, cv, dlog_in, dbias_in, left_one, right_one, left_two, right_two, left_three, right_three,
    dpqk, dpv, dsmall, dcq, dck, dcv, ddecay, product_one, product_two, product_three,
    dstate, nq, nk, nv,
):
    step = pl.program_id(0)
    chunk = pl.num_programs(0) - 1 - step
    heads, dk, dv = dstate.shape
    every = range(heads)

    @pl.when(step == 0)
    def _():
        for ref in (dstate, nq, nk, nv, dcq, dck, dcv, ddecay):
            ref[...] = jnp.zeros_like(ref)

    product_one[...] = mm_tn(left_one[...], right_one[...]).astype(bf16)
    product_two[...] = mm_tn(left_two[...], right_two[...]).astype(bf16)

    @pl.when(step < pieces)
    def _():
        product_three[...] = mm_tn(left_three[...], right_three[...]).astype(bf16)

    down, across = chunk_masks()
    lower = down > across
    full = down >= across
    upper = down < across
    ufull = down <= across
    kslice = [slice(h * dk, (h + 1) * dk) for h in every]
    vslice = [slice(h * dv, (h + 1) * dv) for h in every]
    has_before = jnp.where(chunk > 0, 1.0, 0.0)

    def preact(ref, ref16, taps, where):
        pre = conv_rows(
            ref[:, where].astype(f32), ref16[:, where].astype(f32)[8:] * has_before, taps[:, where]
        )
        sig = sigmoid(pre)
        return pre, sig

    def conv_back(dpre, ref, ref16, taps, where, later, dtaps, dref, base=0):
        rows = ref[:, where].astype(f32)
        longer = jnp.concatenate([ref16[:, where].astype(f32)[8:] * has_before, rows], axis=0)
        after = jnp.concatenate([dpre, later[:, where]], axis=0)
        total = dpre * taps[3:4, where]
        sums = [jnp.sum(dpre * longer[5 + tap : 5 + tap + CHUNK], axis=0, keepdims=True) for tap in range(3)]
        sums.append(jnp.sum(dpre * rows, axis=0, keepdims=True))
        for tap in range(3):
            total = total + after[3 - tap : 3 - tap + CHUNK] * taps[tap : tap + 1, where]
        dtaps[:, where] += jnp.concatenate(sums, axis=0)
        later[:, where] = dpre[:8]
        dref[:, where.start + base : where.stop + base] = total.astype(bf16)

    row_at = chunk * CHUNK + lax.broadcasted_iota(jnp.int32, (CHUNK, 1), 0)
    valid = jnp.where(row_at < scal[0], 1.0, 0.0)
    tri = jnp.where(full, 1.0, 0.0)
    gcol, grow = decay_terms(small[...], dlog_in[...], dbias_in[...], valid, tri)
    last_row = lax.broadcasted_iota(jnp.int32, (CHUNK, 1), 0) == CHUNK - 1
    kpre, ksig, kinv, kunit, keys = [], [], [], [], []
    qpre, qsig, qinv, qunit, queries = [], [], [], [], []
    for h in every:
        pre, sig = preact(pk, pk16, ck, kslice[h])
        u = pre * sig
        inv = unit_factor(u)
        kpre.append(pre), ksig.append(sig), kinv.append(inv), kunit.append(u * inv)
        keys.append(kunit[h].astype(bf16))
    for h in every:
        pre, sig = preact(pq, pq16, cq, kslice[h])
        u = pre * sig
        inv = unit_factor(u)
        qpre.append(pre), qsig.append(sig), qinv.append(inv), qunit.append(u * inv)
        queries.append((qunit[h] * dk ** (-0.5)).astype(bf16))
    gc = [gcol[:, h : h + 1] for h in every]
    gr = [grow[h : h + 1, :] for h in every]
    bc = [gcol[:, heads + h : heads + h + 1] for h in every]
    br = [grow[heads + h : heads + h + 1, :] for h in every]
    do = [do_in[:, vslice[h]] for h in every]
    delta = [delta_in[:, vslice[h]] for h in every]
    dnext = [dstate[h].astype(bf16) for h in every]
    growth = [jnp.exp(gc[h]) for h in every]
    ending = [jnp.exp(gc[h][CHUNK - 1 : CHUNK] - gc[h]) for h in every]
    final = [jnp.exp(gc[h][CHUNK - 1 : CHUNK]) for h in every]
    gamma = [jnp.exp(jnp.where(full, gc[h] - gr[h], -1e30)) for h in every]
    gamma_t = [jnp.exp(jnp.where(ufull, gr[h] - gc[h], -1e30)) for h in every]
    kq = [mm_nt(keys[h], queries[h]) for h in every]
    keys_late = [(keys[h].astype(f32) * ending[h]).astype(bf16) for h in every]
    d_delta = [
        mm(
            jnp.concatenate([(kq[h] * gamma_t[h]).astype(bf16), keys_late[h]], axis=1),
            jnp.concatenate([do[h], dnext[h]], axis=0),
        ).astype(bf16)
        for h in every
    ]
    dr = [mm(tt_in[0, h], d_delta[h]) for h in every]
    dr_low = [dr[h].astype(bf16) for h in every]
    both = [jnp.concatenate([do[h], dr_low[h]], axis=0) for h in every]
    pair = [
        jnp.concatenate(
            [
                (queries[h].astype(f32) * growth[h]).astype(bf16),
                (keys[h].astype(f32) * (-growth[h] * bc[h])).astype(bf16),
            ],
            axis=0,
        )
        for h in every
    ]
    state = [s_in[0, h] for h in every]
    new_dstate = [final[h] * dstate[h] + mm_tn(pair[h], both[h]) for h in every]
    dgamma_end = [
        jnp.sum(jnp.sum(state[h].astype(f32) * dstate[h], axis=0, keepdims=True), axis=1, keepdims=True)
        * final[h]
        for h in every
    ]
    d_keys_late = [mm_nt(delta[h], dnext[h]) * ending[h] for h in every]
    for h in every:
        dstate[h] = new_dstate[h]
    strict = [jnp.where(lower, gamma[h] * bc[h], 0.0) for h in every]
    strict_t = [jnp.where(upper, gamma_t[h] * br[h], 0.0) for h in every]
    outer = [mm_nt(both[h], delta[h]) for h in every]
    outer_t = [mm_nt(delta[h], both[h]) for h in every]
    inner = [
        jnp.concatenate(
            [(outer[h][:CHUNK] * gamma[h]).astype(bf16), (-outer[h][CHUNK:] * strict[h]).astype(bf16)], axis=0
        )
        for h in every
    ]
    inner_t = [
        jnp.concatenate(
            [
                (outer_t[h][:, :CHUNK] * gamma_t[h]).astype(bf16),
                (-outer_t[h][:, CHUNK:] * strict_t[h]).astype(bf16),
            ],
            axis=1,
        )
        for h in every
    ]
    by_state = [mm_nt(both[h], state[h]) for h in every]
    by_key = [mm(inner[h], keys[h]) for h in every]
    d_col = [
        mm(inner_t[h], jnp.concatenate([queries[h], keys[h]], axis=0)) + d_keys_late[h] for h in every
    ]
    scal_cols = []
    dbs = []
    for h in every:
        dq = by_key[h][:CHUNK] + by_state[h][:CHUNK] * growth[h]
        d_row = by_key[h][CHUNK:] - by_state[h][CHUNK:] * (growth[h] * bc[h])
        key_f = keys[h].astype(f32)
        q_along = jnp.sum(queries[h].astype(f32) * dq, axis=-1, keepdims=True)
        row_along = jnp.sum(key_f * d_row, axis=-1, keepdims=True)
        col_along = jnp.sum(key_f * d_col[h], axis=-1, keepdims=True)
        late_along = jnp.sum(key_f * d_keys_late[h], axis=-1, keepdims=True)
        at_end = dgamma_end[h] + jnp.sum(late_along, axis=0, keepdims=True)
        scal_cols.append(q_along + row_along - col_along + jnp.where(last_row, at_end, 0.0))
        dbs.append(jnp.sum(dr[h] * delta[h].astype(f32), axis=-1, keepdims=True))
        du = qinv[h] * (dq * dk ** (-0.5) - qunit[h] * q_along)
        dpre = du * (qsig[h] * (1.0 + qpre[h] * (1.0 - qsig[h])))
        conv_back(dpre, pq, pq16, cq, kslice[h], nq, dcq, dpqk)
        du = kinv[h] * (d_row + d_col[h] - kunit[h] * (row_along + col_along))
        dpre = du * (ksig[h] * (1.0 + kpre[h] * (1.0 - ksig[h])))
        conv_back(dpre, pk, pk16, ck, kslice[h], nk, dck, dpqk, heads * dk)
        pre, sig = preact(pv, pv16, cv, vslice[h])
        dpre = dr[h] * bc[h] * (sig * (1.0 + pre * (1.0 - sig)))
        conv_back(dpre, pv, pv16, cv, vslice[h], nv, dcv, dpv)
    da = exact(jnp.where(ufull, 1.0, 0.0), jnp.concatenate(scal_cols, axis=1))
    log_scale, shifted = dlog_in[...], small[:, :heads] + dbias_in[...]
    scale = -jnp.exp(log_scale) * valid
    dpa = da * scale * sigmoid(shifted)
    dpb = jnp.concatenate(dbs, axis=1) * sigmoid(-small[:, heads:])
    dsmall[...] = jnp.concatenate([dpa, dpb], axis=1).astype(bf16)
    along = jnp.concatenate([da * scale * softplus(shifted), dpa], axis=1)
    ddecay[...] += jnp.sum(along, axis=0, keepdims=True)


def mixer_backward(scal, pq, pk, pv, small, do, delta, s, tt, cq, ck, cv, dlog, dbias, one, two, three):
    rows = pq.shape[0]
    chunks, heads, dk, dv = s.shape
    kw, vw = heads * dk, heads * dv
    per = chunks // 4
    fine = CHUNK // 16
    (left_one, right_one), (left_two, right_two), (left_three, right_three) = one, two, three
    units, piece = left_three.shape[1], 512
    pieces = pl.cdiv(units, piece)
    width = left_one.shape[1]
    each_one, each_two = width // chunks, width // 2 // chunks

    def by_rows(width):
        return pl.BlockSpec((CHUNK, width), lambda c, s: (block_place(chunks - 1 - c, s[1], per), 0))

    def before(width):
        def place(c, s):
            earlier = jnp.maximum(chunks - 2 - c, 0)
            return (block_place(earlier, s[1], per) * fine + fine - 1, 0)

        return pl.BlockSpec((16, width), place)

    def whole(*shape):
        return pl.BlockSpec(shape, lambda c, s: (0,) * len(shape))

    def by_chunk(*shape):
        return pl.BlockSpec((1,) + shape, lambda c, s: (chunks - 1 - c,) + (0,) * len(shape))

    def at_piece(c):
        return jnp.minimum(c, pieces - 1)

    return pl.pallas_call(
        lambda *refs: mixer_backward_kernel(pieces, *refs),
        grid_spec=pltpu.PrefetchScalarGridSpec(
            num_scalar_prefetch=1,
            grid=(chunks,),
            in_specs=[
                by_rows(kw), by_rows(kw), by_rows(vw),
                before(kw), before(kw), before(vw),
                by_rows(2 * heads), by_rows(vw), by_rows(vw),
                by_chunk(heads, dk, dv), by_chunk(heads, CHUNK, CHUNK),
                whole(4, kw), whole(4, kw), whole(4, vw), whole(1, heads), whole(1, heads),
                pl.BlockSpec((rows, each_one), lambda c, s: (0, c)), whole(*right_one.shape),
                pl.BlockSpec((rows, each_two), lambda c, s: (0, chunks + c)), whole(*right_two.shape),
                pl.BlockSpec((rows, piece), lambda c, s: (0, at_piece(c))), whole(rows, width // 2),
            ],
            out_specs=[
                by_rows(2 * kw), by_rows(vw), by_rows(2 * heads),
                whole(4, kw), whole(4, kw), whole(4, vw), whole(1, 2 * heads),
                pl.BlockSpec((each_one, right_one.shape[1]), lambda c, s: (c, 0)),
                pl.BlockSpec((each_two, right_two.shape[1]), lambda c, s: (c, 0)),
                pl.BlockSpec((piece, width // 2), lambda c, s: (at_piece(c), 0)),
            ],
            scratch_shapes=[
                pltpu.VMEM((heads, dk, dv), f32),
                pltpu.VMEM((8, kw), f32), pltpu.VMEM((8, kw), f32), pltpu.VMEM((8, vw), f32),
            ],
        ),
        out_shape=[
            jax.ShapeDtypeStruct((rows, 2 * kw), bf16),
            jax.ShapeDtypeStruct((rows, vw), bf16),
            jax.ShapeDtypeStruct((rows, 2 * heads), bf16),
            jax.ShapeDtypeStruct((4, kw), f32),
            jax.ShapeDtypeStruct((4, kw), f32),
            jax.ShapeDtypeStruct((4, vw), f32),
            jax.ShapeDtypeStruct((1, 2 * heads), f32),
            jax.ShapeDtypeStruct((width, right_one.shape[1]), bf16),
            jax.ShapeDtypeStruct((width // 2, right_two.shape[1]), bf16),
            jax.ShapeDtypeStruct((units, width // 2), bf16),
        ],
        compiler_params=pltpu.CompilerParams(vmem_limit_bytes=56 * 1024 * 1024),
        cost_estimate=LITTLE,
        name="mixer_backward",
    )(
        scal, pq, pk, pv, pq, pk, pv, small, do, delta, s, tt, cq, ck, cv, dlog, dbias,
        left_one, right_one, left_two, right_two, left_three, right_three,
    )


def product_tn(left, right):
    return lax.dot_general(
        left, right, (((0,), (0,)), ((), ())), preferred_element_type=jnp.float32
    )


def product_nt(left, right):
    return lax.dot_general(
        left, right, (((1,), (1,)), ((), ())), preferred_element_type=jnp.float32
    )


def row_stats(rows):
    inverse = lax.rsqrt(jnp.mean(rows * rows, axis=-1, keepdims=True) + 1e-05)
    return (rows * inverse, inverse)


def norm_back(scaled, inverse, gain, upstream):
    along = upstream * gain
    inner = jnp.mean(along * scaled, axis=-1, keepdims=True)
    return (inverse * (along - scaled * inner), jnp.sum(upstream * scaled, axis=0))


VMEM_MOST = 56 * 1024 * 1024
COLUMNS = 512
MESH = pl.DeviceIdType.MESH


def flipped(place, mask, count):
    out, bit = 0, 1
    while bit < count:
        here = (place // bit) % 2
        out = out + bit * ((1 - here) if mask & bit else here)
        bit *= 2
    return out


def group_order(groups):
    order, bit = [0], groups // 2
    while bit >= 1:
        order = order + [place | bit for place in order]
        bit //= 2
    return order


def split_order(groups, place):
    half = groups // 2
    bit = place % 2
    return [2 * at + bit for at in range(half)] + [2 * at + 1 - bit for at in range(half)]


def column_order(kind, groups, place):
    if kind == "split":
        return split_order(groups, place)
    return [flipped(place, mask, groups) for mask in group_order(groups)]


def take_columns(array, kind):
    groups = lax.axis_size("dp")
    order = jnp.stack([jnp.asarray(at, jnp.int32) for at in column_order(kind, groups, lax.axis_index("dp"))])
    parts = array.reshape(array.shape[0], groups, array.shape[1] // groups)
    return jnp.take(parts, order, axis=1).reshape(array.shape)


def column_copies(kind, groups, source, target, sems):
    each = source.shape[1] // groups
    found = []
    for at, chunk in enumerate(column_order(kind, groups, lax.axis_index("dp"))):
        start = pl.multiple_of(chunk * each, each)
        found.append(
            pltpu.make_async_copy(
                source.at[:, pl.ds(start, each)], target.at[:, pl.ds(at * each, each)], sems.at[at]
            )
        )
    return found


class Gather:
    def __init__(self, own, held, whole, send_sem, recv_sem, out_sem, groups, kind):
        self.kind = kind
        self.own, self.held, self.whole, self.groups = own, held, whole, groups
        self.send_sem, self.recv_sem, self.out_sem = send_sem, recv_sem, out_sem
        place = lax.axis_index("tensor")
        self.beside = flipped(place, 1, 4)
        self.across = flipped(place, 2, 4)

    def copy(self, source, slot, to):
        rows = self.own.shape[0]
        return pltpu.make_async_remote_copy(
            src_ref=self.held.at[pl.ds(source * rows, rows)],
            dst_ref=self.held.at[pl.ds(slot * rows, rows)],
            send_sem=self.send_sem.at[slot - 1],
            recv_sem=self.recv_sem.at[slot - 1],
            device_id={"tensor": to},
            device_id_type=MESH,
        )

    def copies(self):
        return self.copy(0, 1, self.beside), self.copy(0, 2, self.across), self.copy(2, 3, self.beside)

    def outward(self):
        if self.groups == 1:
            return [pltpu.make_async_copy(self.held, self.whole, self.out_sem.at[0])]
        return column_copies(self.kind, self.groups, self.held, self.whole, self.out_sem)

    def begin(self):
        self.held[pl.ds(0, self.own.shape[0]), :] = self.own[...]
        barrier = pltpu.get_barrier_semaphore()
        for other in (self.beside, self.across):
            pl.semaphore_signal(barrier, inc=1, device_id={"tensor": other}, device_id_type=MESH)
        pl.semaphore_wait(barrier, 2)
        to_beside, to_across, _ = self.copies()
        to_across.start()
        to_beside.start()

    def near(self):
        self.copies()[0].wait_recv()

    def second(self):
        _, to_across, forward = self.copies()
        to_across.wait_recv()
        forward.start()
        forward.wait_recv()
        for copy in self.outward():
            copy.start()

    def end(self):
        for copy in self.copies():
            copy.wait_send()
        for copy in self.outward():
            copy.wait()

    def at(self, step, steps):
        @pl.when(step == 0)
        def _():
            self.begin()
            self.near()

        pl.when(step == steps // 2)(self.second)

    def rows(self, half):
        count = 2 * self.own.shape[0]
        return self.held[pl.ds(pl.multiple_of(half * count, count), count), :]


def column_groups(width):
    groups = lax.axis_size("dp")
    return 1 if (width // groups) % 128 else groups


def gather_call(kernel, name, collective, own, operands, in_specs, out_specs, out_shape, cost, kind, more=(), grid=None):
    rows, width = own.shape
    groups = column_groups(width)
    count, made = len(operands), len(out_shape)

    def body(own_ref, *refs):
        outs = refs[count : count + made]
        whole, held, send_sem, recv_sem, out_sem = refs[count + made : count + made + 5]
        gather = Gather(own_ref, held, whole, send_sem, recv_sem, out_sem, groups, kind)
        rest = refs[count + made + 5 :]
        if grid is None:
            kernel(gather, *refs[:count], *outs, *rest)
            return
        step = pl.program_id(0)
        gather.at(step, grid)
        kernel(step, gather, *refs[:count], *outs, *rest)
        pl.when(step == grid - 1)(gather.end)

    own_spec = pl.BlockSpec(memory_space=pltpu.VMEM)
    if grid is not None:
        own_spec = pl.BlockSpec((rows, width), lambda j: (0, 0))
    outs = pl.pallas_call(
        body,
        name=name,
        grid=() if grid is None else (grid,),
        in_specs=[own_spec] + in_specs,
        out_specs=out_specs + [pl.BlockSpec(memory_space=pl.ANY)],
        out_shape=out_shape + [jax.ShapeDtypeStruct((4 * rows, width), own.dtype)],
        scratch_shapes=[
            pltpu.VMEM((4 * rows, width), own.dtype),
            pltpu.SemaphoreType.DMA((3,)),
            pltpu.SemaphoreType.DMA((3,)),
            pltpu.SemaphoreType.DMA((groups,)),
        ]
        + list(more),
        compiler_params=pltpu.CompilerParams(
            vmem_limit_bytes=VMEM_MOST, collective_id=collective, has_side_effects=True
        ),
        cost_estimate=LITTLE,
    )(own, *operands)
    if kind is not None and groups == 1:
        outs = list(outs[:-1]) + [take_columns(outs[-1], kind)]
    return outs


def project_kernel(gather, wq, wk, wv, wg, ws, pq, pk, pv, pg, small, held_w, stage, w_sem, o_sem):
    pair = 2 * gather.own.shape[0]
    pieces = []
    for weight, out in ((wq, pq), (wk, pk), (wv, pv), (wg, pg)):
        for start in range(0, weight.shape[1], COLUMNS):
            pieces.append((weight, out, start))

    def block(at):
        return pl.ds(at * COLUMNS, COLUMNS)

    def load(at):
        weight, _, start = pieces[at]
        return pltpu.make_async_copy(
            weight.at[:, pl.ds(start, COLUMNS)], held_w.at[:, block(at)], w_sem.at[at]
        )

    def store(half, at):
        _, out, start = pieces[at]
        rows = pl.ds(half * pair, pair)
        return pltpu.make_async_copy(
            stage.at[rows, block(at)], out.at[rows, pl.ds(start, COLUMNS)], o_sem.at[half * len(pieces) + at]
        )

    load(0).start()
    gather.begin()
    for at in range(1, len(pieces)):
        load(at).start()
    gather.near()
    for half in range(2):
        if half:
            gather.second()
        rows = pl.ds(half * pair, pair)
        for at in range(len(pieces)):
            if half == 0:
                load(at).wait()
            stage[rows, block(at)] = mm(gather.held[rows, :], held_w[:, block(at)]).astype(bf16)
            store(half, at).start()
        small[rows, :] = mm_nt(gather.held[rows, :], ws[...])
    for half in range(2):
        for at in range(len(pieces)):
            store(half, at).wait()
    gather.end()


def project(own, weights):
    rows, width = own.shape
    total = sum(weight.shape[1] for weight in weights[:4])
    blocks = total // COLUMNS
    hbm, vmem = pl.BlockSpec(memory_space=pl.ANY), pl.BlockSpec(memory_space=pltpu.VMEM)
    out_shape = [jax.ShapeDtypeStruct((4 * rows, weight.shape[1]), bf16) for weight in weights[:4]]
    out_shape.append(jax.ShapeDtypeStruct((4 * rows, weights[4].shape[0]), f32))
    return gather_call(
        project_kernel, "project", 0, own, weights, [hbm] * 4 + [vmem], [hbm] * 4 + [vmem], out_shape,
        (40_000_000_000, 40_000_000), "flip",
        [
            pltpu.VMEM((width, total), bf16),
            pltpu.VMEM((4 * rows, total), bf16),
            pltpu.SemaphoreType.DMA((blocks,)),
            pltpu.SemaphoreType.DMA((2 * blocks,)),
        ],
    )


def feed_kernel(
    gather, e0, e1, e2, e3, wg, wu, wd, hidden, d_gate, d_up, e_out,
    e, held_g, held_u, held_d, stage, e_sem, w_sem, o_sem,
):
    count = gather.own.shape[0]
    pair = 2 * count
    units = wg.shape[0]
    blocks = [(start, min(COLUMNS, units - start)) for start in range(0, units, COLUMNS)]
    outs = (hidden, d_gate, d_up)

    def load_rows(at):
        return pltpu.make_async_copy((e0, e1, e2, e3)[at], e.at[pl.ds(at * count, count)], e_sem.at[at])

    def save_rows():
        return pltpu.make_async_copy(e, e_out, e_sem.at[4])

    def load(at, which):
        where = pl.ds(*blocks[at])
        return pltpu.make_async_copy(
            (wg, wu, wd)[which].at[where], (held_g, held_u, held_d)[which].at[where], w_sem.at[3 * at + which]
        )

    def store(half, which):
        rows = pl.ds(half * pair, pair)
        return pltpu.make_async_copy(stage.at[which, rows], outs[which].at[rows], o_sem.at[3 * half + which])

    load(0, 0).start()
    gather.begin()
    for at in range(len(blocks)):
        for which in range(3):
            if at or which:
                load(at, which).start()
        if at == 0:
            for part in range(4):
                load_rows(part).start()
    gather.near()
    for part in range(4):
        load_rows(part).wait()
    save_rows().start()
    for half in range(2):
        if half:
            gather.second()
        rows = pl.ds(half * pair, pair)
        for at, (start, size) in enumerate(blocks):
            where = pl.ds(start, size)
            if half == 0:
                for which in range(3):
                    load(at, which).wait()
            gate = mm_nt(gather.held[rows, :], held_g[where, :])
            up = mm_nt(gather.held[rows, :], held_u[where, :])
            back = mm_nt(e[rows, :], held_d[where, :])
            sig = sigmoid(gate)
            act = gate * sig
            stage[0, rows, where] = (act * up).astype(bf16)
            stage[1, rows, where] = (back * up * (sig + act * (1.0 - sig))).astype(bf16)
            stage[2, rows, where] = (back * act).astype(bf16)
        for which in range(3):
            store(half, which).start()
    for half in range(2):
        for which in range(3):
            store(half, which).wait()
    save_rows().wait()
    gather.end()


def feed(own, e_blocks, wg, wu, wd):
    rows, width = own.shape
    units = wd.shape[0]
    blocks = pl.cdiv(units, COLUMNS)
    hbm = pl.BlockSpec(memory_space=pl.ANY)
    return gather_call(
        feed_kernel, "feed", 1, own, list(e_blocks) + [wg, wu, wd], [hbm] * 7, [hbm] * 4,
        [jax.ShapeDtypeStruct((4 * rows, units), bf16)] * 3
        + [jax.ShapeDtypeStruct((4 * rows, width), bf16)],
        (40_000_000_000, 40_000_000), "split",
        [pltpu.VMEM((4 * rows, width), bf16)]
        + [pltpu.VMEM((units, width), bf16)] * 3
        + [
            pltpu.VMEM((3, 4 * rows, units), bf16),
            pltpu.SemaphoreType.DMA((5,)),
            pltpu.SemaphoreType.DMA((3 * blocks,)),
            pltpu.SemaphoreType.DMA((6,)),
        ],
    )


def gate_back_kernel(heads, step, gather, length, w, pg, o_in, gain, left, right, dpg, do, dgain, leave):
    pair = 2 * gather.own.shape[0]
    each = pair // 2
    dv = gain.shape[1]
    half = step // 2

    @pl.when(step == 0)
    def _():
        dgain[...] = jnp.zeros_like(dgain)

    at = half * pair + lax.broadcasted_iota(jnp.int32, (pair, 1), 0)
    at = (at // each ^ lax.axis_index("tensor").astype(jnp.int32)) * each + at % each
    valid = jnp.where(at < length[0], 1.0, 0.0)
    upstream = mm_nt(gather.rows(half), w[...]) * valid
    for head in range(heads):
        where = slice(head * dv, (head + 1) * dv)
        dg = upstream[:, where]
        gate = pg[:, where].astype(f32)
        sig = sigmoid(gate)
        act = gate * sig
        o = o_in[:, where].astype(f32)
        inv = lax.rsqrt(jnp.mean(o * o, axis=-1, keepdims=True) + 1e-05)
        norm = o * inv
        through = dg * norm
        dgain[...] += jnp.sum(through * act, axis=0, keepdims=True)
        dpg[:, where] = (through * gain[...] * (sig + act * (1.0 - sig))).astype(bf16)
        dn = dg * gain[...] * act
        do[:, where] = (inv * (dn - norm * jnp.mean(dn * norm, axis=-1, keepdims=True))).astype(bf16)

    @pl.when(step == 1)
    def _():
        units = leave.shape[0]
        for start in range(0, units, COLUMNS):
            where = slice(start, min(start + COLUMNS, units))
            leave[where, :] = mm_tn(left[:, where], right[...]).astype(bf16)


def gate_back(own, length, w_out, pg, o, gain, left, right):
    rows, width = own.shape
    pair = 2 * rows
    dv = gain.shape[1]
    heads = w_out.shape[0] // dv // 2
    by_head = pl.BlockSpec((pair, heads * dv), lambda j: (j // 2, j % 2))
    return gather_call(
        lambda *refs: gate_back_kernel(heads, *refs), "gate_back", 2, own, [length, w_out, pg, o, gain, left, right],
        [
            pl.BlockSpec(memory_space=pltpu.SMEM),
            pl.BlockSpec((heads * dv, width), lambda j: (j % 2, 0)),
            by_head, by_head,
            pl.BlockSpec((1, dv), lambda j: (0, 0)),
            pl.BlockSpec(left.shape, lambda j: (0, 0)),
            pl.BlockSpec((right.shape[0], right.shape[1] // 2), lambda j: (0, 1)),
        ],
        [
            by_head, by_head,
            pl.BlockSpec((1, dv), lambda j: (0, 0)),
            pl.BlockSpec((left.shape[1], right.shape[1] // 2), lambda j: (0, 0)),
        ],
        [
            jax.ShapeDtypeStruct(pg.shape, bf16),
            jax.ShapeDtypeStruct(pg.shape, bf16),
            jax.ShapeDtypeStruct((1, dv), f32),
            jax.ShapeDtypeStruct((left.shape[1], right.shape[1] // 2), bf16),
        ],
        (30_000_000_000, 30_000_000), "flip", grid=4,
    )


def scatter_kernel(turned, count, filled, *refs):
    lefts, rights, refs = refs[:count], refs[count : 2 * count], refs[2 * count :]
    sources, refs = refs[: filled + 1 if filled else 0], refs[filled + 1 if filled else 0 :]
    out, fills, refs = refs[0], refs[1 : 1 + filled], refs[1 + filled :]
    far_own, leave, other, send_sem, recv_sem, fill_sem = refs[:6]
    held = refs[6:]
    loads = [pltpu.make_async_copy(source, kept, fill_sem.at[at]) for at, (source, kept) in enumerate(zip(sources, held))]
    step = pl.program_id(0)
    parts = pl.num_programs(0) // 2
    rows = out.shape[0]
    place = lax.axis_index("tensor")
    beside, across = flipped(place, 1, 4), flipped(place, 2, 4)
    multiply = mm_nt if turned else mm
    CORNER, NEAR, ACROSS = 0, 1, 2

    def columns(part):
        return pl.ds(pl.multiple_of(part * COLUMNS, COLUMNS), COLUMNS)

    def copy(kind, part):
        return pltpu.make_async_remote_copy(
            src_ref=leave.at[kind, :, columns(part)],
            dst_ref=other.at[kind, :, columns(part)],
            send_sem=send_sem.at[kind, part],
            recv_sem=recv_sem.at[kind, part],
            device_id={"tensor": across if kind == ACROSS else beside},
            device_id_type=MESH,
        )

    def product():
        total = multiply(lefts[0][...], rights[0][...])
        for at in range(1, count):
            total = total + multiply(lefts[at][...], rights[at][...])
        return total

    def pass_on(part):
        copy(CORNER, part).wait_recv()
        both = far_own[:, columns(part)] + other[CORNER, :, columns(part)].astype(f32)
        leave[ACROSS, :, columns(part)] = both.astype(bf16)
        copy(ACROSS, part).start()

    @pl.when(step == 0)
    def _():
        barrier = pltpu.get_barrier_semaphore()
        for to in (beside, across):
            pl.semaphore_signal(barrier, inc=1, device_id={"tensor": to}, device_id_type=MESH)
        pl.semaphore_wait(barrier, 2)
        for load in loads:
            load.start()

    part = step % parts

    @pl.when(step < parts)
    def _():
        total = product()
        far_own[:, columns(part)] = total[:rows]
        leave[CORNER, :, columns(part)] = total[rows:].astype(bf16)
        copy(CORNER, part).start()

        @pl.when(step > 0)
        def _():
            pass_on(part - 1)

    @pl.when(step >= parts)
    def _():
        @pl.when(step == parts)
        def _():
            pass_on(parts - 1)

        total = product()
        out[:, columns(part)] = total[:rows]
        leave[NEAR, :, columns(part)] = total[rows:].astype(bf16)
        copy(NEAR, part).start()

    @pl.when(step == 2 * parts - 1)
    def _():
        for load in loads:
            load.wait()
        for fill, source in zip(fills, held[1:]):
            for start in range(0, fill.shape[0], COLUMNS):
                where = slice(start, start + COLUMNS)
                fill[where, :] = mm_tn(held[0][:, where], source[...]).astype(bf16)

        def finish(part, carry):
            copy(NEAR, part).wait_recv()
            copy(ACROSS, part).wait_recv()
            where = columns(part)
            out[:, where] = (
                out[:, where] + other[NEAR, :, where].astype(f32) + other[ACROSS, :, where].astype(f32)
            )
            for kind in (CORNER, NEAR, ACROSS):
                copy(kind, part).wait_send()
            return carry

        lax.fori_loop(0, parts, finish, 0)


def scatter_products(lefts, rights, turned, collective, fill=None):
    lefts = [left if isinstance(left, tuple) else (left, 0, left.shape[1]) for left in lefts]
    rows = lefts[0][0].shape[0] // 4
    width = rights[0].shape[0 if turned else 1]
    parts = width // COLUMNS
    total = sum(left[2] for left in lefts)
    flops = 8 * rows * width * total

    def left_spec(block, size):
        return pl.BlockSpec((2 * rows, size), lambda j: (1 - j // parts, block))

    def right_spec(right):
        if turned:
            return pl.BlockSpec((COLUMNS, right.shape[1]), lambda j: (j % parts, 0))
        return pl.BlockSpec((right.shape[0], COLUMNS), lambda j: (0, j % parts))

    in_specs = [left_spec(block, size) for _, block, size in lefts] + [right_spec(right) for right in rights]
    out_specs = [pl.BlockSpec((rows, width), lambda j: (0, 0))]
    out_shape = [jax.ShapeDtypeStruct((rows, width), f32)]
    fill = list(fill or ())
    in_specs += [pl.BlockSpec(memory_space=pl.ANY)] * len(fill)
    for part in fill[1:]:
        made = (fill[0].shape[1], part.shape[1])
        out_specs.append(pl.BlockSpec(made, lambda j: (0, 0)))
        out_shape.append(jax.ShapeDtypeStruct(made, bf16))
    outs = pl.pallas_call(
        lambda *refs: scatter_kernel(turned, len(lefts), max(len(fill) - 1, 0), *refs),
        name="scatter_products",
        grid=(2 * parts,),
        in_specs=in_specs,
        out_specs=out_specs,
        out_shape=out_shape,
        scratch_shapes=[
            pltpu.VMEM((rows, width), f32),
            pltpu.VMEM((3, rows, width), bf16),
            pltpu.VMEM((3, rows, width), bf16),
            pltpu.SemaphoreType.DMA((3, parts)),
            pltpu.SemaphoreType.DMA((3, parts)),
            pltpu.SemaphoreType.DMA((max(len(fill), 1),)),
        ]
        + [pltpu.VMEM(part.shape, bf16) for part in fill],
        compiler_params=pltpu.CompilerParams(
            vmem_limit_bytes=VMEM_MOST, collective_id=collective, has_side_effects=True
        ),
        cost_estimate=LITTLE,
    )(*[left[0] for left in lefts], *rights, *fill)
    return outs if fill else outs[0]


def turned_kernel(added, left, right, *refs):
    total = mm_tn(left[...], right[...])
    if added:
        total = total + refs[0][...].astype(f32)
    refs[-1][...] = total.astype(bf16)


def turned_product(left, right, left_half=None, right_half=None, other=None):
    rows = left.shape[0]
    count = left.shape[1] if left_half is None else left.shape[1] // 2
    width = right.shape[1] if right_half is None else right.shape[1] // 2
    skip = (left_half or 0) * (count // COLUMNS)
    out = pl.BlockSpec((COLUMNS, width), lambda j: (j, 0))
    more = [] if other is None else [other]
    return pl.pallas_call(
        lambda *refs: turned_kernel(len(more), *refs),
        name="turned_product",
        grid=(pl.cdiv(count, COLUMNS),),
        in_specs=[
            pl.BlockSpec((rows, COLUMNS), lambda j: (0, skip + j)),
            pl.BlockSpec((rows, width), lambda j: (0, right_half or 0)),
        ]
        + [out] * len(more),
        out_specs=out,
        out_shape=jax.ShapeDtypeStruct((count, width), bf16),
        compiler_params=pltpu.CompilerParams(vmem_limit_bytes=VMEM_MOST),
        cost_estimate=LITTLE,
    )(left, right, *more)


def low_bit(chunk, groups):
    return groups if chunk == 0 else chunk & -chunk


def reduce_plan(groups, early, late):
    chunks = [chunk for chunk in group_order(groups) if chunk % 2 == 0]
    chunks.sort(key=lambda chunk: low_bit(chunk, groups))
    levels = max(groups.bit_length() - 2, 1)
    plan = []
    for at, tensor in enumerate(late):
        for position, chunk in enumerate(chunks):
            level = low_bit(chunk, groups).bit_length() - 2
            lag = LAST * level / levels if chunk == 0 else NEXT * level
            plan.append((at * len(chunks) + position + lag, tensor, chunk))
    for at, tensor in enumerate(early):
        for position, chunk in enumerate(chunks):
            level = low_bit(chunk, groups).bit_length() - 2
            plan.append((EARLY[0] * at - 1 + EARLY[1] * level + 0.01 * position, tensor, chunk))
    return [step[1:] for step in sorted(plan)], chunks


PARTS = 2
AHEAD = 4
EARLY = (2, 6)
LAST, NEXT = 2.5, 0.5


def reduce_kernel(groups, early, shapes, *refs):
    count = len(shapes)
    late = list(range(len(early), count))
    leaves, refs = refs[:count], refs[count:]
    given, refs = refs[: len(early)], refs[len(early) :]
    (taps_q, taps_k, taps_v, decay, thin, gain_one, gain_two, gain_head, hidden_in, down_in, resid), refs = (
        refs[:11], refs[11:],
    )
    outs = []
    for shape in shapes:
        outs.append(refs[: len(shape)])
        refs = refs[len(shape) :]
    (out_q, out_k, out_v, out_decay, out_thin, out_one, out_two, out_head, mixed), refs = refs[:9], refs[9:]
    lands, refs = refs[:count], refs[count:]
    sends, refs = refs[:count], refs[count:]
    keeps, refs = refs[:count], refs[count:]
    small_land, gains_land, gains_first, rows_leave, rows_land, hidden, down, partial = refs[:8]
    send_sem, recv_sem, sum_send, sum_recv, rows_send, rows_recv, keep_sem, load_sem = refs[8:]
    place = lax.axis_index("dp")
    beside = lax.axis_index("tensor")
    order = group_order(groups)
    position = {chunk: at for at, chunk in enumerate(order)}
    bits = [1 << at for at in range(groups.bit_length() - 1)]
    each = sends[0].shape[0] // (groups // 2 - 1)
    across_core = {"tensor": flipped(beside, 1, 4)}
    across_chip = {"tensor": flipped(beside, 2, 4)}

    size = each // PARTS

    def rows(at, part):
        return pl.ds(at * each + part * size, size)

    def slot(unit, chunk):
        tensor, part = unit
        return rows(chunk // 2 - 1 if tensor in early else chunk - 1, part)

    def copy(unit, chunk):
        tensor, part = unit
        if chunk % 2:
            source = leaves[tensor].at[rows(position[chunk], part)]
        else:
            source = sends[tensor].at[rows(chunk // 2 - 1, part)]
        at = (tensor * PARTS + part) * groups + chunk
        return pltpu.make_async_remote_copy(
            src_ref=source,
            dst_ref=lands[tensor].at[slot(unit, chunk)],
            send_sem=send_sem.at[at],
            recv_sem=recv_sem.at[at],
            device_id={"dp": flipped(place, low_bit(chunk, groups), groups)},
            device_id_type=MESH,
        )

    def keep_copy(tensor):
        return pltpu.make_async_copy(
            leaves[tensor].at[pl.ds(0, keeps[tensor].shape[0])], keeps[tensor], keep_sem.at[tensor]
        )

    for tensor in range(count):
        keep_copy(tensor).start()
    kept = set()
    partners = [{"dp": flipped(place, bit, groups)} for bit in bits] + [across_core, across_chip]
    barrier = pltpu.get_barrier_semaphore()
    for partner in partners:
        pl.semaphore_signal(barrier, inc=1, device_id=partner, device_id_type=MESH)
    pl.semaphore_wait(barrier, len(partners))

    early_units = [(tensor, part) for tensor in early for part in range(PARTS)]
    late_units = [(tensor, part) for tensor in late for part in range(PARTS)]
    plan, chunks = reduce_plan(groups, early_units, late_units)
    pieces = [(unit, chunk + 1) for unit in late_units for chunk in chunks]
    started = []

    def send_piece():
        if len(started) < len(pieces):
            copy(*pieces[len(started)]).start()
            started.append(1)

    for _ in range(AHEAD):
        send_piece()

    def plain_copy(source, land, sems, at, partner):
        return pltpu.make_async_remote_copy(
            src_ref=source, dst_ref=land, send_sem=sems[0].at[at], recv_sem=sems[1].at[at],
            device_id=partner, device_id_type=MESH,
        )

    quarter = mixed.shape[0]
    quarter_width = mixed.shape[1] // 4
    blocks = [pl.ds(at * quarter, quarter) for at in range(4)]
    row_sems = (rows_send, rows_recv)
    corner = plain_copy(partial.at[blocks[3]], rows_land.at[0], row_sems, 0, across_core)
    near = plain_copy(partial.at[blocks[1]], rows_land.at[1], row_sems, 1, across_core)
    far = plain_copy(rows_leave, rows_land.at[2], row_sems, 2, across_chip)
    loads = [
        pltpu.make_async_copy(hidden_in, hidden, load_sem.at[0]),
        pltpu.make_async_copy(down_in, down, load_sem.at[1]),
    ]
    for load in loads:
        load.start()

    kw, line = taps_q.shape[1], taps_v.shape[1]
    lines = gain_one.shape[1] // line
    gains_first[0] = jnp.zeros(gains_first.shape[1:], f32)
    small_land[0] = jnp.zeros(small_land.shape[1:], f32)
    small_land[0, 0:4, :] = taps_v[...]
    small_land[0, 4:8, :kw] = taps_q[...]
    small_land[0, 4:8, kw:] = taps_k[...]
    for at in range(lines):
        where = slice(at * line, (at + 1) * line)
        small_land[0, 8 + 8 * at : 16 + 8 * at, :] = thin[:, where]
        gains_first[0, at : at + 1, :] = gain_one[:, where]
        gains_first[0, lines + at : lines + at + 1, :] = gain_two[:, where]
    small_land[0, 8 + 8 * lines : 9 + 8 * lines, : decay.shape[1]] = decay[...]
    gains_first[0, 2 * lines : 2 * lines + 1, : gain_head.shape[1]] = gain_head[...]
    sum_sems = (sum_send, sum_recv)
    hops = [across_core, across_chip] + [{"dp": flipped(place, bit, groups)} for bit in bits]
    gains_copies = [
        plain_copy(gains_first.at[at], gains_land.at[at], sum_sems, at, partner)
        for at, partner in enumerate(hops)
    ]
    small_copies = [
        plain_copy(small_land.at[2 * at], small_land.at[2 * at + 1], sum_sems, len(hops) + at, partner)
        for at, partner in enumerate(hops[2:])
    ]
    gains_copies[0].start()
    small_copies[0].start()
    done = {"gains": 0, "small": 0}

    def next_sum():
        at = done["gains"]
        if at < len(gains_copies):
            gains_copies[at].wait_recv()
            total = gains_first[at] + gains_land[at]
            if at + 1 < len(gains_copies):
                gains_first[at + 1] = total
                gains_copies[at + 1].start()
            else:
                for row in range(lines):
                    where = slice(row * line, (row + 1) * line)
                    out_one[:, where] = total[row : row + 1, :]
                    out_two[:, where] = total[lines + row : lines + row + 1, :]
                out_head[...] = total[2 * lines : 2 * lines + 1, : gain_head.shape[1]]
            done["gains"] += 1
        at = done["small"]
        if at < len(small_copies):
            small_copies[at].wait_recv()
            total = small_land[2 * at] + small_land[2 * at + 1]
            if at + 1 < len(small_copies):
                small_land[2 * at + 2] = total
                small_copies[at + 1].start()
            else:
                out_v[...] = total[0:4]
                out_q[...] = total[4:8, :kw]
                out_k[...] = total[4:8, kw:]
                for row in range(lines):
                    out_thin[:, row * line : (row + 1) * line] = total[8 + 8 * row : 16 + 8 * row]
                out_decay[...] = total[8 + 8 * lines : 9 + 8 * lines, : decay.shape[1]]
            done["small"] += 1

    def finish(tensor, part, total):
        where = slice(part * size, (part + 1) * size)
        for out, (start, count, turned) in zip(outs[tensor], shapes[tensor]):
            piece = total[:, start : start + count]
            if turned:
                out[:, where] = jnp.transpose(piece)
            else:
                out[where, :] = piece

    for index, (unit, chunk) in enumerate(plan):
        tensor, part = unit
        if index == 3:
            for load in loads:
                load.wait()
        if 4 <= index < 8:
            where = pl.ds((index - 4) * quarter_width, quarter_width)
            partial[:, where] = mm(hidden[...], down[:, where]).astype(bf16)
        if index == 8:
            corner.start()
            near.start()
        if index == 12:
            corner.wait_recv()
            rows_leave[...] = (
                partial[blocks[2], :].astype(f32) + rows_land[0].astype(f32)
            ).astype(bf16)
            far.start()
        if tensor not in kept:
            keep_copy(tensor).wait()
            kept.add(tensor)
        total = keeps[tensor][rows(position[chunk], part), :].astype(f32)
        for bit in bits:
            if bit >= low_bit(chunk, groups):
                break
            if bit == 1 and tensor in early:
                total = total + given[tensor][rows(position[chunk], part), :].astype(f32)
                continue
            copy(unit, chunk + bit).wait_recv()
            if bit == 1:
                send_piece()
            total = total + lands[tensor][slot(unit, chunk + bit), :].astype(f32)
        if chunk:
            sends[tensor][rows(chunk // 2 - 1, part), :] = total.astype(bf16)
            copy(unit, chunk).start()
        else:
            finish(tensor, part, total)
        if index >= 4 and index % 4 == 0:
            next_sum()
        if index == 20:
            near.wait_recv()
            far.wait_recv()
            mixed[...] = (
                resid[...]
                + partial[blocks[0], :].astype(f32)
                + rows_land[1].astype(f32)
                + rows_land[2].astype(f32)
            ).astype(bf16)
    while done["gains"] < len(gains_copies):
        next_sum()
    for unit in early_units + late_units:
        for chunk in range(1, groups):
            if chunk % 2 == 0 or unit[0] in late:
                copy(unit, chunk).wait_send()
    for sent in gains_copies + small_copies + [corner, near, far]:
        sent.wait_send()


def reduce_groups(early_grads, given, late_grads, shapes, small, hidden, down, resid, collective):
    grads = list(early_grads) + list(late_grads)
    early = list(range(len(early_grads)))
    groups = lax.axis_size("dp")
    bits = groups.bit_length() - 1
    each = late_grads[0].shape[0] // groups
    rows, width = resid.shape
    widths = [grad.shape[1] for grad in grads]
    vmem = pl.BlockSpec(memory_space=pltpu.VMEM)
    out_shape = []
    for shape in shapes:
        for _, size, turned in shape:
            out_shape.append(jax.ShapeDtypeStruct((size, each) if turned else (each, size), f32))
    out_shape += [jax.ShapeDtypeStruct(part.shape, f32) for part in small]
    out_shape += [jax.ShapeDtypeStruct((rows, width), bf16)]
    line = small[2].shape[1]
    lines = width // line
    small_shape, gains_shape = (16 + 8 * lines, line), (8 * pl.cdiv(2 * lines + 1, 8), line)
    landed = [(groups // 2 if at in early else groups) - 1 for at in range(len(grads))]
    return pl.pallas_call(
        lambda *refs: reduce_kernel(groups, early, shapes, *refs),
        name="reduce_groups",
        in_specs=[pl.BlockSpec(memory_space=pl.ANY)] * len(grads)
        + [vmem] * (len(given) + len(small))
        + [pl.BlockSpec(memory_space=pl.ANY)] * 2 + [vmem],
        out_specs=[vmem] * len(out_shape),
        out_shape=out_shape,
        scratch_shapes=[pltpu.VMEM((chunks * each, size), bf16) for chunks, size in zip(landed, widths)]
        + [pltpu.VMEM(((groups // 2 - 1) * each, size), bf16) for size in widths]
        + [pltpu.VMEM((groups // 2 * each, size), bf16) for size in widths]
        + [
            pltpu.VMEM((2 * bits,) + small_shape, f32),
            pltpu.VMEM((bits + 2,) + gains_shape, f32),
            pltpu.VMEM((bits + 2,) + gains_shape, f32),
            pltpu.VMEM((rows, width), bf16),
            pltpu.VMEM((3, rows, width), bf16),
            pltpu.VMEM(hidden.shape, bf16),
            pltpu.VMEM(down.shape, bf16),
            pltpu.VMEM((4 * rows, width), bf16),
            pltpu.SemaphoreType.DMA((len(grads) * PARTS * groups,)),
            pltpu.SemaphoreType.DMA((len(grads) * PARTS * groups,)),
            pltpu.SemaphoreType.DMA((2 * bits + 2,)),
            pltpu.SemaphoreType.DMA((2 * bits + 2,)),
            pltpu.SemaphoreType.DMA((3,)),
            pltpu.SemaphoreType.DMA((3,)),
            pltpu.SemaphoreType.DMA((len(grads),)),
            pltpu.SemaphoreType.DMA((2,)),
        ],
        compiler_params=pltpu.CompilerParams(
            vmem_limit_bytes=VMEM_MOST, collective_id=collective, has_side_effects=True
        ),
        cost_estimate=LITTLE,
    )(*grads, *given, *small, hidden, down, resid)


def product_nn(left, right):
    return jnp.dot(left, right, preferred_element_type=jnp.float32)


def tie(value, after):
    return lax.optimization_barrier((value, after))[0]


def together(*values):
    return lax.optimization_barrier(values)


def flip(array, axis, bit):
    size = lax.axis_size(axis)
    return lax.ppermute(array, axis, [(place, place ^ bit) for place in range(size)])


def in_order(array):
    groups = lax.axis_size("dp")
    place = lax.axis_index("dp").astype(jnp.int32)
    found = jnp.array(group_order(groups), jnp.int32)[jnp.arange(groups, dtype=jnp.int32) ^ place]
    return jnp.take(array.reshape(array.shape[0], groups, -1), found, axis=1)


def scatter_far(total):
    groups = lax.axis_size("dp")
    alike = [[place for place in range(groups) if place % 2 == bit] for bit in (0, 1)]
    return lax.psum_scatter(total, "dp", scatter_dimension=1, axis_index_groups=alike, tiled=True)


def per_device(
    tokens,
    norm1_gain,
    w_query,
    w_key,
    w_value,
    w_gate_out,
    w_decay,
    w_beta,
    conv_query,
    conv_key,
    conv_value,
    decay_log,
    decay_bias,
    head_gain,
    w_out,
    norm2_gain,
    w_gate,
    w_up,
    w_down,
    state_in,
    seq_blocks,
    seq_tail,
    cotangent,
):
    width = tokens.shape[1]
    heads = decay_log.shape[0]
    rows_in = tokens.astype(jnp.float32)
    scaled1, inverse1 = row_stats(rows_in)
    normed1 = (scaled1 * norm1_gain).astype(jnp.bfloat16)
    seq_length = (BLOCK * (seq_blocks - 1) + seq_tail).astype(jnp.int32)
    place = lax.axis_index("tensor").astype(jnp.int32)
    scal = jnp.stack([seq_length[0], place])
    gain_row, log_row, bias_row = head_gain[None], decay_log[None], decay_bias[None]
    w_small = jnp.concatenate([w_decay.T, w_beta.T], axis=0)
    weights1 = (w_query, w_key, w_value, w_gate_out, w_small)
    p_query, p_key, p_value, p_gate, p_small, gathered1 = project(normed1, weights1)
    cotangent = tie(cotangent, p_small)
    e_beside, e_across = flip(cotangent, "tensor", 1), flip(cotangent, "tensor", 2)
    gated, final, mixer_out, delta, states, inverse_t = mixer_forward(
        scal, p_query, p_key, p_value, p_gate, p_small,
        conv_query, conv_key, conv_value, log_row, bias_row, gain_row, state_in[0],
    )
    gated, e_across = together(gated, e_across)
    e_corner = flip(e_across, "tensor", 1)
    resid = rows_in + scatter_products([gated], [w_out], False, 3)
    scaled2, inverse2 = row_stats(resid)
    normed2 = (scaled2 * norm2_gain).astype(jnp.bfloat16)
    hidden, d_gate, d_up, cot_full, split2 = feed(
        normed2, (cotangent, e_beside, e_across, e_corner), w_gate.T, w_up.T, w_down
    )
    grad_down = product_tn(hidden, cot_full).astype(jnp.bfloat16)
    half = width // 2
    up_other = product_tn(d_up, split2[:, half:]).astype(jnp.bfloat16)
    d_gate, d_up, grad_down, up_other = together(d_gate, d_up, grad_down, up_other)
    grad_down = scatter_far(grad_down)
    up_other = flip(up_other, "dp", 1)
    d_normed2 = scatter_products([d_gate, d_up], [w_gate.T, w_up.T], False, 4)
    d_resid_part, grad_norm2 = norm_back(scaled2, inverse2, norm2_gain, d_normed2)
    d_resid = (cotangent.astype(jnp.float32) + d_resid_part).astype(jnp.bfloat16)
    dp_gate, do, dgain, gate_other, resid_full = gate_back(
        d_resid, seq_length, w_out, p_gate, mixer_out, gain_row, d_gate, split2
    )
    do, dp_gate, dgain, resid_full, gate_other, up_other = together(
        do, dp_gate, dgain, resid_full, gate_other, up_other
    )
    gate_other = flip(gate_other, "dp", 1)
    up_kept = turned_product(d_up, split2, right_half=0, other=up_other)
    do, up_kept = together(do, up_kept)
    grad_up = scatter_far(up_kept)
    mixer_grads = mixer_backward(
        scal, p_query, p_key, p_value, p_small, do, delta, states, inverse_t,
        conv_query, conv_key, conv_value, log_row, bias_row, (gathered1, dp_gate), (resid_full, gated),
        (d_gate, split2),
    )
    (
        dp_pair, dp_value, dp_small, dc_query, dc_key, dc_value, ddecay, grad_gate_out, out_other, gate_kept,
        grad_down, gate_other,
    ) = together(*mixer_grads, grad_down, gate_other)
    each = width // lax.axis_size("dp")
    bit = lax.axis_index("dp") % 2
    down_keep = lax.dynamic_slice_in_dim(grad_down, bit * each, each, 1)
    down_other = lax.dynamic_slice_in_dim(grad_down, (1 - bit) * each, each, 1)
    out_other, down_other = together(out_other, down_other)
    out_other, down_other = flip(out_other, "dp", 1), flip(down_other, "dp", 1)
    gate_kept = gate_kept.astype(jnp.float32) + gate_other.astype(jnp.float32)
    grad_gate = scatter_far(gate_kept.astype(jnp.bfloat16))
    key_width = w_query.shape[1]
    d_normed1, grad_value, grad_pair = scatter_products(
        [(dp_pair, 0, key_width), (dp_pair, 1, key_width), dp_value, dp_gate, dp_small],
        weights1[:4] + (w_small.T,), True, 5, (gathered1, dp_value, dp_pair),
    )
    out_keep = turned_product(resid_full, gated, left_half=0)
    d_normed1, out_keep, out_other, down_other = together(d_normed1, out_keep, out_other, down_other)
    grad_down = down_keep.astype(jnp.float32) + down_other.astype(jnp.float32)
    grad_small = in_order(product_tn(dp_small, gathered1))
    d_tokens_part, grad_norm1 = norm_back(scaled1, inverse1, norm1_gain, d_normed1)
    tokens_grad = (d_resid.astype(jnp.float32) + d_tokens_part).astype(jnp.bfloat16)
    value_width = w_value.shape[1]
    turn = (width // lax.axis_size("dp")) % 128 == 0
    thin = grad_small.reshape(grad_small.shape[0], width)
    small = [dc_query, dc_key, dc_value, ddecay, thin, grad_norm1[None], grad_norm2[None], dgain]
    (
        grad_out, grad_gate_out, grad_value, grad_query, grad_key,
        dc_query, dc_key, dc_value, ddecay, thin, grad_norm1, grad_norm2, dgain, mixed,
    ) = reduce_groups(
        [out_keep], [out_other], [grad_gate_out, grad_value, grad_pair],
        [
            [(0, value_width, turn)],
            [(0, value_width, False)],
            [(0, value_width, False)],
            [(0, key_width, False), (key_width, key_width, False)],
        ],
        small, hidden, w_down, resid, 6,
    )
    mixed, grad_up = together(mixed, grad_up)
    grad_up, grad_gate = grad_up.astype(jnp.float32), grad_gate.astype(jnp.float32)
    grad_small = lax.dynamic_slice_in_dim(thin, lax.axis_index("dp") * each, each, 1).T
    return (
        mixed,
        final[None],
        tokens_grad,
        grad_norm1[0],
        grad_query,
        grad_key,
        grad_value,
        grad_gate_out,
        grad_small[:, :heads],
        grad_small[:, heads:],
        dc_query,
        dc_key,
        dc_value,
        ddecay[0, :heads],
        ddecay[0, heads:],
        dgain[0],
        grad_out if turn else grad_out.T,
        grad_norm2[0],
        grad_gate.T,
        grad_up.T,
        grad_down,
    )


def solution(mesh):
    in_specs = (
        P(("dp", "tensor"), None),
        P(),
        P(None, "tensor"),
        P(None, "tensor"),
        P(None, "tensor"),
        P(None, "tensor"),
        P(None, "tensor"),
        P(None, "tensor"),
        P(None, "tensor"),
        P(None, "tensor"),
        P(None, "tensor"),
        P("tensor"),
        P("tensor"),
        P(),
        P("tensor", None),
        P(),
        P(None, "tensor"),
        P(None, "tensor"),
        P("tensor", None),
        P("dp", "tensor", None, None),
        P("dp"),
        P("dp"),
        P(("dp", "tensor"), None),
    )
    out_specs = (
        P(("dp", "tensor"), None),
        P("dp", "tensor", None, None),
        P(("dp", "tensor"), None),
        P(),
        P("dp", "tensor"),
        P("dp", "tensor"),
        P("dp", "tensor"),
        P("dp", "tensor"),
        P("dp", "tensor"),
        P("dp", "tensor"),
        P(None, "tensor"),
        P(None, "tensor"),
        P(None, "tensor"),
        P("tensor"),
        P("tensor"),
        P(),
        P("tensor", "dp"),
        P(),
        P("dp", "tensor"),
        P("dp", "tensor"),
        P("tensor", "dp"),
    )
    return jax.shard_map(
        per_device, mesh=mesh, in_specs=in_specs, out_specs=out_specs, check_vma=False
    )
```

```python
import jax
import jax.numpy as jnp
from jax import lax
from jax.experimental import pallas as pl
from jax.experimental.pallas import tpu as pltpu
from jax.sharding import PartitionSpec as P

BLOCK = 64

CHUNK = 128
LITTLE = pl.CostEstimate(flops=1, bytes_accessed=1, transcendentals=0)
f32 = jnp.float32
bf16 = jnp.bfloat16


def mm(left, right):
    return lax.dot_general(
        left.astype(bf16), right.astype(bf16), (((1,), (0,)), ((), ())), preferred_element_type=f32
    )


def mm_nt(left, right):
    return lax.dot_general(
        left.astype(bf16), right.astype(bf16), (((1,), (1,)), ((), ())), preferred_element_type=f32
    )


def mm_tn(left, right):
    return lax.dot_general(
        left.astype(bf16), right.astype(bf16), (((0,), (0,)), ((), ())), preferred_element_type=f32
    )


def conv_rows(rows, before, taps):
    count = rows.shape[0]
    longer = jnp.concatenate([before, rows], axis=0)
    total = rows * taps[3:4]
    for tap in range(3):
        total = total + longer[5 + tap : 5 + tap + count] * taps[tap : tap + 1]
    return total


def sigmoid(value):
    return 1.0 / (1.0 + jnp.exp(-value))


def unit_factor(rows):
    return lax.rsqrt(jnp.sum(rows * rows, axis=-1, keepdims=True) + 1e-06)


def chunk_masks():
    down = lax.broadcasted_iota(jnp.int32, (CHUNK, CHUNK), 0)
    across = lax.broadcasted_iota(jnp.int32, (CHUNK, CHUNK), 1)
    return down, across


def softplus(value):
    return jnp.maximum(value, 0.0) + jnp.log1p(jnp.exp(-jnp.abs(value)))


def exact(left, right):
    return jnp.dot(left, right, preferred_element_type=f32, precision=lax.Precision.HIGHEST)


def block_place(chunk, place, per):
    return ((chunk // per) ^ place) * per + chunk % per


def decay_terms(small, log_scale, bias, valid, tri):
    heads = log_scale.shape[1]
    decays = -jnp.exp(log_scale) * softplus(small[:, :heads] + bias) * valid
    running = exact(tri, decays)
    strength = sigmoid(small[:, heads:]) * valid
    cols = jnp.concatenate([running, strength], axis=1)
    wide = jnp.concatenate([cols, jnp.zeros((CHUNK, CHUNK - 2 * heads), f32)], axis=1)
    return cols, jnp.transpose(wide)[: 2 * heads]


def mixer_forward_kernel(
    scal, pq, pk, pv, pg, small, cq, ck, cv, dlog, dbias, gain, s0,
    gated_out, final_out, o_out, delta_out, s_out, tt_out,
    state, tq, tk, tv,
):
    chunk = pl.program_id(0)
    heads = s0.shape[0]
    dk, dv = s0.shape[1], s0.shape[2]
    every = range(heads)

    @pl.when(chunk == 0)
    def _():
        state[...] = s0[...]
        tq[...] = jnp.zeros_like(tq)
        tk[...] = jnp.zeros_like(tk)
        tv[...] = jnp.zeros_like(tv)

    down, across = chunk_masks()
    lower = down > across
    full = down >= across
    level = jnp.where(lower, down ^ across, 0)
    eye = jnp.where(down == across, 1.0, 0.0)
    eye_low = eye.astype(bf16)
    kslice = [slice(h * dk, (h + 1) * dk) for h in every]
    vslice = [slice(h * dv, (h + 1) * dv) for h in every]

    subs = range(pq.shape[0] // CHUNK)
    units = [(sub, h) for sub in subs for h in every]
    parts = range(len(units))
    tri = jnp.where(full, 1.0, 0.0)
    valid, gcol, grow = [], [], []
    for sub in subs:
        row_at = (chunk * len(subs) + sub) * CHUNK + lax.broadcasted_iota(jnp.int32, (CHUNK, 1), 0)
        valid.append(jnp.where(row_at < scal[0], 1.0, 0.0))
        cols, rows = decay_terms(
            small[sub * CHUNK : (sub + 1) * CHUNK, :], dlog[...], dbias[...], valid[sub], tri
        )
        gcol.append(cols)
        grow.append(rows)

    def activated(ref, tail, taps, where):
        pre = conv_rows(ref[:, where].astype(f32), tail[:, where], taps[:, where])
        return pre * sigmoid(pre)

    def cut(array, sub):
        return array[sub * CHUNK : (sub + 1) * CHUNK]

    all_keys, all_queries, all_values = [], [], []
    for h in every:
        u = activated(pk, tk, ck, kslice[h])
        all_keys.append((u * unit_factor(u)).astype(bf16))
    for h in every:
        u = activated(pq, tq, cq, kslice[h])
        all_queries.append((u * (unit_factor(u) * dk ** (-0.5))).astype(bf16))
    keys = [cut(all_keys[h], sub) for sub, h in units]
    queries = [cut(all_queries[h], sub) for sub, h in units]
    gc = [gcol[sub][:, h : h + 1] for sub, h in units]
    bc = [gcol[sub][:, heads + h : heads + h + 1] for sub, h in units]
    products = [mm_nt(jnp.concatenate([keys[u], queries[u]], axis=0), keys[u]) for u in parts]
    gam = [
        jnp.exp(jnp.where(full, gc[u] - grow[sub][h : h + 1, :], -1e30))
        for u, (sub, h) in enumerate(units)
    ]
    system = [jnp.where(lower, products[u][:CHUNK] * gam[u] * bc[u], 0.0) for u in parts]
    attend = [(products[u][CHUNK:] * gam[u]).astype(bf16) for u in parts]
    system_low = [system[u].astype(bf16) for u in parts]
    first = jnp.where(level == 1, 1.0, 0.0).astype(bf16)
    inverse = [eye_low - system_low[u] * first for u in parts]
    size = 2
    while size < CHUNK:
        mask = jnp.where((level >= size) & (level < 2 * size), 1.0, 0.0).astype(bf16)
        inner = [mm(system_low[u] * mask, inverse[u]).astype(bf16) for u in parts]
        inverse = [inverse[u] - mm(inverse[u], inner[u]).astype(bf16) for u in parts]
        size *= 2
    left_over = [
        (eye - inverse[u].astype(f32))
        - mm(system_low[u], inverse[u])
        - mm((system[u] - system_low[u].astype(f32)).astype(bf16), inverse[u])
        for u in parts
    ]
    inverse = [(inverse[u].astype(f32) + mm(inverse[u], left_over[u])) for u in parts]
    for u, (sub, h) in enumerate(units):
        tt_out[sub, h] = jnp.transpose(inverse[u]).astype(bf16)
    inverse = [inverse[u].astype(bf16) for u in parts]
    for h in every:
        all_values.append(activated(pv, tv, cv, vslice[h]))
    for ref, tail in ((pq, tq), (pk, tk), (pv, tv)):
        tail[...] = ref[ref.shape[0] - 16 :, :].astype(f32)[8:]
    growth = [jnp.exp(gc[u]) for u in parts]
    keys_f = [keys[u].astype(f32) for u in parts]
    pair = [
        jnp.concatenate(
            [(keys_f[u] * growth[u]).astype(bf16), (queries[u].astype(f32) * growth[u]).astype(bf16)], axis=0
        )
        for u in parts
    ]
    now = [state[h] for h in every]
    for sub in subs:
        mine = [sub * heads + h for h in every]
        for h in every:
            s_out[sub, h] = now[h].astype(bf16)
        carried = [mm(pair[u], now[h]) for h, u in enumerate(mine)]
        delta = [
            mm(inverse[u], bc[u] * (cut(all_values[h], sub) - carried[h][:CHUNK])).astype(bf16)
            for h, u in enumerate(mine)
        ]
        out = [carried[h][CHUNK:] + mm(attend[u], delta[h]) for h, u in enumerate(mine)]
        for h, u in enumerate(mine):
            last = gc[u][CHUNK - 1 : CHUNK]
            late = (keys_f[u] * jnp.exp(last - gc[u])).astype(bf16)
            now[h] = jnp.exp(last) * now[h] + mm_tn(late, delta[h])
        here = slice(sub * CHUNK, (sub + 1) * CHUNK)
        for h in every:
            delta_out[here, vslice[h]] = delta[h]
            o_out[here, vslice[h]] = out[h].astype(bf16)
            inv = lax.rsqrt(jnp.mean(out[h] * out[h], axis=-1, keepdims=True) + 1e-05)
            gate = pg[here, vslice[h]].astype(f32)
            gated_out[here, vslice[h]] = (
                out[h] * (inv * valid[sub]) * gain[...] * (gate * sigmoid(gate))
            ).astype(bf16)
    for h in every:
        state[h] = now[h]

    @pl.when(chunk == pl.num_programs(0) - 1)
    def _():
        final_out[...] = state[...]


def mixer_forward(scal, pq, pk, pv, pg, small, cq, ck, cv, dlog, dbias, gain, s0):
    rows = pq.shape[0]
    heads, dk, dv = s0.shape
    chunks = rows // CHUNK
    per = chunks // 4
    joined = 2 if per % 2 == 0 else 1

    def by_rows(width):
        return pl.BlockSpec(
            (joined * CHUNK, width), lambda c, s: (block_place(c, s[1], per // joined), 0)
        )

    def whole(*shape):
        return pl.BlockSpec(shape, lambda c, s: (0,) * len(shape))

    def by_chunk(*shape):
        return pl.BlockSpec((joined,) + shape, lambda c, s: (c,) + (0,) * len(shape))

    kw, vw = heads * dk, heads * dv
    return pl.pallas_call(
        mixer_forward_kernel,
        grid_spec=pltpu.PrefetchScalarGridSpec(
            num_scalar_prefetch=1,
            grid=(chunks // joined,),
            in_specs=[
                by_rows(kw), by_rows(kw), by_rows(vw), by_rows(vw), by_rows(2 * heads),
                whole(4, kw), whole(4, kw), whole(4, vw), whole(1, heads), whole(1, heads),
                whole(1, dv), whole(heads, dk, dv),
            ],
            out_specs=[
                by_rows(vw), whole(heads, dk, dv), by_rows(vw), by_rows(vw),
                by_chunk(heads, dk, dv), by_chunk(heads, CHUNK, CHUNK),
            ],
            scratch_shapes=[
                pltpu.VMEM((heads, dk, dv), f32),
                pltpu.VMEM((8, kw), f32), pltpu.VMEM((8, kw), f32), pltpu.VMEM((8, vw), f32),
            ],
        ),
        out_shape=[
            jax.ShapeDtypeStruct((rows, vw), bf16),
            jax.ShapeDtypeStruct((heads, dk, dv), f32),
            jax.ShapeDtypeStruct((rows, vw), bf16),
            jax.ShapeDtypeStruct((rows, vw), bf16),
            jax.ShapeDtypeStruct((chunks, heads, dk, dv), bf16),
            jax.ShapeDtypeStruct((chunks, heads, CHUNK, CHUNK), bf16),
        ],
        compiler_params=pltpu.CompilerParams(vmem_limit_bytes=56 * 1024 * 1024),
        cost_estimate=LITTLE,
        name="mixer_forward",
    )(scal, pq, pk, pv, pg, small, cq, ck, cv, dlog, dbias, gain, s0)


def mixer_backward_kernel(
    pieces, scal, pq, pk, pv, pq16, pk16, pv16, small, do_in, delta_in, s_in, tt_in,
    cq, ck, cv, dlog_in, dbias_in, left_one, right_one, left_two, right_two, left_three, right_three, left_four,
    dpqk, dpv, dsmall, dcq, dck, dcv, ddecay, product_one, product_two, product_three, product_four,
    dstate, nq, nk, nv,
):
    step = pl.program_id(0)
    chunk = pl.num_programs(0) - 1 - step
    heads, dk, dv = dstate.shape
    every = range(heads)

    @pl.when(step == 0)
    def _():
        for ref in (dstate, nq, nk, nv, dcq, dck, dcv, ddecay):
            ref[...] = jnp.zeros_like(ref)

    product_one[...] = mm_tn(left_one[...], right_one[...]).astype(bf16)
    product_two[...] = mm_tn(left_two[...], right_two[...]).astype(bf16)
    product_four[...] = mm_tn(left_four[...], right_two[...]).astype(bf16)

    @pl.when(step < pieces)
    def _():
        product_three[...] = mm_tn(left_three[...], right_three[...]).astype(bf16)

    down, across = chunk_masks()
    lower = down > across
    full = down >= across
    upper = down < across
    ufull = down <= across
    kslice = [slice(h * dk, (h + 1) * dk) for h in every]
    vslice = [slice(h * dv, (h + 1) * dv) for h in every]
    has_before = jnp.where(chunk > 0, 1.0, 0.0)

    def preact(ref, ref16, taps, where):
        pre = conv_rows(
            ref[:, where].astype(f32), ref16[:, where].astype(f32)[8:] * has_before, taps[:, where]
        )
        sig = sigmoid(pre)
        return pre, sig

    def conv_back(dpre, ref, ref16, taps, where, later, dtaps, dref, base=0):
        rows = ref[:, where].astype(f32)
        longer = jnp.concatenate([ref16[:, where].astype(f32)[8:] * has_before, rows], axis=0)
        after = jnp.concatenate([dpre, later[:, where]], axis=0)
        total = dpre * taps[3:4, where]
        sums = [jnp.sum(dpre * longer[5 + tap : 5 + tap + CHUNK], axis=0, keepdims=True) for tap in range(3)]
        sums.append(jnp.sum(dpre * rows, axis=0, keepdims=True))
        for tap in range(3):
            total = total + after[3 - tap : 3 - tap + CHUNK] * taps[tap : tap + 1, where]
        dtaps[:, where] += jnp.concatenate(sums, axis=0)
        later[:, where] = dpre[:8]
        dref[:, where.start + base : where.stop + base] = total.astype(bf16)

    row_at = chunk * CHUNK + lax.broadcasted_iota(jnp.int32, (CHUNK, 1), 0)
    valid = jnp.where(row_at < scal[0], 1.0, 0.0)
    tri = jnp.where(full, 1.0, 0.0)
    gcol, grow = decay_terms(small[...], dlog_in[...], dbias_in[...], valid, tri)
    last_row = lax.broadcasted_iota(jnp.int32, (CHUNK, 1), 0) == CHUNK - 1
    kpre, ksig, kinv, kunit, keys = [], [], [], [], []
    qpre, qsig, qinv, qunit, queries = [], [], [], [], []
    for h in every:
        pre, sig = preact(pk, pk16, ck, kslice[h])
        u = pre * sig
        inv = unit_factor(u)
        kpre.append(pre), ksig.append(sig), kinv.append(inv), kunit.append(u * inv)
        keys.append(kunit[h].astype(bf16))
    for h in every:
        pre, sig = preact(pq, pq16, cq, kslice[h])
        u = pre * sig
        inv = unit_factor(u)
        qpre.append(pre), qsig.append(sig), qinv.append(inv), qunit.append(u * inv)
        queries.append((qunit[h] * dk ** (-0.5)).astype(bf16))
    gc = [gcol[:, h : h + 1] for h in every]
    gr = [grow[h : h + 1, :] for h in every]
    bc = [gcol[:, heads + h : heads + h + 1] for h in every]
    br = [grow[heads + h : heads + h + 1, :] for h in every]
    do = [do_in[:, vslice[h]] for h in every]
    delta = [delta_in[:, vslice[h]] for h in every]
    dnext = [dstate[h].astype(bf16) for h in every]
    growth = [jnp.exp(gc[h]) for h in every]
    ending = [jnp.exp(gc[h][CHUNK - 1 : CHUNK] - gc[h]) for h in every]
    final = [jnp.exp(gc[h][CHUNK - 1 : CHUNK]) for h in every]
    gamma = [jnp.exp(jnp.where(full, gc[h] - gr[h], -1e30)) for h in every]
    gamma_t = [jnp.exp(jnp.where(ufull, gr[h] - gc[h], -1e30)) for h in every]
    kq = [mm_nt(keys[h], queries[h]) for h in every]
    keys_late = [(keys[h].astype(f32) * ending[h]).astype(bf16) for h in every]
    d_delta = [
        mm(
            jnp.concatenate([(kq[h] * gamma_t[h]).astype(bf16), keys_late[h]], axis=1),
            jnp.concatenate([do[h], dnext[h]], axis=0),
        ).astype(bf16)
        for h in every
    ]
    dr = [mm(tt_in[0, h], d_delta[h]) for h in every]
    dr_low = [dr[h].astype(bf16) for h in every]
    both = [jnp.concatenate([do[h], dr_low[h]], axis=0) for h in every]
    pair = [
        jnp.concatenate(
            [
                (queries[h].astype(f32) * growth[h]).astype(bf16),
                (keys[h].astype(f32) * (-growth[h] * bc[h])).astype(bf16),
            ],
            axis=0,
        )
        for h in every
    ]
    state = [s_in[0, h] for h in every]
    new_dstate = [final[h] * dstate[h] + mm_tn(pair[h], both[h]) for h in every]
    dgamma_end = [
        jnp.sum(jnp.sum(state[h].astype(f32) * dstate[h], axis=0, keepdims=True), axis=1, keepdims=True)
        * final[h]
        for h in every
    ]
    d_keys_late = [mm_nt(delta[h], dnext[h]) * ending[h] for h in every]
    for h in every:
        dstate[h] = new_dstate[h]
    strict = [jnp.where(lower, gamma[h] * bc[h], 0.0) for h in every]
    strict_t = [jnp.where(upper, gamma_t[h] * br[h], 0.0) for h in every]
    outer = [mm_nt(both[h], delta[h]) for h in every]
    outer_t = [mm_nt(delta[h], both[h]) for h in every]
    inner = [
        jnp.concatenate(
            [(outer[h][:CHUNK] * gamma[h]).astype(bf16), (-outer[h][CHUNK:] * strict[h]).astype(bf16)], axis=0
        )
        for h in every
    ]
    inner_t = [
        jnp.concatenate(
            [
                (outer_t[h][:, :CHUNK] * gamma_t[h]).astype(bf16),
                (-outer_t[h][:, CHUNK:] * strict_t[h]).astype(bf16),
            ],
            axis=1,
        )
        for h in every
    ]
    by_state = [mm_nt(both[h], state[h]) for h in every]
    by_key = [mm(inner[h], keys[h]) for h in every]
    d_col = [
        mm(inner_t[h], jnp.concatenate([queries[h], keys[h]], axis=0)) + d_keys_late[h] for h in every
    ]
    scal_cols = []
    dbs = []
    for h in every:
        dq = by_key[h][:CHUNK] + by_state[h][:CHUNK] * growth[h]
        d_row = by_key[h][CHUNK:] - by_state[h][CHUNK:] * (growth[h] * bc[h])
        key_f = keys[h].astype(f32)
        q_along = jnp.sum(queries[h].astype(f32) * dq, axis=-1, keepdims=True)
        row_along = jnp.sum(key_f * d_row, axis=-1, keepdims=True)
        col_along = jnp.sum(key_f * d_col[h], axis=-1, keepdims=True)
        late_along = jnp.sum(key_f * d_keys_late[h], axis=-1, keepdims=True)
        at_end = dgamma_end[h] + jnp.sum(late_along, axis=0, keepdims=True)
        scal_cols.append(q_along + row_along - col_along + jnp.where(last_row, at_end, 0.0))
        dbs.append(jnp.sum(dr[h] * delta[h].astype(f32), axis=-1, keepdims=True))
        du = qinv[h] * (dq * dk ** (-0.5) - qunit[h] * q_along)
        dpre = du * (qsig[h] * (1.0 + qpre[h] * (1.0 - qsig[h])))
        conv_back(dpre, pq, pq16, cq, kslice[h], nq, dcq, dpqk)
        du = kinv[h] * (d_row + d_col[h] - kunit[h] * (row_along + col_along))
        dpre = du * (ksig[h] * (1.0 + kpre[h] * (1.0 - ksig[h])))
        conv_back(dpre, pk, pk16, ck, kslice[h], nk, dck, dpqk, heads * dk)
        pre, sig = preact(pv, pv16, cv, vslice[h])
        dpre = dr[h] * bc[h] * (sig * (1.0 + pre * (1.0 - sig)))
        conv_back(dpre, pv, pv16, cv, vslice[h], nv, dcv, dpv)
    da = exact(jnp.where(ufull, 1.0, 0.0), jnp.concatenate(scal_cols, axis=1))
    log_scale, shifted = dlog_in[...], small[:, :heads] + dbias_in[...]
    scale = -jnp.exp(log_scale) * valid
    dpa = da * scale * sigmoid(shifted)
    dpb = jnp.concatenate(dbs, axis=1) * sigmoid(-small[:, heads:])
    dsmall[...] = jnp.concatenate([dpa, dpb], axis=1).astype(bf16)
    along = jnp.concatenate([da * scale * softplus(shifted), dpa], axis=1)
    ddecay[...] += jnp.sum(along, axis=0, keepdims=True)


def mixer_backward(scal, pq, pk, pv, small, do, delta, s, tt, cq, ck, cv, dlog, dbias, one, two, three):
    rows = pq.shape[0]
    chunks, heads, dk, dv = s.shape
    kw, vw = heads * dk, heads * dv
    per = chunks // 4
    fine = CHUNK // 16
    (left_one, right_one), (left_two, right_two), (left_three, right_three) = one, two, three
    units, piece = left_three.shape[1], 512
    pieces = pl.cdiv(units, piece)
    width = left_one.shape[1]
    each_one, each_two = width // chunks, width // 2 // chunks

    def by_rows(width):
        return pl.BlockSpec((CHUNK, width), lambda c, s: (block_place(chunks - 1 - c, s[1], per), 0))

    def before(width):
        def place(c, s):
            earlier = jnp.maximum(chunks - 2 - c, 0)
            return (block_place(earlier, s[1], per) * fine + fine - 1, 0)

        return pl.BlockSpec((16, width), place)

    def whole(*shape):
        return pl.BlockSpec(shape, lambda c, s: (0,) * len(shape))

    def by_chunk(*shape):
        return pl.BlockSpec((1,) + shape, lambda c, s: (chunks - 1 - c,) + (0,) * len(shape))

    def at_piece(c):
        return jnp.minimum(c, pieces - 1)

    return pl.pallas_call(
        lambda *refs: mixer_backward_kernel(pieces, *refs),
        grid_spec=pltpu.PrefetchScalarGridSpec(
            num_scalar_prefetch=1,
            grid=(chunks,),
            in_specs=[
                by_rows(kw), by_rows(kw), by_rows(vw),
                before(kw), before(kw), before(vw),
                by_rows(2 * heads), by_rows(vw), by_rows(vw),
                by_chunk(heads, dk, dv), by_chunk(heads, CHUNK, CHUNK),
                whole(4, kw), whole(4, kw), whole(4, vw), whole(1, heads), whole(1, heads),
                pl.BlockSpec((rows, each_one), lambda c, s: (0, c)), whole(*right_one.shape),
                pl.BlockSpec((rows, each_two), lambda c, s: (0, chunks + c)), whole(*right_two.shape),
                pl.BlockSpec((rows, piece), lambda c, s: (0, at_piece(c))), whole(rows, width // 2),
                pl.BlockSpec((rows, each_two), lambda c, s: (0, c)),
            ],
            out_specs=[
                by_rows(2 * kw), by_rows(vw), by_rows(2 * heads),
                whole(4, kw), whole(4, kw), whole(4, vw), whole(1, 2 * heads),
                pl.BlockSpec((each_one, right_one.shape[1]), lambda c, s: (c, 0)),
                pl.BlockSpec((each_two, right_two.shape[1]), lambda c, s: (c, 0)),
                pl.BlockSpec((piece, width // 2), lambda c, s: (at_piece(c), 0)),
                pl.BlockSpec((each_two, right_two.shape[1]), lambda c, s: (c, 0)),
            ],
            scratch_shapes=[
                pltpu.VMEM((heads, dk, dv), f32),
                pltpu.VMEM((8, kw), f32), pltpu.VMEM((8, kw), f32), pltpu.VMEM((8, vw), f32),
            ],
        ),
        out_shape=[
            jax.ShapeDtypeStruct((rows, 2 * kw), bf16),
            jax.ShapeDtypeStruct((rows, vw), bf16),
            jax.ShapeDtypeStruct((rows, 2 * heads), bf16),
            jax.ShapeDtypeStruct((4, kw), f32),
            jax.ShapeDtypeStruct((4, kw), f32),
            jax.ShapeDtypeStruct((4, vw), f32),
            jax.ShapeDtypeStruct((1, 2 * heads), f32),
            jax.ShapeDtypeStruct((width, right_one.shape[1]), bf16),
            jax.ShapeDtypeStruct((width // 2, right_two.shape[1]), bf16),
            jax.ShapeDtypeStruct((units, width // 2), bf16),
            jax.ShapeDtypeStruct((width // 2, right_two.shape[1]), bf16),
        ],
        compiler_params=pltpu.CompilerParams(vmem_limit_bytes=56 * 1024 * 1024),
        cost_estimate=LITTLE,
        name="mixer_backward",
    )(
        scal, pq, pk, pv, pq, pk, pv, small, do, delta, s, tt, cq, ck, cv, dlog, dbias,
        left_one, right_one, left_two, right_two, left_three, right_three, left_two,
    )


def product_tn(left, right):
    return lax.dot_general(
        left, right, (((0,), (0,)), ((), ())), preferred_element_type=jnp.float32
    )


def product_nt(left, right):
    return lax.dot_general(
        left, right, (((1,), (1,)), ((), ())), preferred_element_type=jnp.float32
    )


def row_stats(rows):
    inverse = lax.rsqrt(jnp.mean(rows * rows, axis=-1, keepdims=True) + 1e-05)
    return (rows * inverse, inverse)


def norm_back(scaled, inverse, gain, upstream):
    along = upstream * gain
    inner = jnp.mean(along * scaled, axis=-1, keepdims=True)
    return (inverse * (along - scaled * inner), jnp.sum(upstream * scaled, axis=0))


VMEM_MOST = 56 * 1024 * 1024
COLUMNS = 512
FIRST = 128
MESH = pl.DeviceIdType.MESH


def flipped(place, mask, count):
    out, bit = 0, 1
    while bit < count:
        here = (place // bit) % 2
        out = out + bit * ((1 - here) if mask & bit else here)
        bit *= 2
    return out


def group_order(groups):
    order, bit = [0], groups // 2
    while bit >= 1:
        order = order + [place | bit for place in order]
        bit //= 2
    return order


def split_order(groups, place):
    half = groups // 2
    bit = place % 2
    return [2 * at + bit for at in range(half)] + [2 * at + 1 - bit for at in range(half)]


def column_order(kind, groups, place):
    if kind == "split":
        return split_order(groups, place)
    return [flipped(place, mask, groups) for mask in group_order(groups)]


def take_columns(array, kind):
    groups = lax.axis_size("dp")
    order = jnp.stack([jnp.asarray(at, jnp.int32) for at in column_order(kind, groups, lax.axis_index("dp"))])
    parts = array.reshape(array.shape[0], groups, array.shape[1] // groups)
    return jnp.take(parts, order, axis=1).reshape(array.shape)


def column_copies(kind, groups, source, target, sems):
    each = source.shape[1] // groups
    found = []
    for at, chunk in enumerate(column_order(kind, groups, lax.axis_index("dp"))):
        start = pl.multiple_of(chunk * each, each)
        found.append(
            pltpu.make_async_copy(
                source.at[:, pl.ds(start, each)], target.at[:, pl.ds(at * each, each)], sems.at[at]
            )
        )
    return found


class Gather:
    def __init__(self, own, held, whole, send_sem, recv_sem, out_sem, groups, kind):
        self.kind = kind
        self.own, self.held, self.whole, self.groups = own, held, whole, groups
        self.send_sem, self.recv_sem, self.out_sem = send_sem, recv_sem, out_sem
        place = lax.axis_index("tensor")
        self.beside = flipped(place, 1, 4)
        self.across = flipped(place, 2, 4)

    def copy(self, source, slot, to):
        rows = self.own.shape[0]
        return pltpu.make_async_remote_copy(
            src_ref=self.held.at[pl.ds(source * rows, rows)],
            dst_ref=self.held.at[pl.ds(slot * rows, rows)],
            send_sem=self.send_sem.at[slot - 1],
            recv_sem=self.recv_sem.at[slot - 1],
            device_id={"tensor": to},
            device_id_type=MESH,
        )

    def copies(self):
        return self.copy(0, 1, self.beside), self.copy(0, 2, self.across), self.copy(2, 3, self.beside)

    def outward(self):
        if self.groups == 1:
            return [pltpu.make_async_copy(self.held, self.whole, self.out_sem.at[0])]
        return column_copies(self.kind, self.groups, self.held, self.whole, self.out_sem)

    def begin(self):
        self.held[pl.ds(0, self.own.shape[0]), :] = self.own[...]
        barrier = pltpu.get_barrier_semaphore()
        for other in (self.beside, self.across):
            pl.semaphore_signal(barrier, inc=1, device_id={"tensor": other}, device_id_type=MESH)
        pl.semaphore_wait(barrier, 2)
        to_beside, to_across, _ = self.copies()
        to_across.start()
        to_beside.start()

    def near(self):
        self.copies()[0].wait_recv()

    def second(self):
        _, to_across, forward = self.copies()
        to_across.wait_recv()
        forward.start()
        forward.wait_recv()
        for copy in self.outward():
            copy.start()

    def end(self):
        for copy in self.copies():
            copy.wait_send()
        for copy in self.outward():
            copy.wait()

    def at(self, step, steps):
        @pl.when(step == 0)
        def _():
            self.begin()
            self.near()

        pl.when(step == steps // 2)(self.second)

    def rows(self, half):
        count = 2 * self.own.shape[0]
        return self.held[pl.ds(pl.multiple_of(half * count, count), count), :]


def column_groups(width):
    groups = lax.axis_size("dp")
    return 1 if (width // groups) % 128 else groups


def gather_call(kernel, name, collective, own, operands, in_specs, out_specs, out_shape, cost, kind, more=(), grid=None):
    rows, width = own.shape
    groups = column_groups(width)
    count, made = len(operands), len(out_shape)

    def body(own_ref, *refs):
        outs = refs[count : count + made]
        whole, held, send_sem, recv_sem, out_sem = refs[count + made : count + made + 5]
        gather = Gather(own_ref, held, whole, send_sem, recv_sem, out_sem, groups, kind)
        rest = refs[count + made + 5 :]
        if grid is None:
            kernel(gather, *refs[:count], *outs, *rest)
            return
        step = pl.program_id(0)
        gather.at(step, grid)
        kernel(step, gather, *refs[:count], *outs, *rest)
        pl.when(step == grid - 1)(gather.end)

    own_spec = pl.BlockSpec(memory_space=pltpu.VMEM)
    if grid is not None:
        own_spec = pl.BlockSpec((rows, width), lambda j: (0, 0))
    outs = pl.pallas_call(
        body,
        name=name,
        grid=() if grid is None else (grid,),
        in_specs=[own_spec] + in_specs,
        out_specs=out_specs + [pl.BlockSpec(memory_space=pl.ANY)],
        out_shape=out_shape + [jax.ShapeDtypeStruct((4 * rows, width), own.dtype)],
        scratch_shapes=[
            pltpu.VMEM((4 * rows, width), own.dtype),
            pltpu.SemaphoreType.DMA((3,)),
            pltpu.SemaphoreType.DMA((3,)),
            pltpu.SemaphoreType.DMA((groups,)),
        ]
        + list(more),
        compiler_params=pltpu.CompilerParams(
            vmem_limit_bytes=VMEM_MOST, collective_id=collective, has_side_effects=True
        ),
        cost_estimate=LITTLE,
    )(own, *operands)
    if kind is not None and groups == 1:
        outs = list(outs[:-1]) + [take_columns(outs[-1], kind)]
    return outs


def project_kernel(gather, wq, wk, wv, wg, ws, pq, pk, pv, pg, small, held_w, stage, w_sem, o_sem):
    pair = 2 * gather.own.shape[0]
    pieces = []
    for weight, out in ((wq, pq), (wk, pk), (wv, pv), (wg, pg)):
        for start in range(0, weight.shape[1], COLUMNS):
            pieces.append((weight, out, start))

    def block(at):
        return pl.ds(at * COLUMNS, COLUMNS)

    def load(at):
        weight, _, start = pieces[at]
        return pltpu.make_async_copy(
            weight.at[:, pl.ds(start, COLUMNS)], held_w.at[:, block(at)], w_sem.at[at]
        )

    def store(half, at):
        _, out, start = pieces[at]
        rows = pl.ds(half * pair, pair)
        return pltpu.make_async_copy(
            stage.at[rows, block(at)], out.at[rows, pl.ds(start, COLUMNS)], o_sem.at[half * len(pieces) + at]
        )

    load(0).start()
    gather.begin()
    for at in range(1, len(pieces)):
        load(at).start()
    gather.near()
    for half in range(2):
        if half:
            gather.second()
        rows = pl.ds(half * pair, pair)
        for at in range(len(pieces)):
            if half == 0:
                load(at).wait()
            stage[rows, block(at)] = mm(gather.held[rows, :], held_w[:, block(at)]).astype(bf16)
            store(half, at).start()
        small[rows, :] = mm_nt(gather.held[rows, :], ws[...])
    for half in range(2):
        for at in range(len(pieces)):
            store(half, at).wait()
    gather.end()


def project(own, weights):
    rows, width = own.shape
    total = sum(weight.shape[1] for weight in weights[:4])
    blocks = total // COLUMNS
    hbm, vmem = pl.BlockSpec(memory_space=pl.ANY), pl.BlockSpec(memory_space=pltpu.VMEM)
    out_shape = [jax.ShapeDtypeStruct((4 * rows, weight.shape[1]), bf16) for weight in weights[:4]]
    out_shape.append(jax.ShapeDtypeStruct((4 * rows, weights[4].shape[0]), f32))
    return gather_call(
        project_kernel, "project", 0, own, weights, [hbm] * 4 + [vmem], [hbm] * 4 + [vmem], out_shape,
        (40_000_000_000, 40_000_000), "flip",
        [
            pltpu.VMEM((width, total), bf16),
            pltpu.VMEM((4 * rows, total), bf16),
            pltpu.SemaphoreType.DMA((blocks,)),
            pltpu.SemaphoreType.DMA((2 * blocks,)),
        ],
    )


def feed_kernel(
    gather, e0, e1, e2, e3, wg, wu, wd, hidden, d_gate, d_up, e_out,
    e, held_g, held_u, held_d, stage, e_sem, w_sem, o_sem,
):
    count = gather.own.shape[0]
    pair = 2 * count
    units = wg.shape[0]
    blocks = [(start, min(COLUMNS, units - start)) for start in range(0, units, COLUMNS)]
    outs = (hidden, d_gate, d_up)

    def load_rows(at):
        return pltpu.make_async_copy((e0, e1, e2, e3)[at], e.at[pl.ds(at * count, count)], e_sem.at[at])

    def save_rows():
        return pltpu.make_async_copy(e, e_out, e_sem.at[4])

    def load(at, which):
        where = pl.ds(*blocks[at])
        return pltpu.make_async_copy(
            (wg, wu, wd)[which].at[where], (held_g, held_u, held_d)[which].at[where], w_sem.at[3 * at + which]
        )

    def store(half, which):
        rows = pl.ds(half * pair, pair)
        return pltpu.make_async_copy(stage.at[which, rows], outs[which].at[rows], o_sem.at[3 * half + which])

    load(0, 0).start()
    gather.begin()
    for at in range(len(blocks)):
        for which in range(3):
            if at or which:
                load(at, which).start()
        if at == 0:
            for part in range(4):
                load_rows(part).start()
    gather.near()
    for part in range(4):
        load_rows(part).wait()
    save_rows().start()
    for half in range(2):
        if half:
            gather.second()
        rows = pl.ds(half * pair, pair)
        for at, (start, size) in enumerate(blocks):
            where = pl.ds(start, size)
            if half == 0:
                for which in range(3):
                    load(at, which).wait()
            gate = mm_nt(gather.held[rows, :], held_g[where, :])
            up = mm_nt(gather.held[rows, :], held_u[where, :])
            back = mm_nt(e[rows, :], held_d[where, :])
            sig = sigmoid(gate)
            act = gate * sig
            stage[0, rows, where] = (act * up).astype(bf16)
            stage[1, rows, where] = (back * up * (sig + act * (1.0 - sig))).astype(bf16)
            stage[2, rows, where] = (back * act).astype(bf16)
        for which in range(3):
            store(half, which).start()
    for half in range(2):
        for which in range(3):
            store(half, which).wait()
    save_rows().wait()
    gather.end()


def feed(own, e_blocks, wg, wu, wd):
    rows, width = own.shape
    units = wd.shape[0]
    blocks = pl.cdiv(units, COLUMNS)
    hbm = pl.BlockSpec(memory_space=pl.ANY)
    return gather_call(
        feed_kernel, "feed", 1, own, list(e_blocks) + [wg, wu, wd], [hbm] * 7, [hbm] * 4,
        [jax.ShapeDtypeStruct((4 * rows, units), bf16)] * 3
        + [jax.ShapeDtypeStruct((4 * rows, width), bf16)],
        (40_000_000_000, 40_000_000), "split",
        [pltpu.VMEM((4 * rows, width), bf16)]
        + [pltpu.VMEM((units, width), bf16)] * 3
        + [
            pltpu.VMEM((3, 4 * rows, units), bf16),
            pltpu.SemaphoreType.DMA((5,)),
            pltpu.SemaphoreType.DMA((3 * blocks,)),
            pltpu.SemaphoreType.DMA((6,)),
        ],
    )


def gate_back_kernel(heads, step, gather, length, w, pg, o_in, gain, left, right, dpg, do, dgain, leave_one, leave_two):
    pair = 2 * gather.own.shape[0]
    each = pair // 2
    dv = gain.shape[1]
    half = step // 2

    @pl.when(step == 0)
    def _():
        dgain[...] = jnp.zeros_like(dgain)

    at = half * pair + lax.broadcasted_iota(jnp.int32, (pair, 1), 0)
    at = (at // each ^ lax.axis_index("tensor").astype(jnp.int32)) * each + at % each
    valid = jnp.where(at < length[0], 1.0, 0.0)
    upstream = mm_nt(gather.rows(half), w[...]) * valid
    for head in range(heads):
        where = slice(head * dv, (head + 1) * dv)
        dg = upstream[:, where]
        gate = pg[:, where].astype(f32)
        sig = sigmoid(gate)
        act = gate * sig
        o = o_in[:, where].astype(f32)
        inv = lax.rsqrt(jnp.mean(o * o, axis=-1, keepdims=True) + 1e-05)
        norm = o * inv
        through = dg * norm
        dgain[...] += jnp.sum(through * act, axis=0, keepdims=True)
        dpg[:, where] = (through * gain[...] * (sig + act * (1.0 - sig))).astype(bf16)
        dn = dg * gain[...] * act
        do[:, where] = (inv * (dn - norm * jnp.mean(dn * norm, axis=-1, keepdims=True))).astype(bf16)

    @pl.when(step == 1)
    def _():
        units, first = leave_one.shape
        for start in range(0, units, COLUMNS):
            where = slice(start, min(start + COLUMNS, units))
            product = mm_tn(left[:, where], right[...]).astype(bf16)
            leave_one[where, :] = product[:, :first]
            leave_two[where, :] = product[:, first:]


def gate_back(own, length, w_out, pg, o, gain, left, right):
    rows, width = own.shape
    pair = 2 * rows
    dv = gain.shape[1]
    heads = w_out.shape[0] // dv // 2
    by_head = pl.BlockSpec((pair, heads * dv), lambda j: (j // 2, j % 2))
    return gather_call(
        lambda *refs: gate_back_kernel(heads, *refs), "gate_back", 2, own, [length, w_out, pg, o, gain, left, right],
        [
            pl.BlockSpec(memory_space=pltpu.SMEM),
            pl.BlockSpec((heads * dv, width), lambda j: (j % 2, 0)),
            by_head, by_head,
            pl.BlockSpec((1, dv), lambda j: (0, 0)),
            pl.BlockSpec(left.shape, lambda j: (0, 0)),
            pl.BlockSpec((right.shape[0], right.shape[1] // 2), lambda j: (0, 1)),
        ],
        [
            by_head, by_head,
            pl.BlockSpec((1, dv), lambda j: (0, 0)),
            pl.BlockSpec((left.shape[1], FIRST), lambda j: (0, 0)),
            pl.BlockSpec((left.shape[1], right.shape[1] // 2 - FIRST), lambda j: (0, 0)),
        ],
        [
            jax.ShapeDtypeStruct(pg.shape, bf16),
            jax.ShapeDtypeStruct(pg.shape, bf16),
            jax.ShapeDtypeStruct((1, dv), f32),
            jax.ShapeDtypeStruct((left.shape[1], FIRST), bf16),
            jax.ShapeDtypeStruct((left.shape[1], right.shape[1] // 2 - FIRST), bf16),
        ],
        (30_000_000_000, 30_000_000), "flip", grid=4,
    )


def scatter_kernel(turned, count, filled, after, *refs):
    lefts, rights, refs = refs[:count], refs[count : 2 * count], refs[2 * count :]
    extra_in, refs = refs[: after[1]], refs[after[1] :]
    sources, refs = refs[: filled + 1 if filled else 0], refs[filled + 1 if filled else 0 :]
    out, fills, refs = refs[0], refs[1 : 1 + filled], refs[1 + filled :]
    extra_out, refs = refs[: after[2]], refs[after[2] :]
    far_own, leave, other, send_sem, recv_sem, fill_sem = refs[:6]
    held = refs[6:]
    loads = [pltpu.make_async_copy(source, kept, fill_sem.at[at]) for at, (source, kept) in enumerate(zip(sources, held))]
    step = pl.program_id(0)
    parts = pl.num_programs(0) // 2
    rows = out.shape[0]
    place = lax.axis_index("tensor")
    beside, across = flipped(place, 1, 4), flipped(place, 2, 4)
    multiply = mm_nt if turned else mm
    CORNER, NEAR, ACROSS = 0, 1, 2

    def columns(part):
        return pl.ds(pl.multiple_of(part * COLUMNS, COLUMNS), COLUMNS)

    def copy(kind, part):
        return pltpu.make_async_remote_copy(
            src_ref=leave.at[kind, :, columns(part)],
            dst_ref=other.at[kind, :, columns(part)],
            send_sem=send_sem.at[kind, part],
            recv_sem=recv_sem.at[kind, part],
            device_id={"tensor": across if kind == ACROSS else beside},
            device_id_type=MESH,
        )

    def product():
        total = multiply(lefts[0][...], rights[0][...])
        for at in range(1, count):
            total = total + multiply(lefts[at][...], rights[at][...])
        return total

    def pass_on(part):
        copy(CORNER, part).wait_recv()
        both = far_own[:, columns(part)] + other[CORNER, :, columns(part)].astype(f32)
        leave[ACROSS, :, columns(part)] = both.astype(bf16)
        copy(ACROSS, part).start()

    @pl.when(step == 0)
    def _():
        barrier = pltpu.get_barrier_semaphore()
        for to in (beside, across):
            pl.semaphore_signal(barrier, inc=1, device_id={"tensor": to}, device_id_type=MESH)
        pl.semaphore_wait(barrier, 2)
        for load in loads:
            load.start()

    part = step % parts

    @pl.when(step < parts)
    def _():
        total = product()
        far_own[:, columns(part)] = total[:rows]
        leave[CORNER, :, columns(part)] = total[rows:].astype(bf16)
        copy(CORNER, part).start()

        @pl.when(step > 0)
        def _():
            pass_on(part - 1)

    @pl.when(step >= parts)
    def _():
        @pl.when(step == parts)
        def _():
            pass_on(parts - 1)

        total = product()
        out[:, columns(part)] = total[:rows]
        leave[NEAR, :, columns(part)] = total[rows:].astype(bf16)
        copy(NEAR, part).start()

    @pl.when(step == 2 * parts - 1)
    def _():
        for load in loads:
            load.wait()
        for fill, source in zip(fills, held[1:]):
            for start in range(0, fill.shape[0], COLUMNS):
                where = slice(start, start + COLUMNS)
                fill[where, :] = mm_tn(held[0][:, where], source[...]).astype(bf16)

        def finish(part, carry):
            copy(NEAR, part).wait_recv()
            copy(ACROSS, part).wait_recv()
            where = columns(part)
            out[:, where] = (
                out[:, where] + other[NEAR, :, where].astype(f32) + other[ACROSS, :, where].astype(f32)
            )
            for kind in (CORNER, NEAR, ACROSS):
                copy(kind, part).wait_send()
            return carry

        lax.fori_loop(0, parts, finish, 0)
        if after[0] is not None:
            after[0](out, *extra_in, *extra_out)


def norm_after(out, tokens, gain, resid, normed):
    rows = tokens[...].astype(f32) + out[...]
    resid[...] = rows
    inverse = lax.rsqrt(jnp.mean(rows * rows, axis=-1, keepdims=True) + 1e-05)
    normed[...] = (rows * inverse * gain[...]).astype(bf16)


def norm_back_after(out, resid, gain, upstream, d_resid, d_gain):
    rows = resid[...]
    inverse = lax.rsqrt(jnp.mean(rows * rows, axis=-1, keepdims=True) + 1e-05)
    scaled = rows * inverse
    through = out[...]
    d_gain[...] = jnp.sum(through * scaled, axis=0, keepdims=True)
    along = through * gain[...]
    inner = jnp.mean(along * scaled, axis=-1, keepdims=True)
    d_resid[...] = (upstream[...].astype(f32) + inverse * (along - scaled * inner)).astype(bf16)


def scatter_products(lefts, rights, turned, collective, fill=None, after=None, given=(), made_after=()):
    lefts = [left if isinstance(left, tuple) else (left, 0, left.shape[1]) for left in lefts]
    rows = lefts[0][0].shape[0] // 4
    width = rights[0].shape[0 if turned else 1]
    parts = width // COLUMNS
    total = sum(left[2] for left in lefts)
    flops = 8 * rows * width * total

    def left_spec(block, size):
        return pl.BlockSpec((2 * rows, size), lambda j: (1 - j // parts, block))

    def right_spec(right):
        if turned:
            return pl.BlockSpec((COLUMNS, right.shape[1]), lambda j: (j % parts, 0))
        return pl.BlockSpec((right.shape[0], COLUMNS), lambda j: (0, j % parts))

    in_specs = [left_spec(block, size) for _, block, size in lefts] + [right_spec(right) for right in rights]
    out_specs = [pl.BlockSpec((rows, width), lambda j: (0, 0))]
    out_shape = [jax.ShapeDtypeStruct((rows, width), f32)]
    fill = list(fill or ())
    in_specs += [pl.BlockSpec(part.shape, lambda j: (0, 0)) for part in given]
    in_specs += [pl.BlockSpec(memory_space=pl.ANY)] * len(fill)
    for part in fill[1:]:
        made = (fill[0].shape[1], part.shape[1])
        out_specs.append(pl.BlockSpec(made, lambda j: (0, 0)))
        out_shape.append(jax.ShapeDtypeStruct(made, bf16))
    out_specs += [pl.BlockSpec(part.shape, lambda j: (0, 0)) for part in made_after]
    out_shape += list(made_after)
    follow = (after, len(given), len(made_after))
    outs = pl.pallas_call(
        lambda *refs: scatter_kernel(turned, len(lefts), max(len(fill) - 1, 0), follow, *refs),
        name="scatter_products",
        grid=(2 * parts,),
        in_specs=in_specs,
        out_specs=out_specs,
        out_shape=out_shape,
        scratch_shapes=[
            pltpu.VMEM((rows, width), f32),
            pltpu.VMEM((3, rows, width), bf16),
            pltpu.VMEM((3, rows, width), bf16),
            pltpu.SemaphoreType.DMA((3, parts)),
            pltpu.SemaphoreType.DMA((3, parts)),
            pltpu.SemaphoreType.DMA((max(len(fill), 1),)),
        ]
        + [pltpu.VMEM(part.shape, bf16) for part in fill],
        compiler_params=pltpu.CompilerParams(
            vmem_limit_bytes=VMEM_MOST, collective_id=collective, has_side_effects=True
        ),
        cost_estimate=LITTLE,
    )(*[left[0] for left in lefts], *rights, *given, *fill)
    return outs if fill or made_after else outs[0]


def turned_kernel(added, left, right, *refs):
    total = mm_tn(left[...], right[...])
    if added:
        total = total + refs[0][...].astype(f32)
    refs[-1][...] = total.astype(bf16)


def turned_product(left, right, left_half=None, right_half=None, other=None):
    rows = left.shape[0]
    count = left.shape[1] if left_half is None else left.shape[1] // 2
    width = right.shape[1] if right_half is None else right.shape[1] // 2
    skip = (left_half or 0) * (count // COLUMNS)
    out = pl.BlockSpec((COLUMNS, width), lambda j: (j, 0))
    more = [] if other is None else [other]
    return pl.pallas_call(
        lambda *refs: turned_kernel(len(more), *refs),
        name="turned_product",
        grid=(pl.cdiv(count, COLUMNS),),
        in_specs=[
            pl.BlockSpec((rows, COLUMNS), lambda j: (0, skip + j)),
            pl.BlockSpec((rows, width), lambda j: (0, right_half or 0)),
        ]
        + [out] * len(more),
        out_specs=out,
        out_shape=jax.ShapeDtypeStruct((count, width), bf16),
        compiler_params=pltpu.CompilerParams(vmem_limit_bytes=VMEM_MOST),
        cost_estimate=LITTLE,
    )(left, right, *more)


def low_bit(chunk, groups):
    return groups if chunk == 0 else chunk & -chunk


def reduce_plan(groups, early, late):
    chunks = [chunk for chunk in group_order(groups) if chunk % 2 == 0]
    chunks.sort(key=lambda chunk: low_bit(chunk, groups))
    levels = max(groups.bit_length() - 2, 1)
    plan = []
    for at, tensor in enumerate(late):
        for position, chunk in enumerate(chunks):
            level = low_bit(chunk, groups).bit_length() - 2
            lag = LAST * level / levels if chunk == 0 else NEXT * level
            plan.append((at * len(chunks) + position + lag, tensor, chunk))
    for at, tensor in enumerate(early):
        for position, chunk in enumerate(chunks):
            level = low_bit(chunk, groups).bit_length() - 2
            plan.append((EARLY[0] * at - 1 + EARLY[1] * level + 0.01 * position, tensor, chunk))
    return [step[1:] for step in sorted(plan)], chunks


PARTS = 2
AHEAD = 4
EARLY = (2, 6)
LAST, NEXT = 2.5, 0.5


def reduce_kernel(groups, early, shapes, *refs):
    count = len(shapes)
    late = list(range(len(early), count))
    leaves, refs = refs[:count], refs[count:]
    given, refs = refs[: len(early)], refs[len(early) :]
    (taps_q, taps_k, taps_v, decay, thin, gain_one, gain_two, gain_head, hidden_in, down_in, resid), refs = (
        refs[:11], refs[11:],
    )
    outs = []
    for shape in shapes:
        outs.append(refs[: len(shape)])
        refs = refs[len(shape) :]
    (out_q, out_k, out_v, out_decay, out_thin, out_one, out_two, out_head, mixed), refs = refs[:9], refs[9:]
    lands, refs = refs[:count], refs[count:]
    sends, refs = refs[:count], refs[count:]
    keeps, refs = refs[:count], refs[count:]
    small_land, gains_land, gains_first, rows_leave, rows_land, hidden, down, partial = refs[:8]
    send_sem, recv_sem, sum_send, sum_recv, rows_send, rows_recv, keep_sem, load_sem = refs[8:]
    place = lax.axis_index("dp")
    beside = lax.axis_index("tensor")
    order = group_order(groups)
    position = {chunk: at for at, chunk in enumerate(order)}
    bits = [1 << at for at in range(groups.bit_length() - 1)]
    each = sends[0].shape[0] // (groups // 2 - 1)
    across_core = {"tensor": flipped(beside, 1, 4)}
    across_chip = {"tensor": flipped(beside, 2, 4)}

    size = each // PARTS

    def rows(at, part):
        return pl.ds(at * each + part * size, size)

    def slot(unit, chunk):
        tensor, part = unit
        return rows(chunk // 2 - 1 if tensor in early else chunk - 1, part)

    def copy(unit, chunk):
        tensor, part = unit
        if chunk % 2:
            source = leaves[tensor].at[rows(position[chunk], part)]
        else:
            source = sends[tensor].at[rows(chunk // 2 - 1, part)]
        at = (tensor * PARTS + part) * groups + chunk
        return pltpu.make_async_remote_copy(
            src_ref=source,
            dst_ref=lands[tensor].at[slot(unit, chunk)],
            send_sem=send_sem.at[at],
            recv_sem=recv_sem.at[at],
            device_id={"dp": flipped(place, low_bit(chunk, groups), groups)},
            device_id_type=MESH,
        )

    def keep_copy(tensor):
        return pltpu.make_async_copy(
            leaves[tensor].at[pl.ds(0, keeps[tensor].shape[0])], keeps[tensor], keep_sem.at[tensor]
        )

    for tensor in range(count):
        keep_copy(tensor).start()
    kept = set()
    partners = [{"dp": flipped(place, bit, groups)} for bit in bits] + [across_core, across_chip]
    barrier = pltpu.get_barrier_semaphore()
    for partner in partners:
        pl.semaphore_signal(barrier, inc=1, device_id=partner, device_id_type=MESH)
    pl.semaphore_wait(barrier, len(partners))

    early_units = [(tensor, part) for tensor in early for part in range(PARTS)]
    late_units = [(tensor, part) for tensor in late for part in range(PARTS)]
    plan, chunks = reduce_plan(groups, early_units, late_units)
    pieces = [(unit, chunk + 1) for unit in late_units for chunk in chunks]
    started = []

    def send_piece():
        if len(started) < len(pieces):
            copy(*pieces[len(started)]).start()
            started.append(1)

    for _ in range(AHEAD):
        send_piece()

    def plain_copy(source, land, sems, at, partner):
        return pltpu.make_async_remote_copy(
            src_ref=source, dst_ref=land, send_sem=sems[0].at[at], recv_sem=sems[1].at[at],
            device_id=partner, device_id_type=MESH,
        )

    quarter = mixed.shape[0]
    quarter_width = mixed.shape[1] // 4
    blocks = [pl.ds(at * quarter, quarter) for at in range(4)]
    row_sems = (rows_send, rows_recv)
    corner = plain_copy(partial.at[blocks[3]], rows_land.at[0], row_sems, 0, across_core)
    near = plain_copy(partial.at[blocks[1]], rows_land.at[1], row_sems, 1, across_core)
    far = plain_copy(rows_leave, rows_land.at[2], row_sems, 2, across_chip)
    loads = [
        pltpu.make_async_copy(hidden_in, hidden, load_sem.at[0]),
        pltpu.make_async_copy(down_in, down, load_sem.at[1]),
    ]
    for load in loads:
        load.start()

    kw, line = taps_q.shape[1], taps_v.shape[1]
    lines = gain_one.shape[1] // line
    gains_first[0] = jnp.zeros(gains_first.shape[1:], f32)
    small_land[0] = jnp.zeros(small_land.shape[1:], f32)
    small_land[0, 0:4, :] = taps_v[...]
    small_land[0, 4:8, :kw] = taps_q[...]
    small_land[0, 4:8, kw:] = taps_k[...]
    for at in range(lines):
        where = slice(at * line, (at + 1) * line)
        small_land[0, 8 + 8 * at : 16 + 8 * at, :] = thin[:, where]
        gains_first[0, at : at + 1, :] = gain_one[:, where]
        gains_first[0, lines + at : lines + at + 1, :] = gain_two[:, where]
    small_land[0, 8 + 8 * lines : 9 + 8 * lines, : decay.shape[1]] = decay[...]
    gains_first[0, 2 * lines : 2 * lines + 1, : gain_head.shape[1]] = gain_head[...]
    sum_sems = (sum_send, sum_recv)
    hops = [across_core, across_chip] + [{"dp": flipped(place, bit, groups)} for bit in bits]
    gains_copies = [
        plain_copy(gains_first.at[at], gains_land.at[at], sum_sems, at, partner)
        for at, partner in enumerate(hops)
    ]
    small_copies = [
        plain_copy(small_land.at[2 * at], small_land.at[2 * at + 1], sum_sems, len(hops) + at, partner)
        for at, partner in enumerate(hops[2:])
    ]
    gains_copies[0].start()
    small_copies[0].start()
    done = {"gains": 0, "small": 0}

    def next_sum():
        at = done["gains"]
        if at < len(gains_copies):
            gains_copies[at].wait_recv()
            total = gains_first[at] + gains_land[at]
            if at + 1 < len(gains_copies):
                gains_first[at + 1] = total
                gains_copies[at + 1].start()
            else:
                for row in range(lines):
                    where = slice(row * line, (row + 1) * line)
                    out_one[:, where] = total[row : row + 1, :]
                    out_two[:, where] = total[lines + row : lines + row + 1, :]
                out_head[...] = total[2 * lines : 2 * lines + 1, : gain_head.shape[1]]
            done["gains"] += 1
        at = done["small"]
        if at < len(small_copies):
            small_copies[at].wait_recv()
            total = small_land[2 * at] + small_land[2 * at + 1]
            if at + 1 < len(small_copies):
                small_land[2 * at + 2] = total
                small_copies[at + 1].start()
            else:
                out_v[...] = total[0:4]
                out_q[...] = total[4:8, :kw]
                out_k[...] = total[4:8, kw:]
                for row in range(lines):
                    out_thin[:, row * line : (row + 1) * line] = total[8 + 8 * row : 16 + 8 * row]
                out_decay[...] = total[8 + 8 * lines : 9 + 8 * lines, : decay.shape[1]]
            done["small"] += 1

    def finish(tensor, part, total):
        where = slice(part * size, (part + 1) * size)
        for out, (start, count, turned) in zip(outs[tensor], shapes[tensor]):
            piece = total[:, start : start + count]
            if turned:
                out[:, where] = jnp.transpose(piece)
            else:
                out[where, :] = piece

    for index, (unit, chunk) in enumerate(plan):
        tensor, part = unit
        if index == 3:
            for load in loads:
                load.wait()
        if 4 <= index < 8:
            where = pl.ds((index - 4) * quarter_width, quarter_width)
            partial[:, where] = mm(hidden[...], down[:, where]).astype(bf16)
        if index == 8:
            corner.start()
            near.start()
        if index == 12:
            corner.wait_recv()
            rows_leave[...] = (
                partial[blocks[2], :].astype(f32) + rows_land[0].astype(f32)
            ).astype(bf16)
            far.start()
        if tensor not in kept:
            keep_copy(tensor).wait()
            kept.add(tensor)
        total = keeps[tensor][rows(position[chunk], part), :].astype(f32)
        for bit in bits:
            if bit >= low_bit(chunk, groups):
                break
            if bit == 1 and tensor in early:
                total = total + given[tensor][rows(position[chunk], part), :].astype(f32)
                continue
            copy(unit, chunk + bit).wait_recv()
            if bit == 1:
                send_piece()
            total = total + lands[tensor][slot(unit, chunk + bit), :].astype(f32)
        if chunk:
            sends[tensor][rows(chunk // 2 - 1, part), :] = total.astype(bf16)
            copy(unit, chunk).start()
        else:
            finish(tensor, part, total)
        if index >= 4 and index % 4 == 0:
            next_sum()
        if index == 20:
            near.wait_recv()
            far.wait_recv()
            mixed[...] = (
                resid[...]
                + partial[blocks[0], :].astype(f32)
                + rows_land[1].astype(f32)
                + rows_land[2].astype(f32)
            ).astype(bf16)
    while done["gains"] < len(gains_copies):
        next_sum()
    for unit in early_units + late_units:
        for chunk in range(1, groups):
            if chunk % 2 == 0 or unit[0] in late:
                copy(unit, chunk).wait_send()
    for sent in gains_copies + small_copies + [corner, near, far]:
        sent.wait_send()


def reduce_groups(early_grads, given, late_grads, shapes, small, hidden, down, resid, collective):
    grads = list(early_grads) + list(late_grads)
    early = list(range(len(early_grads)))
    groups = lax.axis_size("dp")
    bits = groups.bit_length() - 1
    each = late_grads[0].shape[0] // groups
    rows, width = resid.shape
    widths = [grad.shape[1] for grad in grads]
    vmem = pl.BlockSpec(memory_space=pltpu.VMEM)
    out_shape = []
    for shape in shapes:
        for _, size, turned in shape:
            out_shape.append(jax.ShapeDtypeStruct((size, each) if turned else (each, size), f32))
    out_shape += [jax.ShapeDtypeStruct(part.shape, f32) for part in small]
    out_shape += [jax.ShapeDtypeStruct((rows, width), bf16)]
    line = small[2].shape[1]
    lines = width // line
    small_shape, gains_shape = (16 + 8 * lines, line), (8 * pl.cdiv(2 * lines + 1, 8), line)
    landed = [(groups // 2 if at in early else groups) - 1 for at in range(len(grads))]
    return pl.pallas_call(
        lambda *refs: reduce_kernel(groups, early, shapes, *refs),
        name="reduce_groups",
        in_specs=[pl.BlockSpec(memory_space=pl.ANY)] * len(grads)
        + [vmem] * (len(given) + len(small))
        + [pl.BlockSpec(memory_space=pl.ANY)] * 2 + [vmem],
        out_specs=[vmem] * len(out_shape),
        out_shape=out_shape,
        scratch_shapes=[pltpu.VMEM((chunks * each, size), bf16) for chunks, size in zip(landed, widths)]
        + [pltpu.VMEM(((groups // 2 - 1) * each, size), bf16) for size in widths]
        + [pltpu.VMEM((groups // 2 * each, size), bf16) for size in widths]
        + [
            pltpu.VMEM((2 * bits,) + small_shape, f32),
            pltpu.VMEM((bits + 2,) + gains_shape, f32),
            pltpu.VMEM((bits + 2,) + gains_shape, f32),
            pltpu.VMEM((rows, width), bf16),
            pltpu.VMEM((3, rows, width), bf16),
            pltpu.VMEM(hidden.shape, bf16),
            pltpu.VMEM(down.shape, bf16),
            pltpu.VMEM((4 * rows, width), bf16),
            pltpu.SemaphoreType.DMA((len(grads) * PARTS * groups,)),
            pltpu.SemaphoreType.DMA((len(grads) * PARTS * groups,)),
            pltpu.SemaphoreType.DMA((2 * bits + 2,)),
            pltpu.SemaphoreType.DMA((2 * bits + 2,)),
            pltpu.SemaphoreType.DMA((3,)),
            pltpu.SemaphoreType.DMA((3,)),
            pltpu.SemaphoreType.DMA((len(grads),)),
            pltpu.SemaphoreType.DMA((2,)),
        ],
        compiler_params=pltpu.CompilerParams(
            vmem_limit_bytes=VMEM_MOST, collective_id=collective, has_side_effects=True
        ),
        cost_estimate=LITTLE,
    )(*grads, *given, *small, hidden, down, resid)


def product_nn(left, right):
    return jnp.dot(left, right, preferred_element_type=jnp.float32)


def tie(value, after):
    return lax.optimization_barrier((value, after))[0]


def together(*values):
    return lax.optimization_barrier(values)


def flip(array, axis, bit):
    size = lax.axis_size(axis)
    return lax.ppermute(array, axis, [(place, place ^ bit) for place in range(size)])


def in_order(array):
    groups = lax.axis_size("dp")
    place = lax.axis_index("dp").astype(jnp.int32)
    found = jnp.array(group_order(groups), jnp.int32)[jnp.arange(groups, dtype=jnp.int32) ^ place]
    return jnp.take(array.reshape(array.shape[0], groups, -1), found, axis=1)


def scatter_far(total):
    groups = lax.axis_size("dp")
    alike = [[place for place in range(groups) if place % 2 == bit] for bit in (0, 1)]
    return lax.psum_scatter(total, "dp", scatter_dimension=1, axis_index_groups=alike, tiled=True)


def per_device(
    tokens,
    norm1_gain,
    w_query,
    w_key,
    w_value,
    w_gate_out,
    w_decay,
    w_beta,
    conv_query,
    conv_key,
    conv_value,
    decay_log,
    decay_bias,
    head_gain,
    w_out,
    norm2_gain,
    w_gate,
    w_up,
    w_down,
    state_in,
    seq_blocks,
    seq_tail,
    cotangent,
):
    width = tokens.shape[1]
    heads = decay_log.shape[0]
    rows_in = tokens.astype(jnp.float32)
    scaled1, inverse1 = row_stats(rows_in)
    normed1 = (scaled1 * norm1_gain).astype(jnp.bfloat16)
    seq_length = (BLOCK * (seq_blocks - 1) + seq_tail).astype(jnp.int32)
    place = lax.axis_index("tensor").astype(jnp.int32)
    scal = jnp.stack([seq_length[0], place])
    gain_row, log_row, bias_row = head_gain[None], decay_log[None], decay_bias[None]
    w_small = jnp.concatenate([w_decay.T, w_beta.T], axis=0)
    weights1 = (w_query, w_key, w_value, w_gate_out, w_small)
    p_query, p_key, p_value, p_gate, p_small, gathered1 = project(normed1, weights1)
    cotangent = tie(cotangent, p_small)
    e_beside, e_across = flip(cotangent, "tensor", 1), flip(cotangent, "tensor", 2)
    gated, final, mixer_out, delta, states, inverse_t = mixer_forward(
        scal, p_query, p_key, p_value, p_gate, p_small,
        conv_query, conv_key, conv_value, log_row, bias_row, gain_row, state_in[0],
    )
    gated, e_across = together(gated, e_across)
    e_corner = flip(e_across, "tensor", 1)
    own_rows = jax.ShapeDtypeStruct(tokens.shape, jnp.float32)
    own_low = jax.ShapeDtypeStruct(tokens.shape, jnp.bfloat16)
    gain_line = jax.ShapeDtypeStruct((1, width), jnp.float32)
    _, resid, normed2 = scatter_products(
        [gated], [w_out], False, 3, None, norm_after, [tokens, norm2_gain[None]], [own_rows, own_low]
    )
    hidden, d_gate, d_up, cot_full, split2 = feed(
        normed2, (cotangent, e_beside, e_across, e_corner), w_gate.T, w_up.T, w_down
    )
    grad_down = product_tn(hidden, cot_full).astype(jnp.bfloat16)
    half = width // 2
    up_other = product_tn(d_up, split2[:, half:]).astype(jnp.bfloat16)
    d_gate, d_up, grad_down, up_other = together(d_gate, d_up, grad_down, up_other)
    grad_down = scatter_far(grad_down)
    up_other = flip(up_other, "dp", 1)
    _, d_resid, grad_norm2 = scatter_products(
        [d_gate, d_up], [w_gate.T, w_up.T], False, 4, None,
        norm_back_after, [resid, norm2_gain[None], cotangent], [own_low, gain_line],
    )
    dp_gate, do, dgain, gate_one, gate_two, resid_full = gate_back(
        d_resid, seq_length, w_out, p_gate, mixer_out, gain_row, d_gate, split2
    )
    do, dp_gate, dgain, resid_full, gate_one, gate_two, up_other = together(
        do, dp_gate, dgain, resid_full, gate_one, gate_two, up_other
    )
    gate_one = flip(gate_one, "dp", 1)
    up_kept = turned_product(d_up, split2, right_half=0, other=up_other)
    do, up_kept, gate_one, gate_two = together(do, up_kept, gate_one, gate_two)
    grad_up = scatter_far(up_kept)
    gate_two = flip(gate_two, "dp", 1)
    mixer_grads = mixer_backward(
        scal, p_query, p_key, p_value, p_small, do, delta, states, inverse_t,
        conv_query, conv_key, conv_value, log_row, bias_row, (gathered1, dp_gate), (resid_full, gated),
        (d_gate, split2),
    )
    (
        dp_pair, dp_value, dp_small, dc_query, dc_key, dc_value, ddecay, grad_gate_out, out_other, gate_kept, out_keep,
        grad_down, gate_two,
    ) = together(*mixer_grads, grad_down, gate_two)
    gate_other = jnp.concatenate([gate_one, gate_two], axis=1)
    each = width // lax.axis_size("dp")
    bit = lax.axis_index("dp") % 2
    down_keep = lax.dynamic_slice_in_dim(grad_down, bit * each, each, 1)
    down_other = lax.dynamic_slice_in_dim(grad_down, (1 - bit) * each, each, 1)
    out_other, down_other = together(out_other, down_other)
    out_other, down_other = flip(out_other, "dp", 1), flip(down_other, "dp", 1)
    gate_kept = gate_kept.astype(jnp.float32) + gate_other.astype(jnp.float32)
    grad_gate = scatter_far(gate_kept.astype(jnp.bfloat16))
    key_width = w_query.shape[1]
    d_normed1, grad_value, grad_pair = scatter_products(
        [(dp_pair, 0, key_width), (dp_pair, 1, key_width), dp_value, dp_gate, dp_small],
        weights1[:4] + (w_small.T,), True, 5, (gathered1, dp_value, dp_pair),
    )
    d_normed1, out_other, down_other = together(d_normed1, out_other, down_other)
    grad_down = down_keep.astype(jnp.float32) + down_other.astype(jnp.float32)
    grad_small = in_order(product_tn(dp_small, gathered1))
    d_tokens_part, grad_norm1 = norm_back(scaled1, inverse1, norm1_gain, d_normed1)
    tokens_grad = (d_resid.astype(jnp.float32) + d_tokens_part).astype(jnp.bfloat16)
    value_width = w_value.shape[1]
    turn = (width // lax.axis_size("dp")) % 128 == 0
    thin = grad_small.reshape(grad_small.shape[0], width)
    small = [dc_query, dc_key, dc_value, ddecay, thin, grad_norm1[None], grad_norm2, dgain]
    (
        grad_out, grad_gate_out, grad_value, grad_query, grad_key,
        dc_query, dc_key, dc_value, ddecay, thin, grad_norm1, grad_norm2, dgain, mixed,
    ) = reduce_groups(
        [out_keep], [out_other], [grad_gate_out, grad_value, grad_pair],
        [
            [(0, value_width, turn)],
            [(0, value_width, False)],
            [(0, value_width, False)],
            [(0, key_width, False), (key_width, key_width, False)],
        ],
        small, hidden, w_down, resid, 6,
    )
    mixed, grad_up = together(mixed, grad_up)
    grad_up, grad_gate = grad_up.astype(jnp.float32), grad_gate.astype(jnp.float32)
    grad_small = lax.dynamic_slice_in_dim(thin, lax.axis_index("dp") * each, each, 1).T
    return (
        mixed,
        final[None],
        tokens_grad,
        grad_norm1[0],
        grad_query,
        grad_key,
        grad_value,
        grad_gate_out,
        grad_small[:, :heads],
        grad_small[:, heads:],
        dc_query,
        dc_key,
        dc_value,
        ddecay[0, :heads],
        ddecay[0, heads:],
        dgain[0],
        grad_out if turn else grad_out.T,
        grad_norm2[0],
        grad_gate.T,
        grad_up.T,
        grad_down,
    )


def solution(mesh):
    in_specs = (
        P(("dp", "tensor"), None),
        P(),
        P(None, "tensor"),
        P(None, "tensor"),
        P(None, "tensor"),
        P(None, "tensor"),
        P(None, "tensor"),
        P(None, "tensor"),
        P(None, "tensor"),
        P(None, "tensor"),
        P(None, "tensor"),
        P("tensor"),
        P("tensor"),
        P(),
        P("tensor", None),
        P(),
        P(None, "tensor"),
        P(None, "tensor"),
        P("tensor", None),
        P("dp", "tensor", None, None),
        P("dp"),
        P("dp"),
        P(("dp", "tensor"), None),
    )
    out_specs = (
        P(("dp", "tensor"), None),
        P("dp", "tensor", None, None),
        P(("dp", "tensor"), None),
        P(),
        P("dp", "tensor"),
        P("dp", "tensor"),
        P("dp", "tensor"),
        P("dp", "tensor"),
        P("dp", "tensor"),
        P("dp", "tensor"),
        P(None, "tensor"),
        P(None, "tensor"),
        P(None, "tensor"),
        P("tensor"),
        P("tensor"),
        P(),
        P("tensor", "dp"),
        P(),
        P("dp", "tensor"),
        P("dp", "tensor"),
        P("tensor", "dp"),
    )
    return jax.shard_map(
        per_device, mesh=mesh, in_specs=in_specs, out_specs=out_specs, check_vma=False
    )
```
